32 devices in a mesh: dp: 8 (over z, y), fsdp: 4 (over x, core).
Axes of the slice: x: 2, y: 2, z: 4, core: 2. Of those that a mesh axis runs over, the one named last changes fastest.
Arguments:
- tokens: bfloat16 [32768, 768], P(('dp', 'fsdp')), may hold values from -6 to 6
- cotangent: bfloat16 [32768, 768], P(('dp', 'fsdp')), may hold values from -6 to 6
- lengths: int32 [32, 8], P(('dp', 'fsdp')), may hold values from 0 to 1024, as said below
- norm_params: bfloat16 [768, 4], P('dp', 'fsdp'), may hold values from -1 to 1.65, as said below
- bias_params: bfloat16 [768, 4], P('dp', 'fsdp'), may hold values from -1.75 to 1.75
- w_qkv: bfloat16 [768, 2304], P('dp', 'fsdp'), may hold values from -0.21650635 to 0.21650635
- w_out: bfloat16 [768, 768], P('dp', 'fsdp'), may hold values from -0.4375 to 0.4375
- w_up: bfloat16 [768, 3072], P('dp', 'fsdp'), may hold values from -0.21875 to 0.21875
- up_bias: bfloat16 [768, 4], P('dp', 'fsdp'), may hold values from -1.75 to 1.75
- w_down: bfloat16 [3072, 768], P('dp', 'fsdp'), may hold values from -0.109375 to 0.109375
Outputs:
- outputs: bfloat16 [32768, 768], P(('dp', 'fsdp'))
- input_grad: bfloat16 [32768, 768], P(('dp', 'fsdp'))
- grad_norm_params: float32 [768, 4], P('dp', 'fsdp')
- grad_bias_params: float32 [768, 4], P('dp', 'fsdp')
- grad_w_qkv: float32 [768, 2304], P('dp', 'fsdp')
- grad_w_out: float32 [768, 768], P('dp', 'fsdp')
- grad_w_up: float32 [768, 3072], P('dp', 'fsdp')
- grad_up_bias: float32 [768, 4], P('dp', 'fsdp')
- grad_w_down: float32 [3072, 768], P('dp', 'fsdp')
The draws below stay inside these ranges and needn't reach their ends.
Inputs may be any that keep to these rules, and one draw needn't show every extreme that they name: Row b lists the sequences of token block b in order: positive lengths first, each 128 or more, then zeros; a row sums to 1024 or less, and some row holds a single sequence of exactly 1024 rows. `norm_params`: columns 0 and 2 are the two gains, which are positive; columns 1 and 3 the two shifts.
All inputs are finite; a program needn't handle non-finite values.
Results may differ from the reference program's by a relative error of at most 0.014.
Values may be sent and summed in bfloat16 or wider, within the bound.
A program may use at most 192 MiB of HBM per device.

```python
import jax
import jax.numpy as jnp
from jax import lax

D = 768
HEADS = 12
FF = 3072
TOK_DEV = 1024
MIN_LEN = 128
SLOTS = 8
BUCKETS = 32
TOKENS = 32768


def draw_lengths(key, part):
    pick_key, level_key, other_key, jitter_key = jax.random.split(key, 4)
    levels = jnp.minimum(jax.random.randint(level_key, (BUCKETS, SLOTS), 0, 4), jax.random.randint(other_key, (BUCKETS, SLOTS), 0, 4))
    baseline = MIN_LEN * jnp.power(2, levels).astype(jnp.int32)
    jitter = jax.random.randint(jitter_key, (BUCKETS, SLOTS), 0, baseline)
    drawn = jnp.minimum(baseline + jitter, TOK_DEV)
    running = jnp.cumsum(drawn, axis=1)
    fitted = jnp.where(running <= TOK_DEV, drawn, 0)
    chosen_row = jax.random.randint(pick_key, (), 0, BUCKETS)
    single_row = jnp.zeros((SLOTS,), jnp.int32).at[0].set(TOK_DEV)
    row_ids = jnp.arange(BUCKETS)
    return jnp.where((row_ids == chosen_row)[:, None], single_row[None, :], fitted).astype(jnp.int32)


def draw_norm_params(key, part):
    gain_key, shift_key = jax.random.split(key)
    gains = jax.random.uniform(gain_key, (D, 4), jnp.float32, 0.5, 1.5)
    shifts = jnp.clip(0.4 * jax.random.normal(shift_key, (D, 4), jnp.float32), -1.0, 1.0)
    columns = jnp.arange(4) % 2 == 0
    return jnp.where(columns[None, :], gains, shifts).astype(jnp.bfloat16)


def draw_w_qkv(key, part):
    key = jax.random.fold_in(key, 7)
    entries = jnp.clip(jax.random.normal(key, (D, 3 * D), jnp.float32), -6.0, 6.0)
    columns = jnp.arange(3 * D)
    factor = jnp.where((columns >= D) & (columns < D + D // HEADS), 0.06, 1.0)
    return (entries * factor[None, :] * float(D) ** (-0.5)).astype(jnp.bfloat16)


def level_of(rng, dims, pieces, smallest, largest):
    level, own = 1.0, jax.random.fold_in(rng, 6)
    for dim, parts in pieces:
        draws = jnp.exp(jax.random.uniform(jax.random.fold_in(own, dim), (parts,), jnp.float32, smallest / len(pieces), largest / len(pieces)))
        level = level * jnp.repeat(draws, dims[dim] // parts).reshape([-1 if axis == dim else 1 for axis in range(len(dims))])
    return level


def noise(stream_key, extent, width, reach, cuts=(), kind=jnp.bfloat16):
    values = jax.random.normal(stream_key, extent, jnp.float32) * width
    if len(cuts) > 0:
        values = level_of(stream_key, extent, cuts, -0.22, 0.18) * values
    return jnp.clip(values, min=-reach, max=reach).astype(kind)


def setup_inputs(seed: int = 0) -> dict:
    splits = jax.random.split(jax.random.key(seed), 11)
    return {
        "tokens": noise(splits[0], (TOKENS, D), 1.0, 6.0, ((0, 32),)),
        "cotangent": noise(splits[1], (TOKENS, D), 1.0, 6.0, ((0, 32),)),
        "lengths": draw_lengths(jax.random.fold_in(splits[10], 71), 0),
        "norm_params": draw_norm_params(jax.random.fold_in(splits[10], 71), 0),
        "bias_params": noise(splits[4], (D, 4), 0.3, 1.75, ((0, 8), (1, 4))),
        "w_qkv": draw_w_qkv(jax.random.fold_in(splits[10], 71), 0),
        "w_out": noise(splits[6], (D, D), (D // 4) ** -0.5, 0.4375, ((0, 8), (1, 4))),
        "w_up": noise(splits[7], (D, FF), D ** -0.5, 0.21875, ((0, 8), (1, 4))),
        "up_bias": noise(splits[8], (FF // 4, 4), 0.3, 1.75, ((0, 8), (1, 4))),
        "w_down": noise(splits[9], (FF, D), FF ** -0.5, 0.109375, ((0, 8), (1, 4))),
    }


@jax.custom_vjp
def low(v):
    return lax.optimization_barrier(v.astype(jnp.bfloat16)).astype(jnp.float32)

@jax.custom_vjp
def low_back(v):
    return v

def low_keep(v):
    return (low(v), None)

def low_pass(kept, grad):
    return (grad,)

def back_keep(v):
    return (v, None)

def back_low(kept, grad):
    return (low(grad),)
low.defvjp(low_keep, low_pass)
low_back.defvjp(back_keep, back_low)
EPS = 1e-05
NEG = -1e+30
HIGH = lax.Precision.HIGHEST

def layer_norm(values, gain, shift):
    center = values - lax.optimization_barrier(jnp.mean(values, axis=-1, keepdims=True))
    spread = lax.optimization_barrier(jnp.mean(center * center, axis=-1, keepdims=True))
    return center * lax.rsqrt(spread + EPS) * gain + shift

def rounded(values):
    return low_back(low(values))

def product(left, right):
    return jnp.dot(left, right, precision=HIGH, preferred_element_type=jnp.float32)

def structure(lengths_row, row_count):
    position = jnp.arange(row_count, dtype=jnp.int32)
    ends = jnp.cumsum(lengths_row, dtype=jnp.int32)
    starts = ends - lengths_row
    segment = lax.optimization_barrier(jnp.sum((position[:, None] >= ends[None, :]).astype(jnp.int32), axis=1, dtype=jnp.int32))
    live_rows = position < ends[-1]
    slot_ids = jnp.arange(lengths_row.shape[0], dtype=jnp.int32)
    owner = segment[:, None] == slot_ids[None, :]
    begin = lax.optimization_barrier(jnp.sum(jnp.where(owner, starts[None, :], 0), axis=1, dtype=jnp.int32))
    opening = live_rows & (position == begin)
    segment_id = jnp.where(live_rows, segment, lengths_row.shape[0] + position)
    return (segment_id, opening, live_rows)

def decoder(tokens, norm_params, bias_params, w_qkv, w_out, w_up, up_bias, w_down, causal, chooser, live_rows):
    row_count = tokens.shape[0]
    head_dim = D // HEADS
    scale = float(head_dim) ** (-0.5)
    hidden_one = low(layer_norm(tokens, norm_params[:, 0], norm_params[:, 1]))
    packed = product(hidden_one, w_qkv)
    queries = rounded(packed[:, :D] + bias_params[:, 0])
    keys_all = rounded(packed[:, D:2 * D])
    values_all = rounded(packed[:, 2 * D:] + bias_params[:, 1])
    query_heads = queries.reshape(row_count, HEADS, head_dim)
    key_heads = keys_all.reshape(row_count, HEADS, head_dim)
    value_heads = values_all.reshape(row_count, HEADS, head_dim)
    scores = low_back(jnp.einsum('ihd,jhd->hij', query_heads, key_heads, precision=HIGH) * scale)
    opened = jnp.maximum(scores[0], 0.0)
    chosen = jnp.where(chooser, opened * opened, 0.0)
    carried = jnp.cumsum(chosen, axis=0) - chosen
    logits = jnp.where(causal[None], scores - carried[None], NEG)
    weights_low = low(jax.nn.softmax(logits, axis=-1))
    mixed = rounded(jnp.einsum('hij,jhd->ihd', weights_low, value_heads, precision=HIGH).reshape(row_count, D))
    attended = low_back(product(mixed, w_out) + bias_params[:, 2])
    middle = tokens + attended
    hidden_two = low(layer_norm(middle, norm_params[:, 2], norm_params[:, 3]))
    inner = low_back(product(hidden_two, w_up) + up_bias.reshape(FF))
    activated = low(jax.nn.gelu(inner, approximate=True))
    branch = low_back(product(activated, w_down) + bias_params[:, 3])
    return jnp.where(live_rows[:, None], middle + branch, 0.0)

def reference(tokens, cotangent, lengths, norm_params, bias_params, w_qkv, w_out, w_up, up_bias, w_down):
    params = tuple((weight.astype(jnp.float32) for weight in (norm_params, bias_params, w_qkv, w_out, w_up, up_bias, w_down)))
    token_blocks = tokens.astype(jnp.float32).reshape(BUCKETS, TOK_DEV, D)
    cot_blocks = cotangent.astype(jnp.float32).reshape(BUCKETS, TOK_DEV, D)

    def visit(totals, current):
        block_tokens, block_cot, block_lengths = current
        segment_id, opening, live_rows = structure(block_lengths, TOK_DEV)
        position = jnp.arange(TOK_DEV, dtype=jnp.int32)
        same_doc = segment_id[:, None] == segment_id[None, :]
        causal = same_doc & (position[None, :] <= position[:, None])
        chooser = same_doc & (position[None, :] < position[:, None]) & jnp.logical_not(opening)[None, :]

        def apply_layer(block_in, *weights):
            return decoder(block_in, *weights, causal, chooser, live_rows)
        result, pull = jax.vjp(apply_layer, block_tokens, *params)
        grads = pull(block_cot)
        totals = tuple((total + grad_part for total, grad_part in zip(totals, grads[1:])))
        return (totals, (result.astype(jnp.bfloat16), grads[0].astype(jnp.bfloat16)))
    zeros = tuple((jnp.zeros_like(weight) for weight in params))
    totals, (outputs, input_grads) = lax.scan(visit, zeros, (token_blocks, cot_blocks, lengths))
    return (outputs.reshape(TOKENS, D), input_grads.reshape(TOKENS, D), totals[0], totals[1], totals[2], totals[3], totals[4], totals[5], totals[6])
```

```python
import functools

import jax
import jax.numpy as jnp
from jax import lax
from jax.experimental import pallas as pl
from jax.experimental.pallas import tpu as pltpu
from jax.sharding import PartitionSpec as P

HEADS = 12
EPS = 1e-05
BIG = 1e30
F32, BF16 = jnp.float32, jnp.bfloat16
VLIM = 60 << 20
MESH = pl.DeviceIdType.MESH

class Geo:
    def __init__(self, n_dp, n_fs):
        self.n_dp, self.n_fs = n_dp, n_fs
        self.ny = 2 if n_dp % 2 == 0 else 1
        self.nz = n_dp // self.ny
        self.nc = 2 if n_fs % 2 == 0 else 1
        self.nx = n_fs // self.nc

    def place(self):
        dp, fs = lax.axis_index("dp"), lax.axis_index("fsdp")
        return dp // self.ny, dp % self.ny, fs // self.nc, fs % self.nc

    def dev(self, z, y, x, c):
        return {"dp": z * self.ny + y, "fsdp": x * self.nc + c}


def others(n, me):
    return [lax.rem(me + k, n) for k in range(1, n)]

def barrier(geo):
    z, y, x, c = geo.place()
    sem = pltpu.get_barrier_semaphore()
    count = 0
    for k in range(1, geo.nz):
        pl.semaphore_signal(sem, inc=1, device_id=geo.dev(lax.rem(z + k, geo.nz), y, x, c), device_id_type=MESH); count += 1
    for k in range(1, geo.ny):
        pl.semaphore_signal(sem, inc=1, device_id=geo.dev(z, lax.rem(y + k, geo.ny), x, c), device_id_type=MESH); count += 1
    for k in range(1, geo.nx):
        pl.semaphore_signal(sem, inc=1, device_id=geo.dev(z, y, lax.rem(x + k, geo.nx), c), device_id_type=MESH); count += 1
    for k in range(1, geo.nc):
        pl.semaphore_signal(sem, inc=1, device_id=geo.dev(z, y, x, lax.rem(c + k, geo.nc)), device_id_type=MESH); count += 1
    pl.semaphore_wait(sem, count)

class Gather:
    def __init__(self, geo, shards, outs, sems):
        self.geo, self.shards, self.outs = geo, shards, outs
        self.lsem, self.s0, self.r0, self.s1, self.r1 = sems
        self.z, self.y, self.x, self.c = geo.place()

    def local(self, w, h):
        o = self.outs[w]
        return pltpu.make_async_copy(self.shards[w].at[h], o.at[self.x, self.c, self.z, self.y, h], self.lsem.at[w, h])

    def zcopy(self, w, h, k):
        g = self.geo
        zt = lax.rem(self.z + k, g.nz)
        return pltpu.make_async_remote_copy(
            src_ref=self.shards[w].at[h], dst_ref=self.outs[w].at[self.x, self.c, self.z, self.y, h],
            send_sem=self.s0.at[w, h, k], recv_sem=self.r0.at[w, h, k],
            device_id=g.dev(zt, self.y, self.x, self.c), device_id_type=MESH)

    def zrecv(self, w, h, k):
        g = self.geo
        zf = lax.rem(self.z + g.nz - k, g.nz)
        return pltpu.make_async_remote_copy(
            src_ref=self.shards[w].at[h], dst_ref=self.outs[w].at[self.x, self.c, zf, self.y, h],
            send_sem=self.s0.at[w, h, k], recv_sem=self.r0.at[w, h, k],
            device_id=g.dev(zf, self.y, self.x, self.c), device_id_type=MESH)

    def pair(self, w, h, stage, k, recv):
        g, o = self.geo, self.outs[w]
        z, y, x, c = self.z, self.y, self.x, self.c
        sgn = -1 if recv else 1
        kind = "c" if stage == 3 else ("y" if (stage == 1) == (h == 0) else "x")
        py = lax.rem(y + sgn * k + g.ny, g.ny); px = lax.rem(x + sgn * k + g.nx, g.nx); pc = lax.rem(c + sgn * k + g.nc, g.nc)
        def view(sx, sc, sy):
            if stage == 1: return o.at[sx, sc, :, sy, h]
            if stage == 2: return o.at[sx, sc, :, :, h] if kind == "x" else o.at[:, sc, :, sy, h]
            return o.at[:, sc, :, :, h]
        if kind == "y": peer = g.dev(z, py, x, c); pv = view(x, c, py)
        elif kind == "x": peer = g.dev(z, y, px, c); pv = view(px, c, y)
        else: peer = g.dev(z, y, x, pc); pv = view(x, pc, y)
        mine = view(x, c, y)
        ref = pv if recv else mine
        i = (w, h, stage - 1, k)
        return pltpu.make_async_remote_copy(src_ref=ref, dst_ref=ref, send_sem=self.s1.at[i], recv_sem=self.r1.at[i], device_id=peer, device_id_type=MESH)

    def npeers(self, h, stage):
        g = self.geo
        if stage == 3: return g.nc - 1
        return g.ny - 1 if (stage == 1) == (h == 0) else g.nx - 1

    def start(self, w, h, stage):
        g = self.geo
        if stage == 0:
            self.local(w, h).start()
            for k in range(1, g.nz): self.zcopy(w, h, k).start()
            return
        if stage == 1:
            self.local(w, h).wait()
            for k in range(1, g.nz): self.zrecv(w, h, k).wait_recv()
        else:
            for k in range(1, 1 + self.npeers(h, stage - 1)): self.pair(w, h, stage - 1, k, True).wait_recv()
        for k in range(1, 1 + self.npeers(h, stage)): self.pair(w, h, stage, k, False).start()

    def finish(self, w, h):
        for k in range(1, 1 + self.npeers(h, 3)): self.pair(w, h, 3, k, True).wait_recv()

    def drain(self, w, h):
        g = self.geo
        for k in range(1, g.nz): self.zcopy(w, h, k).wait_send()
        for stage in (1, 2, 3):
            for k in range(1, 1 + self.npeers(h, stage)): self.pair(w, h, stage, k, False).wait_send()

def gather_sems(geo, W):
    m = max(geo.nx, geo.ny, geo.nc)
    D = pltpu.SemaphoreType.DMA
    return [D((W, 2)), D((W, 2, geo.nz)), D((W, 2, geo.nz)), D((W, 2, 3, m)), D((W, 2, 3, m))]

def gather_kernel(geo, W, *refs):
    shards, outs, sems = refs[:W], refs[W:2 * W], refs[2 * W:]
    barrier(geo)
    G = Gather(geo, shards, outs, sems)
    for t in range(W + 4):
        for stage in range(4):
            w = t - stage
            if 0 <= w < W:
                for h in range(2): G.start(w, h, stage)
        if t >= 4:
            for h in range(2): G.finish(t - 4, h)
    for w in range(W):
        for h in range(2): G.drain(w, h)

def gather(geo, shards, collective_id=0):
    W = len(shards)
    outs = [jax.ShapeDtypeStruct((geo.nx, geo.nc, geo.nz, geo.ny) + s.shape, s.dtype) for s in shards]
    A = pl.BlockSpec(memory_space=pl.ANY)
    return pl.pallas_call(
        functools.partial(gather_kernel, geo, W), out_shape=outs, in_specs=[A] * W, out_specs=[A] * W,
        scratch_shapes=gather_sems(geo, W),
        compiler_params=pltpu.CompilerParams(collective_id=collective_id, has_side_effects=True, vmem_limit_bytes=16 << 20),
    )(*shards)

class Scatter:
    def __init__(self, geo, grads, outs, bufs, sems):
        self.geo, self.grads, self.outs, self.bufs = geo, grads, outs, bufs
        self.ss, self.rs = sems
        self.z, self.y, self.x, self.c = geo.place()

    def copies(self, w, h, stage):
        g, q = self.geo, self.grads[w]
        b1, b2, b3, b4 = self.bufs[4 * w : 4 * w + 4]
        z, y, x, c = self.z, self.y, self.x, self.c
        pc, py, px = 1 - c, 1 - y, 1 - x
        if stage == 0:
            moves = [(q.at[:, pc, :, :, h], b1.at[h], g.dev(z, y, x, pc))]
        elif stage == 1 and h == 0:
            moves = [(b1.at[0, px, :, k], b2.at[0, k], g.dev(z, y, px, c)) for k in range(g.ny)]
        elif stage == 1:
            moves = [(b1.at[1, :, :, py], b2.at[1], g.dev(z, py, x, c))]
        elif stage == 2:
            moves = [(b2.at[h, py if h == 0 else px], b3.at[h], g.dev(z, py, x, c) if h == 0 else g.dev(z, y, px, c))]
        else:
            moves = []
            for k in range(1, g.nz):
                zt = lax.rem(z + k, g.nz)
                moves.append((b3.at[h, zt], b4.at[h, k - 1], g.dev(zt, y, x, c)))
        return [
            pltpu.make_async_remote_copy(src_ref=s, dst_ref=d, send_sem=self.ss.at[w, h, stage, i], recv_sem=self.rs.at[w, h, stage, i], device_id=p, device_id_type=MESH)
            for i, (s, d, p) in enumerate(moves)
        ]

    def add(self, w, h, stage):
        g, q = self.geo, self.grads[w]
        b1, b2, b3, b4 = self.bufs[4 * w : 4 * w + 4]
        z, y, x, c = self.z, self.y, self.x, self.c

        def into(ref, at, other):
            ref[at] = (ref[at].astype(F32) + other.astype(F32)).astype(ref.dtype)

        if stage == 0:
            def one(i, _):
                xx, zz, yy = i // (g.nz * g.ny), (i // g.ny) % g.nz, i % g.ny
                into(b1, (h, xx, zz, yy), q[xx, c, zz, yy, h])
                return 0
            lax.fori_loop(0, g.nx * g.nz * g.ny, one, 0)
        elif stage == 1:
            def one(i, _):
                k, zz = i // g.nz, i % g.nz
                into(b2, (h, k, zz), b1[0, x, zz, k] if h == 0 else b1[1, k, zz, y])
                return 0
            lax.fori_loop(0, 2 * g.nz, one, 0)
        elif stage == 2:
            def one(i, _):
                into(b3, (h, i), b2[h, y if h == 0 else x, i])
                return 0
            lax.fori_loop(0, g.nz, one, 0)
        else:
            if g.nz <= 8:
                total = b3[h, z].astype(F32)
                for k in range(g.nz - 1):
                    total = total + b4[h, k].astype(F32)
            else:
                total = lax.fori_loop(0, g.nz - 1, lambda k, t: t + b4[h, k].astype(F32), b3[h, z].astype(F32))
            self.outs[w][h] = total

    def step(self, w, h, stage):
        if stage > 0:
            for cp in self.copies(w, h, stage - 1):
                cp.wait_recv()
            self.add(w, h, stage - 1)
        if stage < 4:
            for cp in self.copies(w, h, stage):
                cp.start()

    def drain(self, w, h):
        for stage in range(4):
            for cp in self.copies(w, h, stage):
                cp.wait_send()


def scatter_bufs(geo, shapes):
    out = []
    for s in shapes:
        r, t, d = s.shape[-2], s.shape[-1], s.dtype
        out += [
            pltpu.VMEM((2, geo.nx, geo.nz, geo.ny, r, t), d), pltpu.VMEM((2, 2, geo.nz, r, t), d),
            pltpu.VMEM((2, geo.nz, r, t), d), pltpu.VMEM((2, geo.nz - 1, r, t), d),
        ]
    return out


def scatter_sems(geo, W):
    n = max(2, geo.nz - 1)
    return [pltpu.SemaphoreType.DMA((W, 2, 4, n)), pltpu.SemaphoreType.DMA((W, 2, 4, n))]


def scatter_kernel(geo, W, *refs):
    grads, outs, bufs, sems = refs[:W], refs[W : 2 * W], refs[2 * W : 6 * W], refs[6 * W :]
    barrier(geo)
    S = Scatter(geo, grads, outs, bufs, sems)
    for t in range(W + 4):
        for stage in range(5):
            w = t - stage
            if 0 <= w < W:
                for h in range(2):
                    S.step(w, h, stage)
    for w in range(W):
        for h in range(2):
            S.drain(w, h)


def scatter(geo, grads, collective_id):
    W = len(grads)
    V = pl.BlockSpec(memory_space=pltpu.VMEM)
    return pl.pallas_call(
        functools.partial(scatter_kernel, geo, W),
        out_shape=[jax.ShapeDtypeStruct(g.shape[4:], F32) for g in grads],
        in_specs=[V] * W, out_specs=[V] * W,
        scratch_shapes=scatter_bufs(geo, grads) + scatter_sems(geo, W),
        compiler_params=pltpu.CompilerParams(collective_id=collective_id, has_side_effects=True, vmem_limit_bytes=60 << 20),
        name="scatter",
    )(*grads)


def nn(a, b):
    return lax.dot_general(a, b, (((1,), (0,)), ((), ())), preferred_element_type=F32)


def nt(a, b):
    return lax.dot_general(a, b, (((1,), (1,)), ((), ())), preferred_element_type=F32)


def tn(a, b):
    return lax.dot_general(a, b, (((0,), (0,)), ((), ())), preferred_element_type=F32)


def vm():
    return pl.BlockSpec(memory_space=pltpu.VMEM)


def sm():
    return pl.BlockSpec(memory_space=pltpu.SMEM)


def ends_of(len_ref):
    total, starts, ends = jnp.int32(0), [], []
    for t in range(len_ref.shape[1]):
        starts.append(total)
        total = total + len_ref[0, t]
        ends.append(total)
    return starts, ends


def segment(pos, ends):
    seg = jnp.zeros_like(pos)
    for e in ends:
        seg = seg + (pos >= e).astype(jnp.int32)
    return jnp.where(pos < ends[-1], seg, len(ends) + pos)


def opens(pos, starts, ends):
    hit = jnp.zeros_like(pos)
    for s in starts:
        hit = jnp.where(pos == s, 1, hit)
    return jnp.where(pos < ends[-1], hit, 0)


def lane_half(rows, which):
    lane = lax.broadcasted_iota(jnp.int32, (rows, 128), 1)
    return (lane < 64) if which == 0 else (lane >= 64)


def only(x, which):
    return jnp.where(lane_half(x.shape[0], which), x, jnp.zeros_like(x))


def masks(len_ref, r0, R, J):
    starts, ends = ends_of(len_ref)
    row = lax.broadcasted_iota(jnp.int32, (R, 1), 0) + r0
    col = lax.broadcasted_iota(jnp.int32, (1, J), 1)
    same = segment(row, ends) == segment(col, ends)
    allow = same & (col <= row)
    pick = same & (col < row) & (opens(col, starts, ends) == 0)
    return allow, pick


def ln_stats(x):
    center = x - jnp.mean(x, axis=-1, keepdims=True)
    spread = jnp.mean(center * center, axis=-1, keepdims=True)
    r = lax.rsqrt(spread + EPS)
    return center * r, r


def ln_back(g_h, n, r, gain):
    g_n = g_h * gain
    return r * (g_n - jnp.mean(g_n, axis=-1, keepdims=True) - n * jnp.mean(g_n * n, axis=-1, keepdims=True))


def unpack_cols(blk_ref, full_ref):
    n, _, w = blk_ref.shape
    for f in range(n):
        full_ref[:, f * w : (f + 1) * w] = blk_ref[f]


def qkv_kernel(x_ref, par_ref, w_ref, h1_ref, q_ref, k_ref, v_ref, wf):
    unpack_cols(w_ref, wf)
    D = x_ref.shape[1]
    R = 256
    for b in range(x_ref.shape[0] // R):
        rows = pl.ds(b * R, R)
        n, _ = ln_stats(x_ref[rows, :].astype(F32))
        h1 = (n * par_ref[0:1, :] + par_ref[1:2, :]).astype(BF16)
        h1_ref[rows, :] = h1
        q = (nn(h1, wf[:, 0:D]) + par_ref[4:5, :]).astype(BF16)
        q_ref[rows, :] = q * jnp.asarray(0.125, BF16)
        k_ref[rows, :] = nn(h1, wf[:, D : 2 * D]).astype(BF16)
        v_ref[rows, :] = (nn(h1, wf[:, 2 * D : 3 * D]) + par_ref[5:6, :]).astype(BF16)


def qkv(x, par, w):
    s = jax.ShapeDtypeStruct(x.shape, BF16)
    return pl.pallas_call(
        qkv_kernel, out_shape=[s] * 4, in_specs=[vm()] * 3, out_specs=[vm()] * 4,
        scratch_shapes=[pltpu.VMEM((w.shape[1], w.shape[0] * w.shape[2]), BF16)],
        compiler_params=pltpu.CompilerParams(vmem_limit_bytes=VLIM),
        name="qkv",
    )(x, par, w)


def attn_fwd_block(b, R, len_ref, q_ref, k_ref, v_ref, o_ref, lse_ref, cm_ref, carry):
    r0, J = b * R, (b + 1) * R
    rows = pl.ds(r0, R)
    allow, pick = masks(len_ref, r0, R, J)
    s0 = jnp.maximum(nt(only(q_ref[rows, 0:128], 0), k_ref[0:J, 0:128]), 0.0)
    chosen = jnp.where(pick, s0 * s0, 0.0)
    hi = chosen.astype(BF16)
    lo = (chosen - hi.astype(F32)).astype(BF16)
    i = lax.broadcasted_iota(jnp.int32, (R, R), 0)
    j = lax.broadcasted_iota(jnp.int32, (R, R), 1)
    lower = jnp.where(j < i, 1.0, 0.0).astype(BF16)
    carried = carry[0:1, 0:J] + (nn(lower, hi) + nn(lower, lo))
    cm_ref[rows, 0:J] = jnp.where(allow, carried, BIG)
    carry[0:1, 0:J] = carry[0:1, 0:J] + jnp.sum(chosen, axis=0, keepdims=True)

    lane = lax.broadcasted_iota(jnp.int32, (R, 128), 1)

    def pair(p, lse_acc):
        cols = pl.ds(pl.multiple_of(p * 128, 128), 128)
        q2, k2, v2 = q_ref[rows, cols], k_ref[0:J, cols], v_ref[0:J, cols]
        outs = []
        for half in range(2):
            logits = nt(only(q2, half), k2) - cm_ref[rows, 0:J]
            m = jnp.max(logits, axis=1, keepdims=True)
            e = jnp.exp(logits - m)
            t = jnp.sum(e, axis=1, keepdims=True)
            pr = (e * (1.0 / t)).astype(BF16)
            outs.append(nn(pr, v2))
            lse_acc = jnp.where(lane == 2 * p + half, m + jnp.log(t), lse_acc)
        o_ref[rows, cols] = jnp.where(lane < 64, outs[0], outs[1]).astype(BF16)
        return lse_acc

    lse_ref[rows, :] = lax.fori_loop(0, HEADS // 2, pair, jnp.zeros((R, 128), F32))


def attn_fwd_kernel(R, len_ref, q_ref, k_ref, v_ref, o_ref, lse_ref, cm_ref, carry):
    carry[...] = jnp.zeros_like(carry)
    for b in range(q_ref.shape[0] // R):
        attn_fwd_block(b, R, len_ref, q_ref, k_ref, v_ref, o_ref, lse_ref, cm_ref, carry)


def attn_fwd(lengths, q, k, v, R=256):
    T = q.shape[0]
    return pl.pallas_call(
        functools.partial(attn_fwd_kernel, R),
        out_shape=[jax.ShapeDtypeStruct(q.shape, BF16), jax.ShapeDtypeStruct((T, 128), F32), jax.ShapeDtypeStruct((T, T), F32)],
        in_specs=[sm()] + [vm()] * 3, out_specs=[vm()] * 3,
        scratch_shapes=[pltpu.VMEM((8, T), F32)],
        compiler_params=pltpu.CompilerParams(vmem_limit_bytes=VLIM),
        name="attn_fwd",
    )(lengths, q, k, v)


def unpack_pairs(blk_ref, full_ref):
    n, w = blk_ref.shape[0], blk_ref.shape[3] // 2
    for f in range(n):
        for s in range(2):
            full_ref[:, s, :, f * w : (f + 1) * w] = blk_ref[f, :, :, s * w : (s + 1) * w]


def mlp_kernel(R, len_ref, x_ref, cot_ref, mix_ref, par_ref, upb_ref, wo_ref, wu_ref, wd_ref,
               out_ref, gmid_ref, gmix_ref, small_ref, gub_ref, dwo_ref, dwu_ref, dwd_ref,
               wo, wd, act, gin, h2s, gbs):
    T, D = x_ref.shape
    FF = upb_ref.shape[1]
    nf, wf = wu_ref.shape[0], wu_ref.shape[2]
    unpack_cols(wo_ref, wo)
    unpack_pairs(wd_ref, wd)
    _, ends = ends_of(len_ref)
    small_ref[...] = jnp.zeros_like(small_ref)
    gub_ref[...] = jnp.zeros_like(gub_ref)
    cpf = wd.shape[0] // nf
    C0, C1 = 0.7978845608028654, 0.044715

    def block(b, _):
        rows = pl.ds(pl.multiple_of(b * R, R), R)
        x = x_ref[rows, :].astype(F32)
        middle = x + nn(mix_ref[rows, :], wo[...]) + par_ref[6:7, :]
        n2, r2 = ln_stats(middle)
        h2 = (n2 * par_ref[2:3, :] + par_ref[3:4, :]).astype(BF16)
        h2s[rows, :] = h2
        pos = lax.broadcasted_iota(jnp.int32, (R, 1), 0) + b * R
        live = pos < ends[-1]
        gb = jnp.where(live, cot_ref[rows, :].astype(F32), 0.0)
        gbl = gb.astype(BF16)
        gbs[rows, :] = gbl
        branch = jnp.zeros((R, D), F32)
        g_h2 = jnp.zeros((R, D), F32)
        for f in range(nf):
            cols = pl.ds(f * wf, wf)
            wdf = wd[f * cpf : (f + 1) * cpf].reshape(wf, D)
            u = nn(h2, wu_ref[f]) + upb_ref[0:1, f * wf : (f + 1) * wf]
            g_act = nt(gbl, wdf)
            u2 = u * u
            t = jnp.tanh(u * (C0 + (C0 * C1) * u2))
            hp = 0.5 + 0.5 * t
            a = u * hp
            al = a.astype(BF16)
            act[rows, cols] = al
            branch = branch + nn(al, wdf)
            d = hp + (a - a * hp) * (2.0 * C0 + (6.0 * C0 * C1) * u2)
            gi = (g_act * d).astype(BF16)
            gin[rows, cols] = gi
            gub_ref[0:1, f * wf : (f + 1) * wf] += jnp.sum(gi.astype(F32), axis=0, keepdims=True)
            g_h2 = g_h2 + nt(gi, wu_ref[f])
        out_ref[rows, :] = jnp.where(live, middle + branch + par_ref[7:8, :], 0.0).astype(BF16)
        small_ref[2:3, :] += jnp.sum(g_h2 * n2, axis=0, keepdims=True)
        small_ref[3:4, :] += jnp.sum(g_h2, axis=0, keepdims=True)
        g_mid = gb + ln_back(g_h2, n2, r2, par_ref[2:3, :])
        gmid_ref[rows, :] = g_mid
        gml = g_mid.astype(BF16)
        small_ref[6:7, :] += jnp.sum(gml.astype(F32), axis=0, keepdims=True)
        small_ref[7:8, :] += jnp.sum(gb, axis=0, keepdims=True)
        gmix_ref[rows, :] = nt(gml, wo[...]).astype(BF16)
        return 0

    lax.fori_loop(0, T // R, block, 0)
    w4 = D // nf

    def put(ref, grad, lead):
        r = ref.shape[2]
        c = grad.shape[0] // (2 * r)
        g = grad.astype(BF16).reshape(c, 2, r, D)
        for f in range(nf):
            for s in range(2):
                ref[f, pl.ds(lead, c), :, s * w4 : (s + 1) * w4] = g[:, s, :, f * w4 : (f + 1) * w4]

    def outp(i, _):
        g = tn(mix_ref[:, pl.ds(pl.multiple_of(i * 384, 128), 384)], gmid_ref[...].astype(BF16)).astype(BF16)
        for f in range(nf):
            dwo_ref[f, pl.ds(pl.multiple_of(i * 384, 128), 384), :] = g[:, f * w4 : (f + 1) * w4]
        return 0

    lax.fori_loop(0, D // 384, outp, 0)
    K = 384
    cpk = K // (2 * dwd_ref.shape[2])

    def down(i, _):
        put(dwd_ref, tn(act[:, pl.ds(pl.multiple_of(i * K, 128), K)], gbs[...]), i * cpk)
        return 0

    lax.fori_loop(0, FF // K, down, 0)
    H = 384

    def up(i, _):
        f, s = i // (wf // H), i % (wf // H)
        dwu_ref[f, :, pl.ds(pl.multiple_of(s * H, 128), H)] = tn(h2s[...], gin[:, pl.ds(pl.multiple_of(i * H, 128), H)]).astype(BF16)
        return 0

    lax.fori_loop(0, FF // H, up, 0)


def mlp(lengths, x, cot, mixed, par, upb, wo, wu, wd, R=256):
    T, D = x.shape
    FF = upb.shape[1]
    S = jax.ShapeDtypeStruct
    V = pltpu.VMEM
    return pl.pallas_call(
        functools.partial(mlp_kernel, R),
        out_shape=[S((T, D), BF16), S((T, D), F32), S((T, D), BF16), S((8, D), F32), S((8, FF), F32),
                   S(wo.shape, BF16), S(wu.shape, BF16), S(wd.shape, BF16)],
        in_specs=[sm()] + [vm()] * 8, out_specs=[vm()] * 8,
        scratch_shapes=[V((D, D), BF16), V((wd.shape[1], 2, wd.shape[2], D), BF16),
                        V((T, FF), BF16), V((T, FF), BF16), V((T, D), BF16), V((T, D), BF16)],
        compiler_params=pltpu.CompilerParams(vmem_limit_bytes=VLIM),
        name="mlp",
    )(lengths, x, cot, mixed, par, upb, wo, wu, wd)


def attn_bwd_block(b, R, len_ref, q_ref, k_ref, v_ref, do_ref, o_ref, lse_ref, cm_ref, gp_ref, dkT, dvT, G, later):
    D = q_ref.shape[1]
    r0, J = b * R, (b + 1) * R
    rows = pl.ds(r0, R)
    lane = lax.broadcasted_iota(jnp.int32, (R, 128), 1)

    def load(p):
        cols = p * 128 if isinstance(p, int) else pl.multiple_of(p * 128, 128)
        c = pl.ds(cols, 128)
        return q_ref[rows, c], k_ref[0:J, c], v_ref[0:J, c], do_ref[rows, c], o_ref[rows, c]

    def head(p, half, t, raw=None):
        q2, k2, v2, do2, o2 = t
        prod = only(do2.astype(F32) * o2.astype(F32), half)
        dsum = jnp.sum(prod, axis=1, keepdims=True)
        lse = jnp.sum(jnp.where(lane == 2 * p + half, lse_ref[rows, :], 0.0), axis=1, keepdims=True)
        s = nt(only(q2, half), k2)
        pr = jnp.exp(s - cm_ref[rows, 0:J] - lse)
        dp = nt(only(do2, half), v2)
        return s, pr.astype(BF16), pr * (dp - dsum)

    def finish(p, t, prA, prB, dsA, dsB):
        q2, k2, v2, do2, o2 = t
        cols = p * 128 if isinstance(p, int) else pl.multiple_of(p * 128, 128)
        c = pl.ds(cols, 128)
        dq = jnp.where(lane < 64, nn(dsA, k2), nn(dsB, k2)) * 0.125
        gp_ref[rows, c] = dq.astype(BF16)
        qT, doT = jnp.transpose(q2), jnp.transpose(do2)
        dkT[c, 0:J] += jnp.concatenate([nn(qT[0:64], dsA), nn(qT[64:128], dsB)], axis=0)
        dvT[c, 0:J] += jnp.concatenate([nn(doT[0:64], prA), nn(doT[64:128], prB)], axis=0)

    G[:, 0:J] = jnp.zeros((R, J), F32)

    def pair(k, _):
        p = HEADS // 2 - 1 - k
        t = load(p)
        _, prA, dsA = head(p, 0, t)
        _, prB, dsB = head(p, 1, t)
        G[:, 0:J] += dsA + dsB
        finish(p, t, prA, prB, dsA.astype(BF16), dsB.astype(BF16))
        return 0

    lax.fori_loop(0, HEADS // 2 - 1, pair, 0)
    t = load(0)
    _, prB, dsB = head(0, 1, t)
    s0, prA, dsA = head(0, 0, t)
    g = -(G[:, 0:J] + dsA + dsB)
    hi = g.astype(BF16)
    lo = (g - hi.astype(F32)).astype(BF16)
    i = lax.broadcasted_iota(jnp.int32, (R, R), 0)
    j = lax.broadcasted_iota(jnp.int32, (R, R), 1)
    upper = jnp.where(j > i, 1.0, 0.0).astype(BF16)
    g_chosen = later[0:1, 0:J] + (nn(upper, hi) + nn(upper, lo))
    later[0:1, 0:J] = later[0:1, 0:J] + jnp.sum(g, axis=0, keepdims=True)
    _, pick = masks(len_ref, r0, R, J)
    dsA = dsA + jnp.where(pick, 2.0 * jnp.maximum(s0, 0.0) * g_chosen, 0.0)
    finish(0, t, prA, prB, dsA.astype(BF16), dsB.astype(BF16))


def attn_bwd_kernel(R, len_ref, q_ref, k_ref, v_ref, do_ref, o_ref, lse_ref, cm_ref, gp_ref, dkT, dvT, G, later):
    T, D = q_ref.shape
    dkT[...] = jnp.zeros_like(dkT)
    dvT[...] = jnp.zeros_like(dvT)
    later[...] = jnp.zeros_like(later)
    for b in reversed(range(T // R)):
        attn_bwd_block(b, R, len_ref, q_ref, k_ref, v_ref, do_ref, o_ref, lse_ref, cm_ref, gp_ref, dkT, dvT, G, later)

    def turn(p, _):
        c = pl.ds(pl.multiple_of(p * 128, 128), 128)
        ck = pl.ds(pl.multiple_of(D + p * 128, 128), 128)
        cv = pl.ds(pl.multiple_of(2 * D + p * 128, 128), 128)
        gp_ref[:, ck] = jnp.transpose(dkT[c, :]).astype(BF16)
        gp_ref[:, cv] = jnp.transpose(dvT[c, :]).astype(BF16)
        return 0

    lax.fori_loop(0, HEADS // 2, turn, 0)


def attn_bwd(lengths, q, k, v, do, o, lse, cm, R=256):
    T, D = q.shape
    V = pltpu.VMEM
    return pl.pallas_call(
        functools.partial(attn_bwd_kernel, R),
        out_shape=jax.ShapeDtypeStruct((T, 3 * D), BF16),
        in_specs=[sm()] + [vm()] * 7, out_specs=vm(),
        scratch_shapes=[V((D, T), F32), V((D, T), F32), V((R, T), F32), V((8, T), F32)],
        compiler_params=pltpu.CompilerParams(vmem_limit_bytes=VLIM),
        name="attn_bwd",
    )(lengths, q, k, v, do, o, lse, cm)


def qkv_back_kernel(x_ref, h1_ref, gp_ref, gmid_ref, par_ref, w_ref, ig_ref, small_ref, dw_ref):
    T, D = x_ref.shape
    n, _, w = w_ref.shape
    R = 256
    for f in range(n):
        dw_ref[f] = tn(h1_ref[...], gp_ref[:, f * w : (f + 1) * w]).astype(BF16)
    small_ref[...] = jnp.zeros_like(small_ref)
    for b in range(T // R):
        rows = pl.ds(b * R, R)
        g_h1 = jnp.zeros((R, D), F32)
        for f in range(n):
            g_h1 = g_h1 + nt(gp_ref[rows, f * w : (f + 1) * w], w_ref[f])
        n1, r1 = ln_stats(x_ref[rows, :].astype(F32))
        small_ref[0:1, :] += jnp.sum(g_h1 * n1, axis=0, keepdims=True)
        small_ref[1:2, :] += jnp.sum(g_h1, axis=0, keepdims=True)
        small_ref[4:5, :] += jnp.sum(gp_ref[rows, 0:D].astype(F32), axis=0, keepdims=True)
        small_ref[5:6, :] += jnp.sum(gp_ref[rows, 2 * D : 3 * D].astype(F32), axis=0, keepdims=True)
        ig_ref[rows, :] = (gmid_ref[rows, :] + ln_back(g_h1, n1, r1, par_ref[0:1, :])).astype(BF16)


def qkv_back(x, h1, gp, gmid, par, w):
    S = jax.ShapeDtypeStruct
    return pl.pallas_call(
        qkv_back_kernel, out_shape=[S(x.shape, BF16), S((8, x.shape[1]), F32), S(w.shape, BF16)],
        in_specs=[vm()] * 6, out_specs=[vm()] * 3,
        compiler_params=pltpu.CompilerParams(vmem_limit_bytes=VLIM),
        name="qkv_back",
    )(x, h1, gp, gmid, par, w)


def pair_up(shard):
    w = shard.shape[1]
    return shard.reshape(2, 2, -1, w).transpose(0, 2, 1, 3).reshape(2, -1, 2 * w)


def pair_down(halves):
    w = halves.shape[2] // 2
    return halves.reshape(2, -1, 2, w).transpose(0, 2, 1, 3).reshape(-1, w)


def repair(blocks, r):
    n, c, r0, w2 = blocks.shape
    if r0 == r:
        return blocks
    w = w2 // 2
    flat = blocks.reshape(n, c, r0, 2, w).transpose(0, 1, 3, 2, 4).reshape(n, -1, 2, r, w)
    return flat.transpose(0, 1, 3, 2, 4).reshape(n, -1, r, w2)


def body(geo, tokens, cotangent, lengths, norm_params, bias_params, w_qkv, w_out, w_up, up_bias, w_down):
    T, D = tokens.shape
    F, n_dp, per = geo.n_fs, geo.n_dp, D // geo.n_dp
    FF = D * up_bias.shape[1] * F
    tiny = jnp.stack([jnp.stack([norm_params[:, 0], bias_params[:, 0]]), jnp.stack([up_bias[:, 0]] * 2)])
    tiny = jnp.pad(tiny, ((0, 0), (0, 14), (0, 128 - per)))

    def halves(shard):
        return shard.reshape(2, -1, shard.shape[1])

    bufs = gather(geo, [tiny, halves(w_qkv), halves(w_out), halves(w_up), pair_up(w_down)])
    t = bufs[0].reshape(F, n_dp, 2, 16, 128)[..., :per].astype(F32)
    par = jnp.concatenate([t[:, :, 0, 0].reshape(F, D), t[:, :, 0, 1].reshape(F, D)], axis=0)
    upb = jnp.broadcast_to(t[:, :, 1, 0].reshape(F, D).T.reshape(1, FF), (8, FF))
    wq, wo, wu = (b.reshape(F, D, b.shape[-1]) for b in bufs[1:4])
    chunk = FF // 32
    wd = repair(bufs[4].reshape((F, n_dp * 2) + bufs[4].shape[-2:]), chunk)

    h1, q, k, v = qkv(tokens, par, wq)
    mixed, lse, cm = attn_fwd(lengths, q, k, v)
    out, gmid, gmix, small_b, gub, dwo, dwu, dwd = mlp(lengths, tokens, cotangent, mixed, par, upb, wo, wu, wd)
    gp = attn_bwd(lengths, q, k, v, gmix, mixed, lse, cm)
    ig, small_a, dwq = qkv_back(tokens, h1, gp, gmid, par, wq)

    small = small_a + small_b
    rows = jnp.stack([small[0:4], small[4:8]]).reshape(2, F, n_dp, per)
    ub = gub[0].reshape(D, F).T.reshape(F, n_dp, per)
    g_tiny = jnp.stack([jnp.stack([rows[0], rows[1]], axis=2), jnp.stack([ub, ub], axis=2)], axis=2)
    g_tiny = jnp.pad(g_tiny, ((0, 0), (0, 0), (0, 0), (0, 6), (0, 128 - per)))

    def split(grad, r):
        return grad.reshape((geo.nx, geo.nc, geo.nz, geo.ny, 2, r, grad.shape[-1]))

    r = per // 2
    dwd = repair(dwd, FF // n_dp // 4)
    parts = [split(g_tiny, 8), split(dwo, r), split(dwu, r), split(dwd, FF // n_dp // 4), split(dwq, r)]
    s_tiny, s_out, s_up, s_down, s_qkv = scatter(geo, parts, 1)
    return (
        out,
        ig,
        s_tiny[0, 0, :per, None],
        s_tiny[0, 1, :per, None],
        s_qkv.reshape(-1, s_qkv.shape[-1]),
        s_out.reshape(-1, s_out.shape[-1]),
        s_up.reshape(-1, s_up.shape[-1]),
        s_tiny[1, 0, :per, None],
        pair_down(s_down),
    )


def solution(mesh):
    geo = Geo(mesh.shape["dp"], mesh.shape["fsdp"])
    both, split = P(("dp", "fsdp"), None), P("dp", "fsdp")
    return jax.shard_map(
        functools.partial(body, geo), mesh=mesh, in_specs=(both,) * 3 + (split,) * 7, out_specs=(both,) * 2 + (split,) * 7, check_vma=False
    )
```

```python
import functools

import jax
import jax.numpy as jnp
from jax import lax
from jax.experimental import pallas as pl
from jax.experimental.pallas import tpu as pltpu
from jax.sharding import PartitionSpec as P

HEADS = 12
EPS = 1e-05
BIG = 1e30
B = 256
F32, BF16 = jnp.float32, jnp.bfloat16
VLIM = 60 << 20
MESH = pl.DeviceIdType.MESH


class Geo:
    def __init__(self, n_dp, n_fs):
        self.n_dp, self.n_fs = n_dp, n_fs
        self.ny = 2 if n_dp % 2 == 0 else 1
        self.nz = n_dp // self.ny
        self.nc = 2 if n_fs % 2 == 0 else 1
        self.nx = n_fs // self.nc

    def place(self):
        dp, fs = lax.axis_index("dp"), lax.axis_index("fsdp")
        return dp // self.ny, dp % self.ny, fs // self.nc, fs % self.nc

    def dev(self, z, y, x, c):
        return {"dp": z * self.ny + y, "fsdp": x * self.nc + c}


def others(n, me):
    return [lax.rem(me + k, n) for k in range(1, n)]

def barrier(geo):
    z, y, x, c = geo.place()
    sem = pltpu.get_barrier_semaphore()
    count = 0
    for k in range(1, geo.nz):
        pl.semaphore_signal(sem, inc=1, device_id=geo.dev(lax.rem(z + k, geo.nz), y, x, c), device_id_type=MESH); count += 1
    for k in range(1, geo.ny):
        pl.semaphore_signal(sem, inc=1, device_id=geo.dev(z, lax.rem(y + k, geo.ny), x, c), device_id_type=MESH); count += 1
    for k in range(1, geo.nx):
        pl.semaphore_signal(sem, inc=1, device_id=geo.dev(z, y, lax.rem(x + k, geo.nx), c), device_id_type=MESH); count += 1
    for k in range(1, geo.nc):
        pl.semaphore_signal(sem, inc=1, device_id=geo.dev(z, y, x, lax.rem(c + k, geo.nc)), device_id_type=MESH); count += 1
    pl.semaphore_wait(sem, count)

class Gather:
    def __init__(self, geo, shards, outs, sems):
        self.geo, self.shards, self.outs = geo, shards, outs
        self.lsem, self.s0, self.r0, self.s1, self.r1 = sems
        self.z, self.y, self.x, self.c = geo.place()

    def local(self, w, h):
        o = self.outs[w]
        return pltpu.make_async_copy(self.shards[w].at[h], o.at[self.x, self.c, self.z, self.y, h], self.lsem.at[w, h])

    def zcopy(self, w, h, k):
        g = self.geo
        zt = lax.rem(self.z + k, g.nz)
        return pltpu.make_async_remote_copy(
            src_ref=self.shards[w].at[h], dst_ref=self.outs[w].at[self.x, self.c, self.z, self.y, h],
            send_sem=self.s0.at[w, h, k], recv_sem=self.r0.at[w, h, k],
            device_id=g.dev(zt, self.y, self.x, self.c), device_id_type=MESH)

    def zrecv(self, w, h, k):
        g = self.geo
        zf = lax.rem(self.z + g.nz - k, g.nz)
        return pltpu.make_async_remote_copy(
            src_ref=self.shards[w].at[h], dst_ref=self.outs[w].at[self.x, self.c, zf, self.y, h],
            send_sem=self.s0.at[w, h, k], recv_sem=self.r0.at[w, h, k],
            device_id=g.dev(zf, self.y, self.x, self.c), device_id_type=MESH)

    def pair(self, w, h, stage, k, recv):
        g, o = self.geo, self.outs[w]
        z, y, x, c = self.z, self.y, self.x, self.c
        sgn = -1 if recv else 1
        kind = "c" if stage == 3 else ("y" if (stage == 1) == (h == 0) else "x")
        py = lax.rem(y + sgn * k + g.ny, g.ny); px = lax.rem(x + sgn * k + g.nx, g.nx); pc = lax.rem(c + sgn * k + g.nc, g.nc)
        def view(sx, sc, sy):
            if stage == 1: return o.at[sx, sc, :, sy, h]
            if stage == 2: return o.at[sx, sc, :, :, h] if kind == "x" else o.at[:, sc, :, sy, h]
            return o.at[:, sc, :, :, h]
        if kind == "y": peer = g.dev(z, py, x, c); pv = view(x, c, py)
        elif kind == "x": peer = g.dev(z, y, px, c); pv = view(px, c, y)
        else: peer = g.dev(z, y, x, pc); pv = view(x, pc, y)
        mine = view(x, c, y)
        ref = pv if recv else mine
        i = (w, h, stage - 1, k)
        return pltpu.make_async_remote_copy(src_ref=ref, dst_ref=ref, send_sem=self.s1.at[i], recv_sem=self.r1.at[i], device_id=peer, device_id_type=MESH)

    def npeers(self, h, stage):
        g = self.geo
        if stage == 3: return g.nc - 1
        return g.ny - 1 if (stage == 1) == (h == 0) else g.nx - 1

    def start(self, w, h, stage):
        g = self.geo
        if stage == 0:
            self.local(w, h).start()
            for k in range(1, g.nz): self.zcopy(w, h, k).start()
            return
        if stage == 1:
            self.local(w, h).wait()
            for k in range(1, g.nz): self.zrecv(w, h, k).wait_recv()
        else:
            for k in range(1, 1 + self.npeers(h, stage - 1)): self.pair(w, h, stage - 1, k, True).wait_recv()
        for k in range(1, 1 + self.npeers(h, stage)): self.pair(w, h, stage, k, False).start()

    def finish(self, w, h):
        for k in range(1, 1 + self.npeers(h, 3)): self.pair(w, h, 3, k, True).wait_recv()

    def drain(self, w, h):
        g = self.geo
        for k in range(1, g.nz): self.zcopy(w, h, k).wait_send()
        for stage in (1, 2, 3):
            for k in range(1, 1 + self.npeers(h, stage)): self.pair(w, h, stage, k, False).wait_send()

def gather_sems(geo, W):
    m = max(geo.nx, geo.ny, geo.nc)
    D = pltpu.SemaphoreType.DMA
    return [D((W, 2)), D((W, 2, geo.nz)), D((W, 2, geo.nz)), D((W, 2, 3, m)), D((W, 2, 3, m))]

def gather_kernel(geo, W, *refs):
    shards, outs, sems = refs[:W], refs[W:2 * W], refs[2 * W:]
    barrier(geo)
    G = Gather(geo, shards, outs, sems)
    for t in range(W + 4):
        for stage in range(4):
            w = t - stage
            if 0 <= w < W:
                for h in range(2): G.start(w, h, stage)
        if t >= 4:
            for h in range(2): G.finish(t - 4, h)
    for w in range(W):
        for h in range(2): G.drain(w, h)

def gather(geo, shards, collective_id=0):
    W = len(shards)
    outs = [jax.ShapeDtypeStruct((geo.nx, geo.nc, geo.nz, geo.ny) + s.shape, s.dtype) for s in shards]
    A = pl.BlockSpec(memory_space=pl.ANY)
    return pl.pallas_call(
        functools.partial(gather_kernel, geo, W), out_shape=outs, in_specs=[A] * W, out_specs=[A] * W,
        scratch_shapes=gather_sems(geo, W),
        compiler_params=pltpu.CompilerParams(collective_id=collective_id, has_side_effects=True, vmem_limit_bytes=16 << 20),
    )(*shards)


class Scatter:

    def __init__(self, geo, grads, outs, bufs, sems):
        self.geo, self.grads, self.outs, self.bufs = geo, grads, outs, bufs
        self.ss, self.rs = sems
        self.z, self.y, self.x, self.c = geo.place()

    def copies(self, w, h, stage):
        g, q = self.geo, self.grads[w]
        b1, b2, b3, b4 = self.bufs[4 * w : 4 * w + 4]
        z, y, x, c = self.z, self.y, self.x, self.c
        pc, py, px = 1 - c, 1 - y, 1 - x
        if stage == 0:
            moves = [(q.at[:, pc, :, :, h], b1.at[h], g.dev(z, y, x, pc))]
        elif stage == 1 and h == 0:
            moves = [(b1.at[0, px, :, k], b2.at[0, k], g.dev(z, y, px, c)) for k in range(g.ny)]
        elif stage == 1:
            moves = [(b1.at[1, :, :, py], b2.at[1], g.dev(z, py, x, c))]
        elif stage == 2:
            moves = [(b2.at[h, py if h == 0 else px], b3.at[h], g.dev(z, py, x, c) if h == 0 else g.dev(z, y, px, c))]
        else:
            moves = []
            for k in range(1, g.nz):
                zt = lax.rem(z + k, g.nz)
                moves.append((b3.at[h, zt], b4.at[h, k - 1], g.dev(zt, y, x, c)))
        return [
            pltpu.make_async_remote_copy(src_ref=s, dst_ref=d, send_sem=self.ss.at[w, h, stage, i], recv_sem=self.rs.at[w, h, stage, i], device_id=p, device_id_type=MESH)
            for i, (s, d, p) in enumerate(moves)
        ]

    def add(self, w, h, stage):
        g, q = self.geo, self.grads[w]
        b1, b2, b3, b4 = self.bufs[4 * w : 4 * w + 4]
        z, y, x, c = self.z, self.y, self.x, self.c

        def into(ref, at, other):
            ref[at] = (ref[at].astype(F32) + other.astype(F32)).astype(ref.dtype)

        if stage == 0:
            def one(i, _):
                xx, zz, yy = i // (g.nz * g.ny), (i // g.ny) % g.nz, i % g.ny
                into(b1, (h, xx, zz, yy), q[xx, c, zz, yy, h])
                return 0
            lax.fori_loop(0, g.nx * g.nz * g.ny, one, 0)
        elif stage == 1:
            def one(i, _):
                k, zz = i // g.nz, i % g.nz
                into(b2, (h, k, zz), b1[0, x, zz, k] if h == 0 else b1[1, k, zz, y])
                return 0
            lax.fori_loop(0, 2 * g.nz, one, 0)
        elif stage == 2:
            def one(i, _):
                into(b3, (h, i), b2[h, y if h == 0 else x, i])
                return 0
            lax.fori_loop(0, g.nz, one, 0)
        else:
            if g.nz <= 8:
                total = b3[h, z].astype(F32)
                for k in range(g.nz - 1):
                    total = total + b4[h, k].astype(F32)
            else:
                total = lax.fori_loop(0, g.nz - 1, lambda k, t: t + b4[h, k].astype(F32), b3[h, z].astype(F32))
            self.outs[w][h] = total

    def step(self, w, h, stage):
        if stage > 0:
            for cp in self.copies(w, h, stage - 1):
                cp.wait_recv()
            self.add(w, h, stage - 1)
        if stage < 4:
            for cp in self.copies(w, h, stage):
                cp.start()

    def drain(self, w, h):
        for stage in range(4):
            for cp in self.copies(w, h, stage):
                cp.wait_send()


def scatter_bufs(geo, shapes):
    out = []
    for s in shapes:
        r, t, d = s.shape[-2], s.shape[-1], s.dtype
        out += [
            pltpu.VMEM((2, geo.nx, geo.nz, geo.ny, r, t), d), pltpu.VMEM((2, 2, geo.nz, r, t), d),
            pltpu.VMEM((2, geo.nz, r, t), d), pltpu.VMEM((2, geo.nz - 1, r, t), d),
        ]
    return out


def scatter_sems(geo, W):
    n = max(2, geo.nz - 1)
    return [pltpu.SemaphoreType.DMA((W, 2, 4, n)), pltpu.SemaphoreType.DMA((W, 2, 4, n))]


def scatter_kernel(geo, W, *refs):
    grads, outs, bufs, sems = refs[:W], refs[W : 2 * W], refs[2 * W : 6 * W], refs[6 * W :]
    barrier(geo)
    S = Scatter(geo, grads, outs, bufs, sems)
    for t in range(W + 4):
        for stage in range(5):
            w = t - stage
            if 0 <= w < W:
                for h in range(2):
                    S.step(w, h, stage)
    for w in range(W):
        for h in range(2):
            S.drain(w, h)


def scatter(geo, grads, collective_id):
    W = len(grads)
    V = pl.BlockSpec(memory_space=pltpu.VMEM)
    return pl.pallas_call(
        functools.partial(scatter_kernel, geo, W),
        out_shape=[jax.ShapeDtypeStruct(g.shape[4:], F32) for g in grads],
        in_specs=[V] * W, out_specs=[V] * W,
        scratch_shapes=scatter_bufs(geo, grads) + scatter_sems(geo, W),
        compiler_params=pltpu.CompilerParams(collective_id=collective_id, has_side_effects=True, vmem_limit_bytes=60 << 20),
        name="scatter",
    )(*grads)


def nn(a, b):
    return lax.dot_general(a, b, (((1,), (0,)), ((), ())), preferred_element_type=F32)


def nt(a, b):
    return lax.dot_general(a, b, (((1,), (1,)), ((), ())), preferred_element_type=F32)


def tn(a, b):
    return lax.dot_general(a, b, (((0,), (0,)), ((), ())), preferred_element_type=F32)


def vm():
    return pl.BlockSpec(memory_space=pltpu.VMEM)


def sm():
    return pl.BlockSpec(memory_space=pltpu.SMEM)


def ends_of(len_ref):
    total, starts, ends = jnp.int32(0), [], []
    for t in range(len_ref.shape[1]):
        starts.append(total)
        total = total + len_ref[0, t]
        ends.append(total)
    return starts, ends


def segment(pos, ends):
    seg = jnp.zeros_like(pos)
    for e in ends:
        seg = seg + (pos >= e).astype(jnp.int32)
    return jnp.where(pos < ends[-1], seg, len(ends) + pos)


def opens(pos, starts, ends):
    hit = jnp.zeros_like(pos)
    for s in starts:
        hit = jnp.where(pos == s, 1, hit)
    return jnp.where(pos < ends[-1], hit, 0)


def lane_half(rows, which):
    lane = lax.broadcasted_iota(jnp.int32, (rows, 128), 1)
    return (lane < 64) if which == 0 else (lane >= 64)


def only(x, which):
    return jnp.where(lane_half(x.shape[0], which), x, jnp.zeros_like(x))


def masks(len_ref, r0, R, J):
    starts, ends = ends_of(len_ref)
    row = lax.broadcasted_iota(jnp.int32, (R, 1), 0) + r0
    col = lax.broadcasted_iota(jnp.int32, (1, J), 1)
    same = segment(row, ends) == segment(col, ends)
    allow = same & (col <= row)
    pick = same & (col < row) & (opens(col, starts, ends) == 0)
    return allow, pick


def ln_stats(x):
    center = x - jnp.mean(x, axis=-1, keepdims=True)
    spread = jnp.mean(center * center, axis=-1, keepdims=True)
    r = lax.rsqrt(spread + EPS)
    return center * r, r


def ln_back(g_h, n, r, gain):
    g_n = g_h * gain
    return r * (g_n - jnp.mean(g_n, axis=-1, keepdims=True) - n * jnp.mean(g_n * n, axis=-1, keepdims=True))


def unpack_cols(blk_ref, full_ref):
    n, _, w = blk_ref.shape
    for f in range(n):
        full_ref[:, f * w : (f + 1) * w] = blk_ref[f]


def qkv_kernel(x_ref, par_ref, w_ref, h1_ref, q_ref, k_ref, v_ref, wf):
    unpack_cols(w_ref, wf)
    D = x_ref.shape[1]
    R = 256
    for b in range(x_ref.shape[0] // R):
        rows = pl.ds(b * R, R)
        n, _ = ln_stats(x_ref[rows, :].astype(F32))
        h1 = (n * par_ref[0:1, :] + par_ref[1:2, :]).astype(BF16)
        h1_ref[rows, :] = h1
        q = (nn(h1, wf[:, 0:D]) + par_ref[4:5, :]).astype(BF16)
        q_ref[rows, :] = q * jnp.asarray(0.125, BF16)
        k_ref[rows, :] = nn(h1, wf[:, D : 2 * D]).astype(BF16)
        v_ref[rows, :] = (nn(h1, wf[:, 2 * D : 3 * D]) + par_ref[5:6, :]).astype(BF16)


def qkv(x, par, w):
    s = jax.ShapeDtypeStruct(x.shape, BF16)
    return pl.pallas_call(
        qkv_kernel, out_shape=[s] * 4, in_specs=[vm()] * 3, out_specs=[vm()] * 4,
        scratch_shapes=[pltpu.VMEM((w.shape[1], w.shape[0] * w.shape[2]), BF16)],
        compiler_params=pltpu.CompilerParams(vmem_limit_bytes=VLIM),
        name="qkv",
    )(x, par, w)


def unpack_pairs(blk_ref, full_ref):
    n, w = blk_ref.shape[0], blk_ref.shape[3] // 2
    for f in range(n):
        for s in range(2):
            full_ref[:, s, :, f * w : (f + 1) * w] = blk_ref[f, :, :, s * w : (s + 1) * w]


def mlp_kernel(R, len_ref, x_ref, cot_ref, mix_ref, par_ref, upb_ref, wo_ref, wu_ref, wd_ref,
               out_ref, gmid_ref, gmix_ref, small_ref, gub_ref, dwo_ref, dwu_ref, dwd_ref,
               wo, wd, act, gin, h2s, gbs):
    T, D = x_ref.shape
    FF = upb_ref.shape[1]
    nf, wf = wu_ref.shape[0], wu_ref.shape[2]
    unpack_cols(wo_ref, wo)
    unpack_pairs(wd_ref, wd)
    _, ends = ends_of(len_ref)
    small_ref[...] = jnp.zeros_like(small_ref)
    gub_ref[...] = jnp.zeros_like(gub_ref)
    cpf = wd.shape[0] // nf
    C0, C1 = 0.7978845608028654, 0.044715

    def block(b, _):
        rows = pl.ds(pl.multiple_of(b * R, R), R)
        x = x_ref[rows, :].astype(F32)
        middle = x + nn(mix_ref[rows, :], wo[...]) + par_ref[6:7, :]
        n2, r2 = ln_stats(middle)
        h2 = (n2 * par_ref[2:3, :] + par_ref[3:4, :]).astype(BF16)
        h2s[rows, :] = h2
        pos = lax.broadcasted_iota(jnp.int32, (R, 1), 0) + b * R
        live = pos < ends[-1]
        gb = jnp.where(live, cot_ref[rows, :].astype(F32), 0.0)
        gbl = gb.astype(BF16)
        gbs[rows, :] = gbl
        branch = jnp.zeros((R, D), F32)
        g_h2 = jnp.zeros((R, D), F32)
        for f in range(nf):
            cols = pl.ds(f * wf, wf)
            wdf = wd[f * cpf : (f + 1) * cpf].reshape(wf, D)
            u = nn(h2, wu_ref[f]) + upb_ref[0:1, f * wf : (f + 1) * wf]
            g_act = nt(gbl, wdf)
            u2 = u * u
            t = jnp.tanh(u * (C0 + (C0 * C1) * u2))
            hp = 0.5 + 0.5 * t
            a = u * hp
            al = a.astype(BF16)
            act[rows, cols] = al
            branch = branch + nn(al, wdf)
            d = hp + (a - a * hp) * (2.0 * C0 + (6.0 * C0 * C1) * u2)
            gi = (g_act * d).astype(BF16)
            gin[rows, cols] = gi
            gub_ref[0:1, f * wf : (f + 1) * wf] += jnp.sum(gi.astype(F32), axis=0, keepdims=True)
            g_h2 = g_h2 + nt(gi, wu_ref[f])
        out_ref[rows, :] = jnp.where(live, middle + branch + par_ref[7:8, :], 0.0).astype(BF16)
        small_ref[2:3, :] += jnp.sum(g_h2 * n2, axis=0, keepdims=True)
        small_ref[3:4, :] += jnp.sum(g_h2, axis=0, keepdims=True)
        g_mid = gb + ln_back(g_h2, n2, r2, par_ref[2:3, :])
        gmid_ref[rows, :] = g_mid
        gml = g_mid.astype(BF16)
        small_ref[6:7, :] += jnp.sum(gml.astype(F32), axis=0, keepdims=True)
        small_ref[7:8, :] += jnp.sum(gb, axis=0, keepdims=True)
        gmix_ref[rows, :] = nt(gml, wo[...]).astype(BF16)
        return 0

    lax.fori_loop(0, T // R, block, 0)
    w4 = D // nf

    def put(ref, grad, lead):
        r = ref.shape[2]
        c = grad.shape[0] // (2 * r)
        g = grad.astype(BF16).reshape(c, 2, r, D)
        for f in range(nf):
            for s in range(2):
                ref[f, pl.ds(lead, c), :, s * w4 : (s + 1) * w4] = g[:, s, :, f * w4 : (f + 1) * w4]

    def outp(i, _):
        g = tn(mix_ref[:, pl.ds(pl.multiple_of(i * 384, 128), 384)], gmid_ref[...].astype(BF16)).astype(BF16)
        for f in range(nf):
            dwo_ref[f, pl.ds(pl.multiple_of(i * 384, 128), 384), :] = g[:, f * w4 : (f + 1) * w4]
        return 0

    lax.fori_loop(0, D // 384, outp, 0)
    K = 384
    cpk = K // (2 * dwd_ref.shape[2])

    def down(i, _):
        put(dwd_ref, tn(act[:, pl.ds(pl.multiple_of(i * K, 128), K)], gbs[...]), i * cpk)
        return 0

    lax.fori_loop(0, FF // K, down, 0)
    H = 384

    def up(i, _):
        f, s = i // (wf // H), i % (wf // H)
        dwu_ref[f, :, pl.ds(pl.multiple_of(s * H, 128), H)] = tn(h2s[...], gin[:, pl.ds(pl.multiple_of(i * H, 128), H)]).astype(BF16)
        return 0

    lax.fori_loop(0, FF // H, up, 0)


def mlp(lengths, x, cot, mixed, par, upb, wo, wu, wd, R=256):
    T, D = x.shape
    FF = upb.shape[1]
    S = jax.ShapeDtypeStruct
    V = pltpu.VMEM
    return pl.pallas_call(
        functools.partial(mlp_kernel, R),
        out_shape=[S((T, D), BF16), S((T, D), F32), S((T, D), BF16), S((8, D), F32), S((8, FF), F32),
                   S(wo.shape, BF16), S(wu.shape, BF16), S(wd.shape, BF16)],
        in_specs=[sm()] + [vm()] * 8, out_specs=[vm()] * 8,
        scratch_shapes=[V((D, D), BF16), V((wd.shape[1], 2, wd.shape[2], D), BF16),
                        V((T, FF), BF16), V((T, FF), BF16), V((T, D), BF16), V((T, D), BF16)],
        compiler_params=pltpu.CompilerParams(vmem_limit_bytes=VLIM),
        name="mlp",
    )(lengths, x, cot, mixed, par, upb, wo, wu, wd)


def qkv_back_kernel(x_ref, h1_ref, gp_ref, gmid_ref, par_ref, w_ref, ig_ref, small_ref, dw_ref):
    T, D = x_ref.shape
    n, _, w = w_ref.shape
    R = 256
    for f in range(n):
        dw_ref[f] = tn(h1_ref[...], gp_ref[:, f * w : (f + 1) * w]).astype(BF16)
    small_ref[...] = jnp.zeros_like(small_ref)
    for b in range(T // R):
        rows = pl.ds(b * R, R)
        g_h1 = jnp.zeros((R, D), F32)
        for f in range(n):
            g_h1 = g_h1 + nt(gp_ref[rows, f * w : (f + 1) * w], w_ref[f])
        n1, r1 = ln_stats(x_ref[rows, :].astype(F32))
        small_ref[0:1, :] += jnp.sum(g_h1 * n1, axis=0, keepdims=True)
        small_ref[1:2, :] += jnp.sum(g_h1, axis=0, keepdims=True)
        small_ref[4:5, :] += jnp.sum(gp_ref[rows, 0:D].astype(F32), axis=0, keepdims=True)
        small_ref[5:6, :] += jnp.sum(gp_ref[rows, 2 * D : 3 * D].astype(F32), axis=0, keepdims=True)
        ig_ref[rows, :] = (gmid_ref[rows, :] + ln_back(g_h1, n1, r1, par_ref[0:1, :])).astype(BF16)


def qkv_back(x, h1, gp, gmid, par, w):
    S = jax.ShapeDtypeStruct
    return pl.pallas_call(
        qkv_back_kernel, out_shape=[S(x.shape, BF16), S((8, x.shape[1]), F32), S(w.shape, BF16)],
        in_specs=[vm()] * 6, out_specs=[vm()] * 3,
        compiler_params=pltpu.CompilerParams(vmem_limit_bytes=VLIM),
        name="qkv_back",
    )(x, h1, gp, gmid, par, w)


def masks_t(len_ref, r0, R, J):
    starts, ends = ends_of(len_ref)
    key = lax.broadcasted_iota(jnp.int32, (J, 1), 0)
    row = lax.broadcasted_iota(jnp.int32, (1, R), 1) + r0
    same = segment(key, ends) == segment(row, ends)
    return same & (key < row) & (opens(key, starts, ends) == 0)


def carried_scores(len_ref, q_ref, k_ref, cm, cmT_ref, carry):
    T = q_ref.shape[0]
    carry[...] = jnp.zeros_like(carry)
    i = lax.broadcasted_iota(jnp.int32, (B, B), 0)
    j = lax.broadcasted_iota(jnp.int32, (B, B), 1)
    lower = jnp.where(j < i, 1.0, 0.0).astype(BF16)
    for b in range(T // B):
        r0, J = b * B, (b + 1) * B
        rows = pl.ds(r0, B)
        allow, pick = masks(len_ref, r0, B, J)
        s0 = jnp.maximum(nt(only(q_ref[rows, 0:128], 0), k_ref[0:J, 0:128]), 0.0)
        chosen = jnp.where(pick, s0 * s0, 0.0)
        hi = chosen.astype(BF16)
        lo = (chosen - hi.astype(F32)).astype(BF16)
        carried = carry[0:1, 0:J] + (nn(lower, hi) + nn(lower, lo))
        c = jnp.where(allow, carried, BIG)
        cm[rows, 0:J] = c
        cmT_ref[0:J, rows] = jnp.transpose(c)
        carry[0:1, 0:J] = carry[0:1, 0:J] + jnp.sum(chosen, axis=0, keepdims=True)


def fwd_pair(p, q_ref, k_ref, v_ref, o_ref, lse, cm, s_sc, p_sc, C):
    T = q_ref.shape[0]
    lane = lax.broadcasted_iota(jnp.int32, (C, 128), 1)
    cols = pl.ds(pl.multiple_of(p * 128, 128), 128)
    k2, v2 = k_ref[:, cols], v_ref[:, cols]
    for half in range(2):
        q2 = only(q_ref[:, cols], half)
        for kb in range(T // B):
            s_sc[half, kb * B :, kb * B : (kb + 1) * B] = nt(q2[kb * B :], k2[kb * B : (kb + 1) * B])
    for rb in range(T // C):
        J = ((rb * C) // B + 1) * B
        rows = slice(rb * C, (rb + 1) * C)
        inv = []
        for half in range(2):
            l = s_sc[half, rows, :J] - cm[rows, :J]
            m = jnp.max(l, axis=1, keepdims=True)
            e = jnp.exp(l - m)
            t = jnp.sum(e, axis=1, keepdims=True)
            p_sc[half, rows, :J] = (e * (1.0 / t)).astype(BF16)
            lse[rows, :] = jnp.where(lane == 2 * p + half, m + jnp.log(t), lse[rows, :])
        if (rb * C) % B == B - C:
            b0 = (rb * C) // B * B
            o = [nn(p_sc[half, b0 : b0 + B, :J], v2[:J]) for half in range(2)]
            lanes = lax.broadcasted_iota(jnp.int32, (B, 128), 1)
            o_ref[b0 : b0 + B, cols] = jnp.where(lanes < 64, o[0], o[1]).astype(BF16)


def attn_fwd_kernel(C, len_ref, q_ref, k_ref, v_ref, o_ref, lseT_ref, cmT_ref, cm, lse, s_sc, p_sc, carry):
    carried_scores(len_ref, q_ref, k_ref, cm, cmT_ref, carry)

    def pair(p, _):
        fwd_pair(p, q_ref, k_ref, v_ref, o_ref, lse, cm, s_sc, p_sc, C)
        return 0

    lax.fori_loop(0, HEADS // 2, pair, 0)
    lseT_ref[...] = jnp.transpose(lse[...])[0:16]


def attn_fwd(lengths, q, k, v, C=64):
    T = q.shape[0]
    V = pltpu.VMEM
    return pl.pallas_call(
        functools.partial(attn_fwd_kernel, C),
        out_shape=[jax.ShapeDtypeStruct(q.shape, BF16), jax.ShapeDtypeStruct((16, T), F32), jax.ShapeDtypeStruct((T, T), F32)],
        in_specs=[sm()] + [vm()] * 3, out_specs=[vm()] * 3,
        scratch_shapes=[V((T, T), F32), V((T, 128), F32), V((2, T, T), F32), V((2, T, T), BF16), V((8, T), F32)],
        compiler_params=pltpu.CompilerParams(vmem_limit_bytes=VLIM),
        name="attn_fwd",
    )(lengths, q, k, v)


def row_sums(do_ref, o_ref, DT):
    T, D = do_ref.shape
    f = lax.broadcasted_iota(jnp.int32, (D, 128), 0)
    h = lax.broadcasted_iota(jnp.int32, (D, 128), 1)
    E = jnp.where((f >= h * 64) & (f < h * 64 + 64), 1.0, 0.0).astype(BF16)
    for b in range(T // B):
        rows = pl.ds(b * B, B)
        x = do_ref[rows, :].astype(F32) * o_ref[rows, :].astype(F32)
        hi = x.astype(BF16)
        lo = (x - hi.astype(F32)).astype(BF16)
        DT[:, rows] = jnp.transpose(nn(hi, E) + nn(lo, E))[0:16]


def bwd_scores(p, half, q_ref, k_ref, v_ref, do_ref, sT, dpT):
    T = q_ref.shape[0]
    cols = p * 128 if isinstance(p, int) else pl.multiple_of(p * 128, 128)
    c = pl.ds(cols, 128)
    k2, v2 = k_ref[:, c], v_ref[:, c]
    q2, do2 = only(q_ref[:, c], half), only(do_ref[:, c], half)
    for rb in range(T // B):
        J, r = (rb + 1) * B, slice(rb * B, (rb + 1) * B)
        sT[0:J, r] = nt(k2[0:J], q2[r])
        dpT[0:J, r] = nt(v2[0:J], do2[r])


def bwd_softmax(h, sT, dpT, pT, dsT, lseT, DT, cmT, C, add_into=None, keep=None):
    T = sT.shape[0]
    for kc in range(T // C):
        i0 = (kc * C) // B * B
        keys = slice(kc * C, (kc + 1) * C)
        pr = jnp.exp(sT[keys, i0:] - cmT[keys, i0:] - lseT[pl.ds(h, 1), i0:])
        ds = pr * (dpT[keys, i0:] - DT[pl.ds(h, 1), i0:])
        pT[keys, i0:] = pr.astype(BF16)
        if keep is not None:
            keep[keys, i0:] = ds
        else:
            dsT[keys, i0:] = ds.astype(BF16)
        add_into[keys, i0:] += ds


def bwd_products(p, half, q_ref, k_ref, do_ref, pT, dsT, gp_ref, dk, dv, first):
    T, D = q_ref.shape
    cols = p * 128 if isinstance(p, int) else pl.multiple_of(p * 128, 128)
    c = pl.ds(cols, 128)
    k2 = k_ref[:, c]
    q2, do2 = only(q_ref[:, c], half), only(do_ref[:, c], half)
    for kb in range(T // B):
        keys = slice(kb * B, (kb + 1) * B)
        a = nn(pT[keys, kb * B :], do2[kb * B :])
        d = nn(dsT[keys, kb * B :], q2[kb * B :])
        if first:
            dv[keys, :], dk[keys, :] = a, d
        else:
            dv[keys, :] += a
            dk[keys, :] += d
    lanes = lax.broadcasted_iota(jnp.int32, (B, 128), 1)
    for rb in range(T // B):
        J, r = (rb + 1) * B, slice(rb * B, (rb + 1) * B)
        dq = (tn(dsT[0:J, r], k2[0:J]) * 0.125).astype(BF16)
        if first:
            gp_ref[r, c] = dq
        else:
            gp_ref[r, c] = jnp.where((lanes < 64) == (half == 0), dq, gp_ref[r, c])


def attn_bwd_kernel(C, len_ref, q_ref, k_ref, v_ref, do_ref, o_ref, lseT, cmT, gp_ref, DT, sT, dpT, pT, dsT, G, dk, dv):
    T, D = q_ref.shape
    row_sums(do_ref, o_ref, DT)
    G[...] = jnp.zeros_like(G)

    def put(p):
        ck = D + p * 128 if isinstance(p, int) else pl.multiple_of(D + p * 128, 128)
        cv = 2 * D + p * 128 if isinstance(p, int) else pl.multiple_of(2 * D + p * 128, 128)
        gp_ref[:, pl.ds(ck, 128)] = dk[...].astype(BF16)
        gp_ref[:, pl.ds(cv, 128)] = dv[...].astype(BF16)

    def pair(k, _):
        p = HEADS // 2 - 1 - k
        for half in range(2):
            bwd_scores(p, half, q_ref, k_ref, v_ref, do_ref, sT.at[half], dpT.at[half])
        for half in range(2):
            bwd_softmax(2 * p + half, sT.at[half], dpT.at[half], pT.at[half], dsT.at[half], lseT, DT, cmT, C, G)
        for half in range(2):
            bwd_products(p, half, q_ref, k_ref, do_ref, pT.at[half], dsT.at[half], gp_ref, dk, dv, half == 0)
        put(p)
        return 0

    lax.fori_loop(0, HEADS // 2 - 1, pair, 0)
    bwd_scores(0, 1, q_ref, k_ref, v_ref, do_ref, sT.at[1], dpT.at[1])
    bwd_softmax(1, sT.at[1], dpT.at[1], pT.at[1], dsT.at[1], lseT, DT, cmT, C, G)
    bwd_products(0, 1, q_ref, k_ref, do_ref, pT.at[1], dsT.at[1], gp_ref, dk, dv, True)
    bwd_scores(0, 0, q_ref, k_ref, v_ref, do_ref, sT.at[0], dpT.at[0])
    ds0 = dpT.at[1]
    bwd_softmax(0, sT.at[0], dpT.at[0], pT.at[0], dsT.at[0], lseT, DT, cmT, C, G, keep=ds0)
    i = lax.broadcasted_iota(jnp.int32, (B, B), 0)
    j = lax.broadcasted_iota(jnp.int32, (B, B), 1)
    after = jnp.where(i > j, 1.0, 0.0).astype(BF16)
    later = jnp.zeros((T, 1), F32)
    for rb in reversed(range(T // B)):
        J, r = (rb + 1) * B, slice(rb * B, (rb + 1) * B)
        g = -G[0:J, r]
        hi = g.astype(BF16)
        lo = (g - hi.astype(F32)).astype(BF16)
        g_chosen = later[0:J] + (nn(hi, after) + nn(lo, after))
        later = later[0:J] + jnp.sum(g, axis=1, keepdims=True)
        pick = masks_t(len_ref, rb * B, B, J)
        full = ds0[0:J, r] + jnp.where(pick, 2.0 * jnp.maximum(sT[0, 0:J, r], 0.0) * g_chosen, 0.0)
        dsT[0, 0:J, r] = full.astype(BF16)
    bwd_products(0, 0, q_ref, k_ref, do_ref, pT.at[0], dsT.at[0], gp_ref, dk, dv, False)
    put(0)


def attn_bwd(lengths, q, k, v, do, o, lseT, cmT, C=64):
    T, D = q.shape
    V = pltpu.VMEM
    return pl.pallas_call(
        functools.partial(attn_bwd_kernel, C),
        out_shape=jax.ShapeDtypeStruct((T, 3 * D), BF16),
        in_specs=[sm()] + [vm()] * 7, out_specs=vm(),
        scratch_shapes=[V((16, T), F32), V((2, T, T), F32), V((2, T, T), F32), V((2, T, T), BF16), V((2, T, T), BF16), V((T, T), F32), V((T, 128), F32), V((T, 128), F32)],
        compiler_params=pltpu.CompilerParams(vmem_limit_bytes=VLIM),
        name="attn_bwd",
    )(lengths, q, k, v, do, o, lseT, cmT)


def fold_tiny(tiny, par, per, n_dp, F):
    for f in range(F):
        for d in range(n_dp):
            for s in range(2):
                par[s * F + f : s * F + f + 1, d * per : (d + 1) * per] = tiny[f, d, 0, s : s + 1, 0:per].astype(F32)


def front_kernel(geo, C, *refs):
    len_ref, x_ref = refs[0:2]
    shards, bufs = refs[2:7], refs[7:12]
    h1_o, q_o, k_o, v_o, mix_o, lseT_o, cmT_o = refs[12:19]
    tiny_v, wq_v, wf, par, h1, q, k, v, mix, cmT, cm, lse, s_sc, p_sc, carry, lsem, osem = refs[19:36]
    sems = refs[36:]
    T, D = x_ref.shape
    F, per = geo.n_fs, D // geo.n_dp
    barrier(geo)
    G = Gather(geo, shards, bufs, sems)

    def ev(*items):
        for w, stage in items:
            for h in range(2):
                if stage == 4:
                    G.finish(w, h)
                else:
                    G.start(w, h, stage)

    ev((0, 0), (1, 0), (2, 0))
    for b in range(T // B):
        rows = pl.ds(b * B, B)
        n, _ = ln_stats(x_ref[rows, :].astype(F32))
        s_sc[0, rows, 0:D] = n
    ev((0, 1), (1, 1), (3, 0), (0, 2), (1, 2), (2, 1), (0, 3), (1, 3), (2, 2), (4, 0), (3, 1), (0, 4), (1, 4))
    get_t = pltpu.make_async_copy(bufs[0], tiny_v, lsem.at[0])
    get_q = pltpu.make_async_copy(bufs[1], wq_v, lsem.at[1])
    get_t.start()
    get_q.start()
    get_t.wait()
    fold_tiny(tiny_v.reshape(F, geo.n_dp, 2, 16, 128), par, per, geo.n_dp, F)
    get_q.wait()
    unpack_cols(wq_v.reshape(F, D, wq_v.shape[-1]), wf)
    outs = [pltpu.make_async_copy(a, b, osem.at[i]) for i, (a, b) in enumerate(((h1, h1_o), (q, q_o), (k, k_o), (v, v_o), (cmT, cmT_o), (mix, mix_o), (lse, lse))[:6])]
    for b in range(T // B):
        rows = pl.ds(b * B, B)
        hb = (s_sc[0, rows, 0:D] * par[0:1, :] + par[1:2, :]).astype(BF16)
        h1[rows, :] = hb
        q[rows, :] = (nn(hb, wf[:, 0:D]) + par[4:5, :]).astype(BF16) * jnp.asarray(0.125, BF16)
        k[rows, :] = nn(hb, wf[:, D : 2 * D]).astype(BF16)
        v[rows, :] = (nn(hb, wf[:, 2 * D : 3 * D]) + par[5:6, :]).astype(BF16)
        if b == 1:
            ev((2, 3), (3, 2))
    for i in range(4):
        outs[i].start()
    ev((4, 1))
    carried_scores(len_ref, q, k, cm, cmT, carry)
    outs[4].start()
    plan = {1: ((3, 3), (4, 2)), 4: ((4, 3),)}

    def pair(p, _):
        for at, items in plan.items():
            @pl.when(p == at)
            def _():
                ev(*items)
        fwd_pair(p, q, k, v, mix, lse, cm, s_sc, p_sc, C)
        return 0

    lax.fori_loop(0, HEADS // 2, pair, 0)
    outs[5].start()
    lseT_o[...] = jnp.transpose(lse[...])[0:16]
    ev((2, 4), (3, 4), (4, 4))
    for w in range(5):
        for h in range(2):
            G.drain(w, h)
    for i in range(6):
        outs[i].wait()


def front(geo, lengths, x, shards, collective_id=0, C=64):
    T, D = x.shape
    V, S, A = pltpu.VMEM, jax.ShapeDtypeStruct, pl.BlockSpec(memory_space=pl.ANY)
    lead = (geo.nx, geo.nc, geo.nz, geo.ny)
    tok = S((T, D), BF16)
    res = pl.pallas_call(
        functools.partial(front_kernel, geo, C),
        out_shape=[S(lead + s.shape, s.dtype) for s in shards] + [tok] * 5 + [S((16, T), F32), S((T, T), F32)],
        in_specs=[sm(), vm()] + [A] * 5,
        out_specs=[A] * 10 + [vm(), A],
        scratch_shapes=[V(lead + shards[0].shape, BF16), V(lead + shards[1].shape, BF16), V((D, 3 * D), BF16), V((8, D), F32)]
        + [V((T, D), BF16)] * 5 + [V((T, T), F32), V((T, T), F32), V((T, 128), F32), V((2, T, T), F32), V((2, T, T), BF16), V((8, T), F32)]
        + [pltpu.SemaphoreType.DMA((2,)), pltpu.SemaphoreType.DMA((6,))] + gather_sems(geo, 5),
        compiler_params=pltpu.CompilerParams(collective_id=collective_id, has_side_effects=True, vmem_limit_bytes=VLIM),
        name="front",
    )(lengths, x, *shards)
    return res[:5], res[5:]


def pair_up(shard):
    w = shard.shape[1]
    return shard.reshape(2, 2, -1, w).transpose(0, 2, 1, 3).reshape(2, -1, 2 * w)


def pair_down(halves):
    w = halves.shape[2] // 2
    return halves.reshape(2, -1, 2, w).transpose(0, 2, 1, 3).reshape(-1, w)


def repair(blocks, r):
    n, c, r0, w2 = blocks.shape
    if r0 == r:
        return blocks
    w = w2 // 2
    flat = blocks.reshape(n, c, r0, 2, w).transpose(0, 1, 3, 2, 4).reshape(n, -1, 2, r, w)
    return flat.transpose(0, 1, 3, 2, 4).reshape(n, -1, r, w2)


def body(geo, tokens, cotangent, lengths, norm_params, bias_params, w_qkv, w_out, w_up, up_bias, w_down):
    T, D = tokens.shape
    F, n_dp, per = geo.n_fs, geo.n_dp, D // geo.n_dp
    FF = D * F * up_bias.shape[1]
    fused = (per // 2) % 16 == 0
    tiny = jnp.stack([jnp.stack([norm_params[:, 0], bias_params[:, 0]]), jnp.stack([up_bias[:, 0]] * 2)])
    tiny = jnp.pad(tiny, ((0, 0), (0, 14), (0, 128 - per)))

    def halves(shard):
        return shard.reshape(2, -1, shard.shape[1])

    shards = [tiny, halves(w_qkv), halves(w_out), halves(w_up), pair_up(w_down)]
    if fused:
        bufs, (h1, q, k, v, mixed, lse, cm) = front(geo, lengths, tokens, shards)
    else:
        bufs = gather(geo, shards)
    t = bufs[0].reshape(F, n_dp, 2, 16, 128)[..., :per].astype(F32)
    par = jnp.concatenate([t[:, :, 0, 0].reshape(F, D), t[:, :, 0, 1].reshape(F, D)], axis=0)
    upb = jnp.broadcast_to(t[:, :, 1, 0].reshape(F, D).T.reshape(1, FF), (8, FF))
    wq, wo, wu = (b.reshape(F, D, b.shape[-1]) for b in bufs[1:4])
    wd = repair(bufs[4].reshape((F, n_dp * 2) + bufs[4].shape[-2:]), FF // 32)
    if not fused:
        h1, q, k, v = qkv(tokens, par, wq)
        mixed, lse, cm = attn_fwd(lengths, q, k, v)

    out, gmid, gmix, small_b, gub, dwo, dwu, dwd = mlp(lengths, tokens, cotangent, mixed, par, upb, wo, wu, wd)
    r = per // 2

    def split(grad, rows):
        return grad.reshape((geo.nx, geo.nc, geo.nz, geo.ny, 2, rows, grad.shape[-1]))

    ub = gub[0].reshape(D, F).T.reshape(F, n_dp, per)

    def pack(small):
        rows = jnp.stack([small[0:4], small[4:8]]).reshape(2, F, n_dp, per)
        g = jnp.stack([jnp.stack([rows[0], rows[1]], axis=2), jnp.stack([ub, ub], axis=2)], axis=2)
        return split(jnp.pad(g, ((0, 0), (0, 0), (0, 0), (0, 6), (0, 128 - per))), 8)

    dwd = repair(dwd, FF // n_dp // 4)
    parts = [split(dwo, r), split(dwu, r), split(dwd, FF // n_dp // 4)]
    gp = attn_bwd(lengths, q, k, v, gmix, mixed, lse, cm)
    ig, small_a, dwq = qkv_back(tokens, h1, gp, gmid, par, wq)
    s_tiny, s_out, s_up, s_down, s_qkv = scatter(geo, [pack(small_a + small_b)] + parts + [split(dwq, r)], 1)
    return (
        out,
        ig,
        s_tiny[0, 0, :per, None],
        s_tiny[0, 1, :per, None],
        s_qkv.reshape(-1, s_qkv.shape[-1]),
        s_out.reshape(-1, s_out.shape[-1]),
        s_up.reshape(-1, s_up.shape[-1]),
        s_tiny[1, 0, :per, None],
        pair_down(s_down),
    )


def solution(mesh):
    geo = Geo(mesh.shape["dp"], mesh.shape["fsdp"])
    both, split = P(("dp", "fsdp"), None), P("dp", "fsdp")
    return jax.shard_map(
        functools.partial(body, geo), mesh=mesh, in_specs=(both,) * 3 + (split,) * 7, out_specs=(both,) * 2 + (split,) * 7, check_vma=False
    )
```

```python
import functools

import jax
import jax.numpy as jnp
from jax import lax
from jax.experimental import pallas as pl
from jax.experimental.pallas import tpu as pltpu
from jax.sharding import PartitionSpec as P

HEADS = 12
EPS = 1e-05
BIG = 1e30
B = 256
F32, BF16 = jnp.float32, jnp.bfloat16
VLIM = 60 << 20
MESH = pl.DeviceIdType.MESH


class Geo:
    def __init__(self, n_dp, n_fs):
        self.n_dp, self.n_fs = n_dp, n_fs
        self.ny = 2 if n_dp % 2 == 0 else 1
        self.nz = n_dp // self.ny
        self.nc = 2 if n_fs % 2 == 0 else 1
        self.nx = n_fs // self.nc

    def place(self):
        dp, fs = lax.axis_index("dp"), lax.axis_index("fsdp")
        return dp // self.ny, dp % self.ny, fs // self.nc, fs % self.nc

    def dev(self, z, y, x, c):
        return {"dp": z * self.ny + y, "fsdp": x * self.nc + c}


def others(n, me):
    return [lax.rem(me + k, n) for k in range(1, n)]

def barrier(geo):
    z, y, x, c = geo.place()
    sem = pltpu.get_barrier_semaphore()
    count = 0
    for k in range(1, geo.nz):
        pl.semaphore_signal(sem, inc=1, device_id=geo.dev(lax.rem(z + k, geo.nz), y, x, c), device_id_type=MESH); count += 1
    for k in range(1, geo.ny):
        pl.semaphore_signal(sem, inc=1, device_id=geo.dev(z, lax.rem(y + k, geo.ny), x, c), device_id_type=MESH); count += 1
    for k in range(1, geo.nx):
        pl.semaphore_signal(sem, inc=1, device_id=geo.dev(z, y, lax.rem(x + k, geo.nx), c), device_id_type=MESH); count += 1
    for k in range(1, geo.nc):
        pl.semaphore_signal(sem, inc=1, device_id=geo.dev(z, y, x, lax.rem(c + k, geo.nc)), device_id_type=MESH); count += 1
    pl.semaphore_wait(sem, count)

class Gather:
    def __init__(self, geo, shards, outs, sems):
        self.geo, self.shards, self.outs = geo, shards, outs
        self.lsem, self.s0, self.r0, self.s1, self.r1 = sems
        self.z, self.y, self.x, self.c = geo.place()

    def local(self, w, h):
        o = self.outs[w]
        return pltpu.make_async_copy(self.shards[w].at[h], o.at[self.x, self.c, self.z, self.y, h], self.lsem.at[w, h])

    def zcopy(self, w, h, k):
        g = self.geo
        zt = lax.rem(self.z + k, g.nz)
        return pltpu.make_async_remote_copy(
            src_ref=self.shards[w].at[h], dst_ref=self.outs[w].at[self.x, self.c, self.z, self.y, h],
            send_sem=self.s0.at[w, h, k], recv_sem=self.r0.at[w, h, k],
            device_id=g.dev(zt, self.y, self.x, self.c), device_id_type=MESH)

    def zrecv(self, w, h, k):
        g = self.geo
        zf = lax.rem(self.z + g.nz - k, g.nz)
        return pltpu.make_async_remote_copy(
            src_ref=self.shards[w].at[h], dst_ref=self.outs[w].at[self.x, self.c, zf, self.y, h],
            send_sem=self.s0.at[w, h, k], recv_sem=self.r0.at[w, h, k],
            device_id=g.dev(zf, self.y, self.x, self.c), device_id_type=MESH)

    def pair(self, w, h, stage, k, recv):
        g, o = self.geo, self.outs[w]
        z, y, x, c = self.z, self.y, self.x, self.c
        sgn = -1 if recv else 1
        kind = "c" if stage == 3 else ("y" if (stage == 1) == (h == 0) else "x")
        py = lax.rem(y + sgn * k + g.ny, g.ny); px = lax.rem(x + sgn * k + g.nx, g.nx); pc = lax.rem(c + sgn * k + g.nc, g.nc)
        def view(sx, sc, sy):
            if stage == 1: return o.at[sx, sc, :, sy, h]
            if stage == 2: return o.at[sx, sc, :, :, h] if kind == "x" else o.at[:, sc, :, sy, h]
            return o.at[:, sc, :, :, h]
        if kind == "y": peer = g.dev(z, py, x, c); pv = view(x, c, py)
        elif kind == "x": peer = g.dev(z, y, px, c); pv = view(px, c, y)
        else: peer = g.dev(z, y, x, pc); pv = view(x, pc, y)
        mine = view(x, c, y)
        ref = pv if recv else mine
        i = (w, h, stage - 1, k)
        return pltpu.make_async_remote_copy(src_ref=ref, dst_ref=ref, send_sem=self.s1.at[i], recv_sem=self.r1.at[i], device_id=peer, device_id_type=MESH)

    def npeers(self, h, stage):
        g = self.geo
        if stage == 3: return g.nc - 1
        return g.ny - 1 if (stage == 1) == (h == 0) else g.nx - 1

    def start(self, w, h, stage):
        g = self.geo
        if stage == 0:
            self.local(w, h).start()
            for k in range(1, g.nz): self.zcopy(w, h, k).start()
            return
        if stage == 1:
            self.local(w, h).wait()
            for k in range(1, g.nz): self.zrecv(w, h, k).wait_recv()
        else:
            for k in range(1, 1 + self.npeers(h, stage - 1)): self.pair(w, h, stage - 1, k, True).wait_recv()
        for k in range(1, 1 + self.npeers(h, stage)): self.pair(w, h, stage, k, False).start()

    def finish(self, w, h):
        for k in range(1, 1 + self.npeers(h, 3)): self.pair(w, h, 3, k, True).wait_recv()

    def drain(self, w, h):
        g = self.geo
        for k in range(1, g.nz): self.zcopy(w, h, k).wait_send()
        for stage in (1, 2, 3):
            for k in range(1, 1 + self.npeers(h, stage)): self.pair(w, h, stage, k, False).wait_send()

def gather_sems(geo, W):
    m = max(geo.nx, geo.ny, geo.nc)
    D = pltpu.SemaphoreType.DMA
    return [D((W, 2)), D((W, 2, geo.nz)), D((W, 2, geo.nz)), D((W, 2, 3, m)), D((W, 2, 3, m))]

def gather_kernel(geo, W, *refs):
    shards, outs, sems = refs[:W], refs[W:2 * W], refs[2 * W:]
    barrier(geo)
    G = Gather(geo, shards, outs, sems)
    for t in range(W + 4):
        for stage in range(4):
            w = t - stage
            if 0 <= w < W:
                for h in range(2): G.start(w, h, stage)
        if t >= 4:
            for h in range(2): G.finish(t - 4, h)
    for w in range(W):
        for h in range(2): G.drain(w, h)

def gather(geo, shards, collective_id=0):
    W = len(shards)
    outs = [jax.ShapeDtypeStruct((geo.nx, geo.nc, geo.nz, geo.ny) + s.shape, s.dtype) for s in shards]
    A = pl.BlockSpec(memory_space=pl.ANY)
    return pl.pallas_call(
        functools.partial(gather_kernel, geo, W), out_shape=outs, in_specs=[A] * W, out_specs=[A] * W,
        scratch_shapes=gather_sems(geo, W),
        compiler_params=pltpu.CompilerParams(collective_id=collective_id, has_side_effects=True, vmem_limit_bytes=16 << 20),
    )(*shards)


class Scatter:

    def __init__(self, geo, grads, outs, bufs, sems, owns=None, own_sem=None):
        self.geo, self.grads, self.outs, self.bufs = geo, list(grads), outs, bufs
        self.ss, self.rs = sems
        self.owns, self.own_sem = owns or [None] * len(grads), own_sem
        self.z, self.y, self.x, self.c = geo.place()

    def copies(self, w, h, stage):
        g, q = self.geo, self.grads[w]
        b1, b2, b3, b4 = self.bufs[4 * w : 4 * w + 4]
        z, y, x, c = self.z, self.y, self.x, self.c
        pc, py, px = 1 - c, 1 - y, 1 - x
        if stage == 0:
            moves = [(q.at[:, pc, :, :, h], b1.at[h], g.dev(z, y, x, pc))]
        elif stage == 1 and h == 0:
            moves = [(b1.at[0, px, :, k], b2.at[0, k], g.dev(z, y, px, c)) for k in range(g.ny)]
        elif stage == 1:
            moves = [(b1.at[1, :, :, py], b2.at[1], g.dev(z, py, x, c))]
        elif stage == 2:
            moves = [(b2.at[h, py if h == 0 else px], b3.at[h], g.dev(z, py, x, c) if h == 0 else g.dev(z, y, px, c))]
        else:
            moves = []
            for k in range(1, g.nz):
                zt = lax.rem(z + k, g.nz)
                moves.append((b3.at[h, zt], b4.at[h, k - 1], g.dev(zt, y, x, c)))
        return [
            pltpu.make_async_remote_copy(src_ref=s, dst_ref=d, send_sem=self.ss.at[w, h, stage, i], recv_sem=self.rs.at[w, h, stage, i], device_id=p, device_id_type=MESH)
            for i, (s, d, p) in enumerate(moves)
        ]

    def own_copy(self, w, h):
        return pltpu.make_async_copy(self.grads[w].at[:, self.c, :, :, h], self.owns[w].at[h], self.own_sem.at[w, h])

    def add(self, w, h, stage):
        g, q = self.geo, self.grads[w]
        b1, b2, b3, b4 = self.bufs[4 * w : 4 * w + 4]
        z, y, x, c = self.z, self.y, self.x, self.c

        def into(ref, at, other):
            ref[at] = (ref[at].astype(F32) + other.astype(F32)).astype(ref.dtype)

        if stage == 0:
            def one(i, _):
                xx, zz, yy = i // (g.nz * g.ny), (i // g.ny) % g.nz, i % g.ny
                mine = q[xx, c, zz, yy, h] if self.owns[w] is None else self.owns[w][h, xx, zz, yy]
                into(b1, (h, xx, zz, yy), mine)
                return 0
            lax.fori_loop(0, g.nx * g.nz * g.ny, one, 0)
        elif stage == 1:
            def one(i, _):
                k, zz = i // g.nz, i % g.nz
                into(b2, (h, k, zz), b1[0, x, zz, k] if h == 0 else b1[1, k, zz, y])
                return 0
            lax.fori_loop(0, 2 * g.nz, one, 0)
        elif stage == 2:
            def one(i, _):
                into(b3, (h, i), b2[h, y if h == 0 else x, i])
                return 0
            lax.fori_loop(0, g.nz, one, 0)
        else:
            if g.nz <= 8:
                total = b3[h, z].astype(F32)
                for k in range(g.nz - 1):
                    total = total + b4[h, k].astype(F32)
            else:
                total = lax.fori_loop(0, g.nz - 1, lambda k, t: t + b4[h, k].astype(F32), b3[h, z].astype(F32))
            self.outs[w][h] = total

    def step(self, w, h, stage):
        if self.owns[w] is not None:
            if stage == 0:
                self.own_copy(w, h).start()
            elif stage == 1:
                self.own_copy(w, h).wait()
        if stage > 0:
            for cp in self.copies(w, h, stage - 1):
                cp.wait_recv()
            self.add(w, h, stage - 1)
        if stage < 4:
            for cp in self.copies(w, h, stage):
                cp.start()

    def drain(self, w, h):
        for stage in range(4):
            for cp in self.copies(w, h, stage):
                cp.wait_send()


def scatter_bufs(geo, shapes):
    out = []
    for s in shapes:
        r, t, d = s.shape[-2], s.shape[-1], s.dtype
        out += [
            pltpu.VMEM((2, geo.nx, geo.nz, geo.ny, r, t), d), pltpu.VMEM((2, 2, geo.nz, r, t), d),
            pltpu.VMEM((2, geo.nz, r, t), d), pltpu.VMEM((2, geo.nz - 1, r, t), d),
        ]
    return out


def scatter_sems(geo, W):
    n = max(2, geo.nz - 1)
    return [pltpu.SemaphoreType.DMA((W, 2, 4, n)), pltpu.SemaphoreType.DMA((W, 2, 4, n))]


def scatter_kernel(geo, W, *refs):
    grads, outs, bufs, sems = refs[:W], refs[W : 2 * W], refs[2 * W : 6 * W], refs[6 * W :]
    barrier(geo)
    S = Scatter(geo, grads, outs, bufs, sems)
    for t in range(W + 4):
        for stage in range(5):
            w = t - stage
            if 0 <= w < W:
                for h in range(2):
                    S.step(w, h, stage)
    for w in range(W):
        for h in range(2):
            S.drain(w, h)


def scatter(geo, grads, collective_id):
    W = len(grads)
    V = pl.BlockSpec(memory_space=pltpu.VMEM)
    return pl.pallas_call(
        functools.partial(scatter_kernel, geo, W),
        out_shape=[jax.ShapeDtypeStruct(g.shape[4:], F32) for g in grads],
        in_specs=[V] * W, out_specs=[V] * W,
        scratch_shapes=scatter_bufs(geo, grads) + scatter_sems(geo, W),
        compiler_params=pltpu.CompilerParams(collective_id=collective_id, has_side_effects=True, vmem_limit_bytes=60 << 20),
        name="scatter",
    )(*grads)


def nn(a, b):
    return lax.dot_general(a, b, (((1,), (0,)), ((), ())), preferred_element_type=F32)


def nt(a, b):
    return lax.dot_general(a, b, (((1,), (1,)), ((), ())), preferred_element_type=F32)


def tn(a, b):
    return lax.dot_general(a, b, (((0,), (0,)), ((), ())), preferred_element_type=F32)


def vm():
    return pl.BlockSpec(memory_space=pltpu.VMEM)


def sm():
    return pl.BlockSpec(memory_space=pltpu.SMEM)


def ends_of(len_ref):
    total, starts, ends = jnp.int32(0), [], []
    for t in range(len_ref.shape[1]):
        starts.append(total)
        total = total + len_ref[0, t]
        ends.append(total)
    return starts, ends


def segment(pos, ends):
    seg = jnp.zeros_like(pos)
    for e in ends:
        seg = seg + (pos >= e).astype(jnp.int32)
    return jnp.where(pos < ends[-1], seg, len(ends) + pos)


def opens(pos, starts, ends):
    hit = jnp.zeros_like(pos)
    for s in starts:
        hit = jnp.where(pos == s, 1, hit)
    return jnp.where(pos < ends[-1], hit, 0)


def lane_half(rows, which):
    lane = lax.broadcasted_iota(jnp.int32, (rows, 128), 1)
    return (lane < 64) if which == 0 else (lane >= 64)


def only(x, which):
    return jnp.where(lane_half(x.shape[0], which), x, jnp.zeros_like(x))


def masks(len_ref, r0, R, J):
    starts, ends = ends_of(len_ref)
    row = lax.broadcasted_iota(jnp.int32, (R, 1), 0) + r0
    col = lax.broadcasted_iota(jnp.int32, (1, J), 1)
    same = segment(row, ends) == segment(col, ends)
    allow = same & (col <= row)
    pick = same & (col < row) & (opens(col, starts, ends) == 0)
    return allow, pick


def ln_stats(x):
    center = x - jnp.mean(x, axis=-1, keepdims=True)
    spread = jnp.mean(center * center, axis=-1, keepdims=True)
    r = lax.rsqrt(spread + EPS)
    return center * r, r


def ln_back(g_h, n, r, gain):
    g_n = g_h * gain
    return r * (g_n - jnp.mean(g_n, axis=-1, keepdims=True) - n * jnp.mean(g_n * n, axis=-1, keepdims=True))


def unpack_cols(blk_ref, full_ref):
    n, _, w = blk_ref.shape
    for f in range(n):
        full_ref[:, f * w : (f + 1) * w] = blk_ref[f]


def qkv_kernel(x_ref, par_ref, w_ref, h1_ref, q_ref, k_ref, v_ref, wf):
    unpack_cols(w_ref, wf)
    D = x_ref.shape[1]
    R = 256
    for b in range(x_ref.shape[0] // R):
        rows = pl.ds(b * R, R)
        n, _ = ln_stats(x_ref[rows, :].astype(F32))
        h1 = (n * par_ref[0:1, :] + par_ref[1:2, :]).astype(BF16)
        h1_ref[rows, :] = h1
        q = (nn(h1, wf[:, 0:D]) + par_ref[4:5, :]).astype(BF16)
        q_ref[rows, :] = q * jnp.asarray(0.125, BF16)
        k_ref[rows, :] = nn(h1, wf[:, D : 2 * D]).astype(BF16)
        v_ref[rows, :] = (nn(h1, wf[:, 2 * D : 3 * D]) + par_ref[5:6, :]).astype(BF16)


def qkv(x, par, w):
    s = jax.ShapeDtypeStruct(x.shape, BF16)
    return pl.pallas_call(
        qkv_kernel, out_shape=[s] * 4, in_specs=[vm()] * 3, out_specs=[vm()] * 4,
        scratch_shapes=[pltpu.VMEM((w.shape[1], w.shape[0] * w.shape[2]), BF16)],
        compiler_params=pltpu.CompilerParams(vmem_limit_bytes=VLIM),
        name="qkv",
    )(x, par, w)


def unpack_pairs(blk_ref, full_ref):
    n, w = blk_ref.shape[0], blk_ref.shape[3] // 2
    for f in range(n):
        for s in range(2):
            full_ref[:, s, :, f * w : (f + 1) * w] = blk_ref[f, :, :, s * w : (s + 1) * w]


def mlp_kernel(R, len_ref, x_ref, cot_ref, mix_ref, par_ref, upb_ref, wo_ref, wu_ref, wd_ref,
               out_ref, gmid_ref, gmix_ref, small_ref, gub_ref, dwo_ref, dwu_ref, dwd_ref,
               wo, wd, act, gin, h2s, gbs):
    T, D = x_ref.shape
    FF = upb_ref.shape[1]
    nf, wf = wu_ref.shape[0], wu_ref.shape[2]
    unpack_cols(wo_ref, wo)
    unpack_pairs(wd_ref, wd)
    _, ends = ends_of(len_ref)
    small_ref[...] = jnp.zeros_like(small_ref)
    gub_ref[...] = jnp.zeros_like(gub_ref)
    cpf = wd.shape[0] // nf
    C0, C1 = 0.7978845608028654, 0.044715

    def block(b, _):
        rows = pl.ds(pl.multiple_of(b * R, R), R)
        x = x_ref[rows, :].astype(F32)
        middle = x + nn(mix_ref[rows, :], wo[...]) + par_ref[6:7, :]
        n2, r2 = ln_stats(middle)
        h2 = (n2 * par_ref[2:3, :] + par_ref[3:4, :]).astype(BF16)
        h2s[rows, :] = h2
        pos = lax.broadcasted_iota(jnp.int32, (R, 1), 0) + b * R
        live = pos < ends[-1]
        gb = jnp.where(live, cot_ref[rows, :].astype(F32), 0.0)
        gbl = gb.astype(BF16)
        gbs[rows, :] = gbl
        branch = jnp.zeros((R, D), F32)
        g_h2 = jnp.zeros((R, D), F32)
        for f in range(nf):
            cols = pl.ds(f * wf, wf)
            wdf = wd[f * cpf : (f + 1) * cpf].reshape(wf, D)
            u = nn(h2, wu_ref[f]) + upb_ref[0:1, f * wf : (f + 1) * wf]
            g_act = nt(gbl, wdf)
            u2 = u * u
            t = jnp.tanh(u * (C0 + (C0 * C1) * u2))
            hp = 0.5 + 0.5 * t
            a = u * hp
            al = a.astype(BF16)
            act[rows, cols] = al
            branch = branch + nn(al, wdf)
            d = hp + (a - a * hp) * (2.0 * C0 + (6.0 * C0 * C1) * u2)
            gi = (g_act * d).astype(BF16)
            gin[rows, cols] = gi
            gub_ref[0:1, f * wf : (f + 1) * wf] += jnp.sum(gi.astype(F32), axis=0, keepdims=True)
            g_h2 = g_h2 + nt(gi, wu_ref[f])
        out_ref[rows, :] = jnp.where(live, middle + branch + par_ref[7:8, :], 0.0).astype(BF16)
        small_ref[2:3, :] += jnp.sum(g_h2 * n2, axis=0, keepdims=True)
        small_ref[3:4, :] += jnp.sum(g_h2, axis=0, keepdims=True)
        g_mid = gb + ln_back(g_h2, n2, r2, par_ref[2:3, :])
        gmid_ref[rows, :] = g_mid
        gml = g_mid.astype(BF16)
        small_ref[6:7, :] += jnp.sum(gml.astype(F32), axis=0, keepdims=True)
        small_ref[7:8, :] += jnp.sum(gb, axis=0, keepdims=True)
        gmix_ref[rows, :] = nt(gml, wo[...]).astype(BF16)
        return 0

    lax.fori_loop(0, T // R, block, 0)
    w4 = D // nf

    def put(ref, grad, lead):
        r = ref.shape[2]
        c = grad.shape[0] // (2 * r)
        g = grad.astype(BF16).reshape(c, 2, r, D)
        for f in range(nf):
            for s in range(2):
                ref[f, pl.ds(lead, c), :, s * w4 : (s + 1) * w4] = g[:, s, :, f * w4 : (f + 1) * w4]

    def outp(i, _):
        g = tn(mix_ref[:, pl.ds(pl.multiple_of(i * 384, 128), 384)], gmid_ref[...].astype(BF16)).astype(BF16)
        for f in range(nf):
            dwo_ref[f, pl.ds(pl.multiple_of(i * 384, 128), 384), :] = g[:, f * w4 : (f + 1) * w4]
        return 0

    lax.fori_loop(0, D // 384, outp, 0)
    K = 384
    cpk = K // (2 * dwd_ref.shape[2])

    def down(i, _):
        put(dwd_ref, tn(act[:, pl.ds(pl.multiple_of(i * K, 128), K)], gbs[...]), i * cpk)
        return 0

    lax.fori_loop(0, FF // K, down, 0)
    H = 384

    def up(i, _):
        f, s = i // (wf // H), i % (wf // H)
        dwu_ref[f, :, pl.ds(pl.multiple_of(s * H, 128), H)] = tn(h2s[...], gin[:, pl.ds(pl.multiple_of(i * H, 128), H)]).astype(BF16)
        return 0

    lax.fori_loop(0, FF // H, up, 0)


def mlp(lengths, x, cot, mixed, par, upb, wo, wu, wd, R=256):
    T, D = x.shape
    FF = upb.shape[1]
    S = jax.ShapeDtypeStruct
    V = pltpu.VMEM
    return pl.pallas_call(
        functools.partial(mlp_kernel, R),
        out_shape=[S((T, D), BF16), S((T, D), F32), S((T, D), BF16), S((8, D), F32), S((8, FF), F32),
                   S(wo.shape, BF16), S(wu.shape, BF16), S(wd.shape, BF16)],
        in_specs=[sm()] + [vm()] * 8, out_specs=[vm()] * 8,
        scratch_shapes=[V((D, D), BF16), V((wd.shape[1], 2, wd.shape[2], D), BF16),
                        V((T, FF), BF16), V((T, FF), BF16), V((T, D), BF16), V((T, D), BF16)],
        compiler_params=pltpu.CompilerParams(vmem_limit_bytes=VLIM),
        name="mlp",
    )(lengths, x, cot, mixed, par, upb, wo, wu, wd)


def qkv_back_kernel(x_ref, h1_ref, gp_ref, gmid_ref, par_ref, w_ref, ig_ref, small_ref, dw_ref):
    T, D = x_ref.shape
    n, _, w = w_ref.shape
    R = 256
    for f in range(n):
        dw_ref[f] = tn(h1_ref[...], gp_ref[:, f * w : (f + 1) * w]).astype(BF16)
    small_ref[...] = jnp.zeros_like(small_ref)
    for b in range(T // R):
        rows = pl.ds(b * R, R)
        g_h1 = jnp.zeros((R, D), F32)
        for f in range(n):
            g_h1 = g_h1 + nt(gp_ref[rows, f * w : (f + 1) * w], w_ref[f])
        n1, r1 = ln_stats(x_ref[rows, :].astype(F32))
        small_ref[0:1, :] += jnp.sum(g_h1 * n1, axis=0, keepdims=True)
        small_ref[1:2, :] += jnp.sum(g_h1, axis=0, keepdims=True)
        small_ref[4:5, :] += jnp.sum(gp_ref[rows, 0:D].astype(F32), axis=0, keepdims=True)
        small_ref[5:6, :] += jnp.sum(gp_ref[rows, 2 * D : 3 * D].astype(F32), axis=0, keepdims=True)
        ig_ref[rows, :] = (gmid_ref[rows, :] + ln_back(g_h1, n1, r1, par_ref[0:1, :])).astype(BF16)


def qkv_back(x, h1, gp, gmid, par, w):
    S = jax.ShapeDtypeStruct
    return pl.pallas_call(
        qkv_back_kernel, out_shape=[S(x.shape, BF16), S((8, x.shape[1]), F32), S(w.shape, BF16)],
        in_specs=[vm()] * 6, out_specs=[vm()] * 3,
        compiler_params=pltpu.CompilerParams(vmem_limit_bytes=VLIM),
        name="qkv_back",
    )(x, h1, gp, gmid, par, w)


def masks_t(len_ref, r0, R, J):
    starts, ends = ends_of(len_ref)
    key = lax.broadcasted_iota(jnp.int32, (J, 1), 0)
    row = lax.broadcasted_iota(jnp.int32, (1, R), 1) + r0
    same = segment(key, ends) == segment(row, ends)
    return same & (key < row) & (opens(key, starts, ends) == 0)


def carried_scores(len_ref, q_ref, k_ref, cm, cmT_ref, carry):
    T = q_ref.shape[0]
    carry[...] = jnp.zeros_like(carry)
    i = lax.broadcasted_iota(jnp.int32, (B, B), 0)
    j = lax.broadcasted_iota(jnp.int32, (B, B), 1)
    lower = jnp.where(j < i, 1.0, 0.0).astype(BF16)
    for b in range(T // B):
        r0, J = b * B, (b + 1) * B
        rows = pl.ds(r0, B)
        allow, pick = masks(len_ref, r0, B, J)
        s0 = jnp.maximum(nt(only(q_ref[rows, 0:128], 0), k_ref[0:J, 0:128]), 0.0)
        chosen = jnp.where(pick, s0 * s0, 0.0)
        hi = chosen.astype(BF16)
        lo = (chosen - hi.astype(F32)).astype(BF16)
        carried = carry[0:1, 0:J] + (nn(lower, hi) + nn(lower, lo))
        c = jnp.where(allow, carried, BIG)
        cm[rows, 0:J] = c
        cmT_ref[0:J, rows] = jnp.transpose(c)
        carry[0:1, 0:J] = carry[0:1, 0:J] + jnp.sum(chosen, axis=0, keepdims=True)


def fwd_pair(p, q_ref, k_ref, v_ref, o_ref, lse, cm, s_sc, p_sc, C):
    T = q_ref.shape[0]
    lane = lax.broadcasted_iota(jnp.int32, (C, 128), 1)
    cols = pl.ds(pl.multiple_of(p * 128, 128), 128)
    k2, v2 = k_ref[:, cols], v_ref[:, cols]
    for half in range(2):
        q2 = only(q_ref[:, cols], half)
        for kb in range(T // B):
            s_sc[half, kb * B :, kb * B : (kb + 1) * B] = nt(q2[kb * B :], k2[kb * B : (kb + 1) * B])
    for rb in range(T // C):
        J = ((rb * C) // B + 1) * B
        rows = slice(rb * C, (rb + 1) * C)
        inv = []
        for half in range(2):
            l = s_sc[half, rows, :J] - cm[rows, :J]
            m = jnp.max(l, axis=1, keepdims=True)
            e = jnp.exp(l - m)
            t = jnp.sum(e, axis=1, keepdims=True)
            p_sc[half, rows, :J] = (e * (1.0 / t)).astype(BF16)
            lse[rows, :] = jnp.where(lane == 2 * p + half, m + jnp.log(t), lse[rows, :])
        if (rb * C) % B == B - C:
            b0 = (rb * C) // B * B
            o = [nn(p_sc[half, b0 : b0 + B, :J], v2[:J]) for half in range(2)]
            lanes = lax.broadcasted_iota(jnp.int32, (B, 128), 1)
            o_ref[b0 : b0 + B, cols] = jnp.where(lanes < 64, o[0], o[1]).astype(BF16)


def attn_fwd_kernel(C, len_ref, q_ref, k_ref, v_ref, o_ref, lseT_ref, cmT_ref, cm, lse, s_sc, p_sc, carry):
    carried_scores(len_ref, q_ref, k_ref, cm, cmT_ref, carry)

    def pair(p, _):
        fwd_pair(p, q_ref, k_ref, v_ref, o_ref, lse, cm, s_sc, p_sc, C)
        return 0

    lax.fori_loop(0, HEADS // 2, pair, 0)
    lseT_ref[...] = jnp.transpose(lse[...])[0:16]


def attn_fwd(lengths, q, k, v, C=64):
    T = q.shape[0]
    V = pltpu.VMEM
    return pl.pallas_call(
        functools.partial(attn_fwd_kernel, C),
        out_shape=[jax.ShapeDtypeStruct(q.shape, BF16), jax.ShapeDtypeStruct((16, T), F32), jax.ShapeDtypeStruct((T, T), F32)],
        in_specs=[sm()] + [vm()] * 3, out_specs=[vm()] * 3,
        scratch_shapes=[V((T, T), F32), V((T, 128), F32), V((2, T, T), F32), V((2, T, T), BF16), V((8, T), F32)],
        compiler_params=pltpu.CompilerParams(vmem_limit_bytes=VLIM),
        name="attn_fwd",
    )(lengths, q, k, v)


def row_sums(do_ref, o_ref, DT):
    T, D = do_ref.shape
    f = lax.broadcasted_iota(jnp.int32, (D, 128), 0)
    h = lax.broadcasted_iota(jnp.int32, (D, 128), 1)
    E = jnp.where((f >= h * 64) & (f < h * 64 + 64), 1.0, 0.0).astype(BF16)
    for b in range(T // B):
        rows = pl.ds(b * B, B)
        x = do_ref[rows, :].astype(F32) * o_ref[rows, :].astype(F32)
        hi = x.astype(BF16)
        lo = (x - hi.astype(F32)).astype(BF16)
        DT[:, rows] = jnp.transpose(nn(hi, E) + nn(lo, E))[0:16]


def bwd_scores(p, half, q_ref, k_ref, v_ref, do_ref, sT, dpT):
    T = q_ref.shape[0]
    cols = p * 128 if isinstance(p, int) else pl.multiple_of(p * 128, 128)
    c = pl.ds(cols, 128)
    k2, v2 = k_ref[:, c], v_ref[:, c]
    q2, do2 = only(q_ref[:, c], half), only(do_ref[:, c], half)
    for rb in range(T // B):
        J, r = (rb + 1) * B, slice(rb * B, (rb + 1) * B)
        sT[0:J, r] = nt(k2[0:J], q2[r])
        dpT[0:J, r] = nt(v2[0:J], do2[r])


def bwd_softmax(h, sT, dpT, pT, dsT, lseT, DT, cmT, C, add_into=None, keep=None):
    T = sT.shape[0]
    for kc in range(T // C):
        i0 = (kc * C) // B * B
        keys = slice(kc * C, (kc + 1) * C)
        pr = jnp.exp(sT[keys, i0:] - cmT[keys, i0:] - lseT[pl.ds(h, 1), i0:])
        ds = pr * (dpT[keys, i0:] - DT[pl.ds(h, 1), i0:])
        pT[keys, i0:] = pr.astype(BF16)
        if keep is not None:
            keep[keys, i0:] = ds
        else:
            dsT[keys, i0:] = ds.astype(BF16)
        add_into[keys, i0:] += ds


def bwd_products(p, half, q_ref, k_ref, do_ref, pT, dsT, gp_ref, dk, dv, first):
    T, D = q_ref.shape
    cols = p * 128 if isinstance(p, int) else pl.multiple_of(p * 128, 128)
    c = pl.ds(cols, 128)
    k2 = k_ref[:, c]
    q2, do2 = only(q_ref[:, c], half), only(do_ref[:, c], half)
    for kb in range(T // B):
        keys = slice(kb * B, (kb + 1) * B)
        a = nn(pT[keys, kb * B :], do2[kb * B :])
        d = nn(dsT[keys, kb * B :], q2[kb * B :])
        if first:
            dv[keys, :], dk[keys, :] = a, d
        else:
            dv[keys, :] += a
            dk[keys, :] += d
    lanes = lax.broadcasted_iota(jnp.int32, (B, 128), 1)
    for rb in range(T // B):
        J, r = (rb + 1) * B, slice(rb * B, (rb + 1) * B)
        dq = (tn(dsT[0:J, r], k2[0:J]) * 0.125).astype(BF16)
        if first:
            gp_ref[r, c] = dq
        else:
            gp_ref[r, c] = jnp.where((lanes < 64) == (half == 0), dq, gp_ref[r, c])


def first_head(len_ref, sT, ds0, dsT, G):
    T = sT.shape[0]
    i = lax.broadcasted_iota(jnp.int32, (B, B), 0)
    j = lax.broadcasted_iota(jnp.int32, (B, B), 1)
    after = jnp.where(i > j, 1.0, 0.0).astype(BF16)
    later = jnp.zeros((T, 1), F32)
    for rb in reversed(range(T // B)):
        J, r = (rb + 1) * B, slice(rb * B, (rb + 1) * B)
        g = -G[0:J, r]
        hi = g.astype(BF16)
        lo = (g - hi.astype(F32)).astype(BF16)
        g_chosen = later[0:J] + (nn(hi, after) + nn(lo, after))
        later = later[0:J] + jnp.sum(g, axis=1, keepdims=True)
        pick = masks_t(len_ref, rb * B, B, J)
        full = ds0[0:J, r] + jnp.where(pick, 2.0 * jnp.maximum(sT[0:J, r], 0.0) * g_chosen, 0.0)
        dsT[0:J, r] = full.astype(BF16)


def attn_bwd_kernel(C, len_ref, q_ref, k_ref, v_ref, do_ref, o_ref, lseT, cmT, gp_ref, DT, sT, dpT, pT, dsT, G, dk, dv):
    T, D = q_ref.shape
    row_sums(do_ref, o_ref, DT)
    G[...] = jnp.zeros_like(G)

    def put(p):
        ck = D + p * 128 if isinstance(p, int) else pl.multiple_of(D + p * 128, 128)
        cv = 2 * D + p * 128 if isinstance(p, int) else pl.multiple_of(2 * D + p * 128, 128)
        gp_ref[:, pl.ds(ck, 128)] = dk[...].astype(BF16)
        gp_ref[:, pl.ds(cv, 128)] = dv[...].astype(BF16)

    def pair(k, _):
        p = HEADS // 2 - 1 - k
        for half in range(2):
            bwd_scores(p, half, q_ref, k_ref, v_ref, do_ref, sT.at[half], dpT.at[half])
        for half in range(2):
            bwd_softmax(2 * p + half, sT.at[half], dpT.at[half], pT.at[half], dsT.at[half], lseT, DT, cmT, C, G)
        for half in range(2):
            bwd_products(p, half, q_ref, k_ref, do_ref, pT.at[half], dsT.at[half], gp_ref, dk, dv, half == 0)
        put(p)
        return 0

    lax.fori_loop(0, HEADS // 2 - 1, pair, 0)
    bwd_scores(0, 1, q_ref, k_ref, v_ref, do_ref, sT.at[1], dpT.at[1])
    bwd_softmax(1, sT.at[1], dpT.at[1], pT.at[1], dsT.at[1], lseT, DT, cmT, C, G)
    bwd_products(0, 1, q_ref, k_ref, do_ref, pT.at[1], dsT.at[1], gp_ref, dk, dv, True)
    bwd_scores(0, 0, q_ref, k_ref, v_ref, do_ref, sT.at[0], dpT.at[0])
    bwd_softmax(0, sT.at[0], dpT.at[0], pT.at[0], dsT.at[0], lseT, DT, cmT, C, G, keep=dpT.at[0])
    first_head(len_ref, sT.at[0], dpT.at[0], dsT.at[0], G)
    bwd_products(0, 0, q_ref, k_ref, do_ref, pT.at[0], dsT.at[0], gp_ref, dk, dv, False)
    put(0)


def attn_bwd(lengths, q, k, v, do, o, lseT, cmT, C=64):
    T, D = q.shape
    V = pltpu.VMEM
    return pl.pallas_call(
        functools.partial(attn_bwd_kernel, C),
        out_shape=jax.ShapeDtypeStruct((T, 3 * D), BF16),
        in_specs=[sm()] + [vm()] * 7, out_specs=vm(),
        scratch_shapes=[V((16, T), F32), V((2, T, T), F32), V((2, T, T), F32), V((2, T, T), BF16), V((2, T, T), BF16), V((T, T), F32), V((T, 128), F32), V((T, 128), F32)],
        compiler_params=pltpu.CompilerParams(vmem_limit_bytes=VLIM),
        name="attn_bwd",
    )(lengths, q, k, v, do, o, lseT, cmT)


def fold_tiny(tiny, par, per, n_dp, F):
    for f in range(F):
        for d in range(n_dp):
            for s in range(2):
                par[s * F + f : s * F + f + 1, d * per : (d + 1) * per] = tiny[f, d, 0, s : s + 1, 0:per].astype(F32)


def front_kernel(geo, C, *refs):
    len_ref, x_ref = refs[0:2]
    shards, bufs = refs[2:7], refs[7:12]
    h1_o, q_o, k_o, v_o, mix_o, lseT_o, cmT_o = refs[12:19]
    tiny_v, wq_v, wf, par, h1, q, k, v, mix, cmT, cm, lse, s_sc, p_sc, carry, lsem, osem = refs[19:36]
    sems = refs[36:]
    T, D = x_ref.shape
    F, per = geo.n_fs, D // geo.n_dp
    barrier(geo)
    G = Gather(geo, shards, bufs, sems)

    def ev(*items):
        for w, stage in items:
            for h in range(2):
                if stage == 4:
                    G.finish(w, h)
                else:
                    G.start(w, h, stage)

    ev((0, 0), (1, 0), (2, 0))
    for b in range(T // B):
        rows = pl.ds(b * B, B)
        n, _ = ln_stats(x_ref[rows, :].astype(F32))
        s_sc[0, rows, 0:D] = n
    ev((0, 1), (1, 1), (3, 0), (0, 2), (1, 2), (2, 1), (0, 3), (1, 3), (2, 2), (4, 0), (3, 1), (0, 4), (1, 4))
    get_t = pltpu.make_async_copy(bufs[0], tiny_v, lsem.at[0])
    get_q = pltpu.make_async_copy(bufs[1], wq_v, lsem.at[1])
    get_t.start()
    get_q.start()
    get_t.wait()
    fold_tiny(tiny_v.reshape(F, geo.n_dp, 2, 16, 128), par, per, geo.n_dp, F)
    get_q.wait()
    unpack_cols(wq_v.reshape(F, D, wq_v.shape[-1]), wf)
    outs = [pltpu.make_async_copy(a, b, osem.at[i]) for i, (a, b) in enumerate(((h1, h1_o), (q, q_o), (k, k_o), (v, v_o), (cmT, cmT_o), (mix, mix_o), (lse, lse))[:6])]
    for b in range(T // B):
        rows = pl.ds(b * B, B)
        hb = (s_sc[0, rows, 0:D] * par[0:1, :] + par[1:2, :]).astype(BF16)
        h1[rows, :] = hb
        q[rows, :] = (nn(hb, wf[:, 0:D]) + par[4:5, :]).astype(BF16) * jnp.asarray(0.125, BF16)
        k[rows, :] = nn(hb, wf[:, D : 2 * D]).astype(BF16)
        v[rows, :] = (nn(hb, wf[:, 2 * D : 3 * D]) + par[5:6, :]).astype(BF16)
        if b == 1:
            ev((2, 3), (3, 2))
    for i in range(4):
        outs[i].start()
    ev((4, 1))
    carried_scores(len_ref, q, k, cm, cmT, carry)
    outs[4].start()
    plan = {1: ((3, 3), (4, 2)), 4: ((4, 3),)}

    def pair(p, _):
        for at, items in plan.items():
            @pl.when(p == at)
            def _():
                ev(*items)
        fwd_pair(p, q, k, v, mix, lse, cm, s_sc, p_sc, C)
        return 0

    lax.fori_loop(0, HEADS // 2, pair, 0)
    outs[5].start()
    lseT_o[...] = jnp.transpose(lse[...])[0:16]
    ev((2, 4), (3, 4), (4, 4))
    for w in range(5):
        for h in range(2):
            G.drain(w, h)
    for i in range(6):
        outs[i].wait()


def front(geo, lengths, x, shards, collective_id=0, C=64):
    T, D = x.shape
    V, S, A = pltpu.VMEM, jax.ShapeDtypeStruct, pl.BlockSpec(memory_space=pl.ANY)
    lead = (geo.nx, geo.nc, geo.nz, geo.ny)
    tok = S((T, D), BF16)
    res = pl.pallas_call(
        functools.partial(front_kernel, geo, C),
        out_shape=[S(lead + s.shape, s.dtype) for s in shards] + [tok] * 5 + [S((16, T), F32), S((T, T), F32)],
        in_specs=[sm(), vm()] + [A] * 5,
        out_specs=[A] * 10 + [vm(), A],
        scratch_shapes=[V(lead + shards[0].shape, BF16), V(lead + shards[1].shape, BF16), V((D, 3 * D), BF16), V((8, D), F32)]
        + [V((T, D), BF16)] * 5 + [V((T, T), F32), V((T, T), F32), V((T, 128), F32), V((2, T, T), F32), V((2, T, T), BF16), V((8, T), F32)]
        + [pltpu.SemaphoreType.DMA((2,)), pltpu.SemaphoreType.DMA((6,))] + gather_sems(geo, 5),
        compiler_params=pltpu.CompilerParams(collective_id=collective_id, has_side_effects=True, vmem_limit_bytes=VLIM),
        name="front",
    )(lengths, x, *shards)
    return res[:5], res[5:]


def spread_tiny(small, tiny, per, n_dp, F):
    for f in range(F):
        for d in range(n_dp):
            for s in range(2):
                tiny[f, d, 0, s : s + 1, 0:per] = small[s * F + f : s * F + f + 1, d * per : (d + 1) * per]


def back_kernel(geo, C, *refs):
    len_ref, lseT, tiny_in, small_b, par = refs[0:5]
    q_h, k_h, v_h, do_h, o_h, cmT_h, x_h, h1_h, gmid_h, wq_h = refs[5:15]
    parts = refs[15:18]
    ig_o = refs[18]
    outs = refs[19:24]
    gp, DT, small, tiny, isem, osem, own_sem = refs[24:31]
    owns = list(refs[31:34]) + [None, None]
    bufs, sems = refs[34:54], refs[54:56]
    D, T = gp.shape[1] // 3, gp.shape[0]
    F, n_dp = geo.n_fs, geo.n_dp
    per = D // n_dp
    barrier(geo)
    S = Scatter(geo, list(parts) + [None, tiny], outs, bufs, sems, owns, own_sem)
    DOWN, UP, OUT, QKV, TINY = range(5)

    def ev(*items):
        for w, stage in items:
            for h in range(2):
                S.step(w, h, stage)

    ev((DOWN, 0), (UP, 0), (OUT, 0))

    def attention(q, k, v, do, o, cmT, sT, dpT, pT, dsT, G, dk, dv):
        ins = [pltpu.make_async_copy(a, b, isem.at[i]) for i, (a, b) in enumerate(((do_h, do), (o_h, o), (q_h, q), (k_h, k), (v_h, v), (cmT_h, cmT)))]
        for cp in ins:
            cp.start()
        G[...] = jnp.zeros_like(G)
        ins[0].wait()
        ins[1].wait()
        row_sums(do, o, DT)
        for cp in ins[2:]:
            cp.wait()

        def put(p):
            ck = D + p * 128 if isinstance(p, int) else pl.multiple_of(D + p * 128, 128)
            cv = 2 * D + p * 128 if isinstance(p, int) else pl.multiple_of(2 * D + p * 128, 128)
            gp[:, pl.ds(ck, 128)] = dk[...].astype(BF16)
            gp[:, pl.ds(cv, 128)] = dv[...].astype(BF16)

        plan = {(0, 0): ((DOWN, 1),), (0, 1): ((UP, 1),), (2, 1): ((DOWN, 2),), (3, 0): ((OUT, 1),), (4, 0): ((DOWN, 3),)}

        def pair(n, _):
            p = HEADS // 2 - 1 - n
            for half in range(2):
                for (at, hf), items in plan.items():
                    if hf == half:
                        @pl.when(n == at)
                        def _():
                            ev(*items)
                bwd_scores(p, half, q, k, v, do, sT, dpT)
                bwd_softmax(2 * p + half, sT, dpT, pT, dsT, lseT, DT, cmT, C, G)
                bwd_products(p, half, q, k, do, pT, dsT, gp, dk, dv, half == 0)
            put(p)
            return 0

        lax.fori_loop(0, HEADS // 2 - 1, pair, 0)
        ev((UP, 2))
        bwd_scores(0, 1, q, k, v, do, sT, dpT)
        bwd_softmax(1, sT, dpT, pT, dsT, lseT, DT, cmT, C, G)
        bwd_products(0, 1, q, k, do, pT, dsT, gp, dk, dv, True)
        ev((OUT, 2), (DOWN, 4))
        bwd_scores(0, 0, q, k, v, do, sT, dpT)
        bwd_softmax(0, sT, dpT, pT, dsT, lseT, DT, cmT, C, G, keep=dpT)
        first_head(len_ref, sT, dpT, dsT, G)
        bwd_products(0, 0, q, k, do, pT, dsT, gp, dk, dv, False)
        put(0)

    V = pltpu.VMEM
    pl.run_scoped(
        attention, *[V((T, D), BF16)] * 5, V((T, T), F32), V((T, T), F32), V((T, T), F32), V((T, T), BF16), V((T, T), BF16), V((T, T), F32),
        V((T, 128), F32), V((T, 128), F32),
    )

    def projections(x, h1, gmid, wq, dwq, ig):
        ins = [pltpu.make_async_copy(a, b, isem.at[i]) for i, (a, b) in enumerate(((h1_h, h1), (wq_h, wq), (x_h, x), (gmid_h, gmid)))]
        for cp in ins:
            cp.start()
        n, _, w = wq.shape
        dw = dwq.reshape(n, D, w)
        ins[0].wait()
        for f in range(n):
            dw[f] = tn(h1[...], gp[:, f * w : (f + 1) * w]).astype(BF16)
            if f == 1:
                ev((UP, 3), (OUT, 3))
        S.grads[QKV] = dwq
        ev((QKV, 0))
        small[...] = small_b[...]
        for cp in ins[1:]:
            cp.wait()
        for b in range(T // B):
            rows = pl.ds(b * B, B)
            g_h1 = jnp.zeros((B, D), F32)
            for f in range(n):
                g_h1 = g_h1 + nt(gp[rows, f * w : (f + 1) * w], wq[f])
            n1, r1 = ln_stats(x[rows, :].astype(F32))
            small[0:1, :] += jnp.sum(g_h1 * n1, axis=0, keepdims=True)
            small[1:2, :] += jnp.sum(g_h1, axis=0, keepdims=True)
            small[4:5, :] += jnp.sum(gp[rows, 0:D].astype(F32), axis=0, keepdims=True)
            small[5:6, :] += jnp.sum(gp[rows, 2 * D : 3 * D].astype(F32), axis=0, keepdims=True)
            ig[rows, :] = (gmid[rows, :] + ln_back(g_h1, n1, r1, par[0:1, :])).astype(BF16)
            if b == 1:
                ev((QKV, 1))
        out_cp = pltpu.make_async_copy(ig, ig_o, osem)
        out_cp.start()
        tiny[...] = tiny_in[...]
        spread_tiny(small, tiny.reshape(F, n_dp, 2, 8, 128), per, n_dp, F)
        ev((TINY, 0), (TINY, 1), (QKV, 2), (TINY, 2), (UP, 4), (OUT, 4), (TINY, 3), (QKV, 3), (TINY, 4), (QKV, 4))
        for wt in range(5):
            for h in range(2):
                S.drain(wt, h)
        out_cp.wait()

    pl.run_scoped(projections, V((T, D), BF16), V((T, D), BF16), V((T, D), F32), V(wq_h.shape, BF16), V((geo.nx, geo.nc, geo.nz, geo.ny, 2, per // 2, wq_h.shape[-1]), BF16), V((T, D), BF16))


def back(geo, lengths, lseT, tiny_in, small_b, par, q, k, v, do, o, cmT, x, h1, gmid, wq, parts, collective_id=1, C=64):
    T, D = x.shape
    V, S, A, D_ = pltpu.VMEM, jax.ShapeDtypeStruct, pl.BlockSpec(memory_space=pl.ANY), pltpu.SemaphoreType.DMA
    per = D // geo.n_dp
    dwq = S((geo.nx, geo.nc, geo.nz, geo.ny, 2, per // 2, wq.shape[-1]), BF16)
    grads = list(parts) + [dwq, S(tiny_in.shape, F32)]
    owns = [V((2, geo.nx, geo.nz, geo.ny) + g.shape[5:], BF16) for g in parts]
    return pl.pallas_call(
        functools.partial(back_kernel, geo, C),
        out_shape=[S((T, D), BF16)] + [S(g.shape[4:], F32) for g in grads],
        in_specs=[sm()] + [vm()] * 4 + [A] * 13,
        out_specs=[A] + [vm()] * 5,
        scratch_shapes=[V((T, 3 * D), BF16), V((16, T), F32), V((8, D), F32), V(tiny_in.shape, F32), D_((6,)), D_, D_((3, 2))]
        + owns + scatter_bufs(geo, grads) + scatter_sems(geo, 5),
        compiler_params=pltpu.CompilerParams(collective_id=collective_id, has_side_effects=True, vmem_limit_bytes=VLIM),
        name="back",
    )(lengths, lseT, tiny_in, small_b, par, q, k, v, do, o, cmT, x, h1, gmid, wq, *parts)


def pair_up(shard):
    w = shard.shape[1]
    return shard.reshape(2, 2, -1, w).transpose(0, 2, 1, 3).reshape(2, -1, 2 * w)


def pair_down(halves):
    w = halves.shape[2] // 2
    return halves.reshape(2, -1, 2, w).transpose(0, 2, 1, 3).reshape(-1, w)


def repair(blocks, r):
    n, c, r0, w2 = blocks.shape
    if r0 == r:
        return blocks
    w = w2 // 2
    flat = blocks.reshape(n, c, r0, 2, w).transpose(0, 1, 3, 2, 4).reshape(n, -1, 2, r, w)
    return flat.transpose(0, 1, 3, 2, 4).reshape(n, -1, r, w2)


def body(geo, tokens, cotangent, lengths, norm_params, bias_params, w_qkv, w_out, w_up, up_bias, w_down):
    T, D = tokens.shape
    F, n_dp, per = geo.n_fs, geo.n_dp, D // geo.n_dp
    FF = D * F * up_bias.shape[1]
    fused = (per // 2) % 16 == 0
    tiny = jnp.stack([jnp.stack([norm_params[:, 0], bias_params[:, 0]]), jnp.stack([up_bias[:, 0]] * 2)])
    tiny = jnp.pad(tiny, ((0, 0), (0, 14), (0, 128 - per)))

    def halves(shard):
        return shard.reshape(2, -1, shard.shape[1])

    shards = [tiny, halves(w_qkv), halves(w_out), halves(w_up), pair_up(w_down)]
    if fused:
        bufs, (h1, q, k, v, mixed, lse, cm) = front(geo, lengths, tokens, shards)
    else:
        bufs = gather(geo, shards)
    t = bufs[0].reshape(F, n_dp, 2, 16, 128)[..., :per].astype(F32)
    par = jnp.concatenate([t[:, :, 0, 0].reshape(F, D), t[:, :, 0, 1].reshape(F, D)], axis=0)
    upb = jnp.broadcast_to(t[:, :, 1, 0].reshape(F, D).T.reshape(1, FF), (8, FF))
    wq, wo, wu = (b.reshape(F, D, b.shape[-1]) for b in bufs[1:4])
    wd = repair(bufs[4].reshape((F, n_dp * 2) + bufs[4].shape[-2:]), FF // 32)
    if not fused:
        h1, q, k, v = qkv(tokens, par, wq)
        mixed, lse, cm = attn_fwd(lengths, q, k, v)

    out, gmid, gmix, small_b, gub, dwo, dwu, dwd = mlp(lengths, tokens, cotangent, mixed, par, upb, wo, wu, wd)
    r = per // 2

    def split(grad, rows):
        return grad.reshape((geo.nx, geo.nc, geo.nz, geo.ny, 2, rows, grad.shape[-1]))

    ub = gub[0].reshape(D, F).T.reshape(F, n_dp, per)

    def pack(small):
        rows = jnp.stack([small[0:4], small[4:8]]).reshape(2, F, n_dp, per)
        g = jnp.stack([jnp.stack([rows[0], rows[1]], axis=2), jnp.stack([ub, ub], axis=2)], axis=2)
        return split(jnp.pad(g, ((0, 0), (0, 0), (0, 0), (0, 6), (0, 128 - per))), 8)

    dwd = repair(dwd, FF // n_dp // 4)
    parts = [split(dwo, r), split(dwu, r), split(dwd, FF // n_dp // 4)]
    if fused:
        ig, s_down, s_up, s_out, s_qkv, s_tiny = back(
            geo, lengths, lse, pack(jnp.zeros_like(small_b)), small_b, par, q, k, v, gmix, mixed, cm, tokens, h1, gmid, wq, parts[::-1]
        )
    else:
        gp = attn_bwd(lengths, q, k, v, gmix, mixed, lse, cm)
        ig, small_a, dwq = qkv_back(tokens, h1, gp, gmid, par, wq)
        s_tiny, s_out, s_up, s_down, s_qkv = scatter(geo, [pack(small_a + small_b)] + parts + [split(dwq, r)], 1)
    return (
        out,
        ig,
        s_tiny[0, 0, :per, None],
        s_tiny[0, 1, :per, None],
        s_qkv.reshape(-1, s_qkv.shape[-1]),
        s_out.reshape(-1, s_out.shape[-1]),
        s_up.reshape(-1, s_up.shape[-1]),
        s_tiny[1, 0, :per, None],
        pair_down(s_down),
    )


def solution(mesh):
    geo = Geo(mesh.shape["dp"], mesh.shape["fsdp"])
    both, split = P(("dp", "fsdp"), None), P("dp", "fsdp")
    return jax.shard_map(
        functools.partial(body, geo), mesh=mesh, in_specs=(both,) * 3 + (split,) * 7, out_specs=(both,) * 2 + (split,) * 7, check_vma=False
    )
```

```python
import functools

import jax
import jax.numpy as jnp
from jax import lax
from jax.experimental import pallas as pl
from jax.experimental.pallas import tpu as pltpu
from jax.sharding import PartitionSpec as P

HEADS = 12
EPS = 1e-05
BIG = 1e30
B = 256
F32, BF16 = jnp.float32, jnp.bfloat16
VLIM = 60 << 20
MESH = pl.DeviceIdType.MESH


class Geo:
    def __init__(self, n_dp, n_fs):
        self.n_dp, self.n_fs = n_dp, n_fs
        self.ny = 2 if n_dp % 2 == 0 else 1
        self.nz = n_dp // self.ny
        self.nc = 2 if n_fs % 2 == 0 else 1
        self.nx = n_fs // self.nc

    def place(self):
        dp, fs = lax.axis_index("dp"), lax.axis_index("fsdp")
        return dp // self.ny, dp % self.ny, fs // self.nc, fs % self.nc

    def dev(self, z, y, x, c):
        return {"dp": z * self.ny + y, "fsdp": x * self.nc + c}


def others(n, me):
    return [lax.rem(me + k, n) for k in range(1, n)]

def barrier(geo):
    z, y, x, c = geo.place()
    sem = pltpu.get_barrier_semaphore()
    count = 0
    for k in range(1, geo.nz):
        pl.semaphore_signal(sem, inc=1, device_id=geo.dev(lax.rem(z + k, geo.nz), y, x, c), device_id_type=MESH); count += 1
    for k in range(1, geo.ny):
        pl.semaphore_signal(sem, inc=1, device_id=geo.dev(z, lax.rem(y + k, geo.ny), x, c), device_id_type=MESH); count += 1
    for k in range(1, geo.nx):
        pl.semaphore_signal(sem, inc=1, device_id=geo.dev(z, y, lax.rem(x + k, geo.nx), c), device_id_type=MESH); count += 1
    for k in range(1, geo.nc):
        pl.semaphore_signal(sem, inc=1, device_id=geo.dev(z, y, x, lax.rem(c + k, geo.nc)), device_id_type=MESH); count += 1
    pl.semaphore_wait(sem, count)

class Gather:
    def __init__(self, geo, shards, outs, sems):
        self.geo, self.shards, self.outs = geo, shards, outs
        self.lsem, self.s0, self.r0, self.s1, self.r1 = sems
        self.z, self.y, self.x, self.c = geo.place()

    def local(self, w, h):
        o = self.outs[w]
        return pltpu.make_async_copy(self.shards[w].at[h], o.at[self.x, self.c, self.z, self.y, h], self.lsem.at[w, h])

    def zcopy(self, w, h, k):
        g = self.geo
        zt = lax.rem(self.z + k, g.nz)
        return pltpu.make_async_remote_copy(
            src_ref=self.shards[w].at[h], dst_ref=self.outs[w].at[self.x, self.c, self.z, self.y, h],
            send_sem=self.s0.at[w, h, k], recv_sem=self.r0.at[w, h, k],
            device_id=g.dev(zt, self.y, self.x, self.c), device_id_type=MESH)

    def zrecv(self, w, h, k):
        g = self.geo
        zf = lax.rem(self.z + g.nz - k, g.nz)
        return pltpu.make_async_remote_copy(
            src_ref=self.shards[w].at[h], dst_ref=self.outs[w].at[self.x, self.c, zf, self.y, h],
            send_sem=self.s0.at[w, h, k], recv_sem=self.r0.at[w, h, k],
            device_id=g.dev(zf, self.y, self.x, self.c), device_id_type=MESH)

    def pair(self, w, h, stage, k, recv):
        g, o = self.geo, self.outs[w]
        z, y, x, c = self.z, self.y, self.x, self.c
        sgn = -1 if recv else 1
        kind = "c" if stage == 3 else ("y" if (stage == 1) == (h == 0) else "x")
        py = lax.rem(y + sgn * k + g.ny, g.ny); px = lax.rem(x + sgn * k + g.nx, g.nx); pc = lax.rem(c + sgn * k + g.nc, g.nc)
        def view(sx, sc, sy):
            if stage == 1: return o.at[sx, sc, :, sy, h]
            if stage == 2: return o.at[sx, sc, :, :, h] if kind == "x" else o.at[:, sc, :, sy, h]
            return o.at[:, sc, :, :, h]
        if kind == "y": peer = g.dev(z, py, x, c); pv = view(x, c, py)
        elif kind == "x": peer = g.dev(z, y, px, c); pv = view(px, c, y)
        else: peer = g.dev(z, y, x, pc); pv = view(x, pc, y)
        mine = view(x, c, y)
        ref = pv if recv else mine
        i = (w, h, stage - 1, k)
        return pltpu.make_async_remote_copy(src_ref=ref, dst_ref=ref, send_sem=self.s1.at[i], recv_sem=self.r1.at[i], device_id=peer, device_id_type=MESH)

    def npeers(self, h, stage):
        g = self.geo
        if stage == 3: return g.nc - 1
        return g.ny - 1 if (stage == 1) == (h == 0) else g.nx - 1

    def send(self, w, h, stage):
        if stage == 0:
            self.local(w, h).start()
            for k in range(1, self.geo.nz):
                self.zcopy(w, h, k).start()
        else:
            for k in range(1, 1 + self.npeers(h, stage)):
                self.pair(w, h, stage, k, False).start()

    def recv(self, w, h, stage):
        if stage == 0:
            self.local(w, h).wait()
            for k in range(1, self.geo.nz):
                self.zrecv(w, h, k).wait_recv()
        else:
            for k in range(1, 1 + self.npeers(h, stage)):
                self.pair(w, h, stage, k, True).wait_recv()

    def start(self, w, h, stage):
        if stage > 0:
            self.recv(w, h, stage - 1)
        self.send(w, h, stage)

    def finish(self, w, h):
        self.recv(w, h, 3)

    def drain(self, w, h, stages=(0, 1, 2, 3)):
        for stage in stages:
            if stage == 0:
                for k in range(1, self.geo.nz):
                    self.zcopy(w, h, k).wait_send()
            else:
                for k in range(1, 1 + self.npeers(h, stage)):
                    self.pair(w, h, stage, k, False).wait_send()


def gather_sems(geo, W):
    m = max(geo.nx, geo.ny, geo.nc)
    D = pltpu.SemaphoreType.DMA
    return [D((W, 2)), D((W, 2, geo.nz)), D((W, 2, geo.nz)), D((W, 2, 3, m)), D((W, 2, 3, m))]

def gather_kernel(geo, W, *refs):
    shards, outs, sems = refs[:W], refs[W:2 * W], refs[2 * W:]
    barrier(geo)
    G = Gather(geo, shards, outs, sems)
    for t in range(W + 4):
        for stage in range(4):
            w = t - stage
            if 0 <= w < W:
                for h in range(2): G.start(w, h, stage)
        if t >= 4:
            for h in range(2): G.finish(t - 4, h)
    for w in range(W):
        for h in range(2): G.drain(w, h)

def gather(geo, shards, collective_id=0):
    W = len(shards)
    outs = [jax.ShapeDtypeStruct((geo.nx, geo.nc, geo.nz, geo.ny) + s.shape, s.dtype) for s in shards]
    A = pl.BlockSpec(memory_space=pl.ANY)
    return pl.pallas_call(
        functools.partial(gather_kernel, geo, W), out_shape=outs, in_specs=[A] * W, out_specs=[A] * W,
        scratch_shapes=gather_sems(geo, W),
        compiler_params=pltpu.CompilerParams(collective_id=collective_id, has_side_effects=True, vmem_limit_bytes=16 << 20),
    )(*shards)


class Scatter:

    def __init__(self, geo, grads, outs, bufs, sems, owns=None, own_sem=None):
        self.geo, self.grads, self.outs, self.bufs = geo, list(grads), outs, bufs
        self.ss, self.rs = sems
        self.owns, self.own_sem = owns or [None] * len(grads), own_sem
        self.z, self.y, self.x, self.c = geo.place()

    def copies(self, w, h, stage):
        g, q = self.geo, self.grads[w]
        b1, b2, b3, b4 = self.bufs[4 * w : 4 * w + 4]
        z, y, x, c = self.z, self.y, self.x, self.c
        pc, py, px = 1 - c, 1 - y, 1 - x
        if stage == 0:
            moves = [(q.at[:, pc, :, :, h], b1.at[h], g.dev(z, y, x, pc))]
        elif stage == 1 and h == 0:
            moves = [(b1.at[0, px, :, k], b2.at[0, k], g.dev(z, y, px, c)) for k in range(g.ny)]
        elif stage == 1:
            moves = [(b1.at[1, :, :, py], b2.at[1], g.dev(z, py, x, c))]
        elif stage == 2:
            moves = [(b2.at[h, py if h == 0 else px], b3.at[h], g.dev(z, py, x, c) if h == 0 else g.dev(z, y, px, c))]
        else:
            moves = []
            for k in range(1, g.nz):
                zt = lax.rem(z + k, g.nz)
                moves.append((b3.at[h, zt], b4.at[h, k - 1], g.dev(zt, y, x, c)))
        return [
            pltpu.make_async_remote_copy(src_ref=s, dst_ref=d, send_sem=self.ss.at[w, h, stage, i], recv_sem=self.rs.at[w, h, stage, i], device_id=p, device_id_type=MESH)
            for i, (s, d, p) in enumerate(moves)
        ]

    def own_copy(self, w, h):
        return pltpu.make_async_copy(self.grads[w].at[:, self.c, :, :, h], self.owns[w].at[h], self.own_sem.at[w, h])

    def add(self, w, h, stage):
        g, q = self.geo, self.grads[w]
        b1, b2, b3, b4 = self.bufs[4 * w : 4 * w + 4]
        z, y, x, c = self.z, self.y, self.x, self.c

        def into(ref, at, other):
            ref[at] = (ref[at].astype(F32) + other.astype(F32)).astype(ref.dtype)

        if stage == 0:
            def one(i, _):
                xx, zz, yy = i // (g.nz * g.ny), (i // g.ny) % g.nz, i % g.ny
                mine = q[xx, c, zz, yy, h] if self.owns[w] is None else self.owns[w][h, xx, zz, yy]
                into(b1, (h, xx, zz, yy), mine)
                return 0
            lax.fori_loop(0, g.nx * g.nz * g.ny, one, 0)
        elif stage == 1:
            def one(i, _):
                k, zz = i // g.nz, i % g.nz
                into(b2, (h, k, zz), b1[0, x, zz, k] if h == 0 else b1[1, k, zz, y])
                return 0
            lax.fori_loop(0, 2 * g.nz, one, 0)
        elif stage == 2:
            def one(i, _):
                into(b3, (h, i), b2[h, y if h == 0 else x, i])
                return 0
            lax.fori_loop(0, g.nz, one, 0)
        else:
            if g.nz <= 8:
                total = b3[h, z].astype(F32)
                for k in range(g.nz - 1):
                    total = total + b4[h, k].astype(F32)
            else:
                total = lax.fori_loop(0, g.nz - 1, lambda k, t: t + b4[h, k].astype(F32), b3[h, z].astype(F32))
            self.outs[w][h] = total

    def step(self, w, h, stage):
        if self.owns[w] is not None:
            if stage == 0:
                self.own_copy(w, h).start()
            elif stage == 1:
                self.own_copy(w, h).wait()
        if stage > 0:
            for cp in self.copies(w, h, stage - 1):
                cp.wait_recv()
            self.add(w, h, stage - 1)
        if stage < 4:
            for cp in self.copies(w, h, stage):
                cp.start()

    def drain(self, w, h, stages=(0, 1, 2, 3)):
        for stage in stages:
            for cp in self.copies(w, h, stage):
                cp.wait_send()


def scatter_bufs(geo, shapes):
    out = []
    for s in shapes:
        r, t, d = s.shape[-2], s.shape[-1], s.dtype
        out += [
            pltpu.VMEM((2, geo.nx, geo.nz, geo.ny, r, t), d), pltpu.VMEM((2, 2, geo.nz, r, t), d),
            pltpu.VMEM((2, geo.nz, r, t), d), pltpu.VMEM((2, geo.nz - 1, r, t), d),
        ]
    return out


def scatter_sems(geo, W):
    n = max(2, geo.nz - 1)
    return [pltpu.SemaphoreType.DMA((W, 2, 4, n)), pltpu.SemaphoreType.DMA((W, 2, 4, n))]


def scatter_kernel(geo, W, *refs):
    grads, outs, bufs, sems = refs[:W], refs[W : 2 * W], refs[2 * W : 6 * W], refs[6 * W :]
    barrier(geo)
    S = Scatter(geo, grads, outs, bufs, sems)
    for t in range(W + 4):
        for stage in range(5):
            w = t - stage
            if 0 <= w < W:
                for h in range(2):
                    S.step(w, h, stage)
    for w in range(W):
        for h in range(2):
            S.drain(w, h)


def scatter(geo, grads, collective_id):
    W = len(grads)
    V = pl.BlockSpec(memory_space=pltpu.VMEM)
    return pl.pallas_call(
        functools.partial(scatter_kernel, geo, W),
        out_shape=[jax.ShapeDtypeStruct(g.shape[4:], F32) for g in grads],
        in_specs=[V] * W, out_specs=[V] * W,
        scratch_shapes=scatter_bufs(geo, grads) + scatter_sems(geo, W),
        compiler_params=pltpu.CompilerParams(collective_id=collective_id, has_side_effects=True, vmem_limit_bytes=60 << 20),
        name="scatter",
    )(*grads)


def nn(a, b):
    return lax.dot_general(a, b, (((1,), (0,)), ((), ())), preferred_element_type=F32)


def nt(a, b):
    return lax.dot_general(a, b, (((1,), (1,)), ((), ())), preferred_element_type=F32)


def tn(a, b):
    return lax.dot_general(a, b, (((0,), (0,)), ((), ())), preferred_element_type=F32)


def vm():
    return pl.BlockSpec(memory_space=pltpu.VMEM)


def sm():
    return pl.BlockSpec(memory_space=pltpu.SMEM)


def ends_of(len_ref):
    total, starts, ends = jnp.int32(0), [], []
    for t in range(len_ref.shape[1]):
        starts.append(total)
        total = total + len_ref[0, t]
        ends.append(total)
    return starts, ends


def segment(pos, ends):
    seg = jnp.zeros_like(pos)
    for e in ends:
        seg = seg + (pos >= e).astype(jnp.int32)
    return jnp.where(pos < ends[-1], seg, len(ends) + pos)


def opens(pos, starts, ends):
    hit = jnp.zeros_like(pos)
    for s in starts:
        hit = jnp.where(pos == s, 1, hit)
    return jnp.where(pos < ends[-1], hit, 0)


def lane_half(rows, which):
    lane = lax.broadcasted_iota(jnp.int32, (rows, 128), 1)
    return (lane < 64) if which == 0 else (lane >= 64)


def only(x, which):
    return jnp.where(lane_half(x.shape[0], which), x, jnp.zeros_like(x))


def masks(len_ref, r0, R, J):
    starts, ends = ends_of(len_ref)
    row = lax.broadcasted_iota(jnp.int32, (R, 1), 0) + r0
    col = lax.broadcasted_iota(jnp.int32, (1, J), 1)
    same = segment(row, ends) == segment(col, ends)
    allow = same & (col <= row)
    pick = same & (col < row) & (opens(col, starts, ends) == 0)
    return allow, pick


def ln_stats(x):
    center = x - jnp.mean(x, axis=-1, keepdims=True)
    spread = jnp.mean(center * center, axis=-1, keepdims=True)
    r = lax.rsqrt(spread + EPS)
    return center * r, r


def ln_back(g_h, n, r, gain):
    g_n = g_h * gain
    return r * (g_n - jnp.mean(g_n, axis=-1, keepdims=True) - n * jnp.mean(g_n * n, axis=-1, keepdims=True))


def unpack_cols(blk_ref, full_ref):
    n, _, w = blk_ref.shape
    for f in range(n):
        full_ref[:, f * w : (f + 1) * w] = blk_ref[f]


def qkv_kernel(x_ref, par_ref, w_ref, h1_ref, q_ref, k_ref, v_ref, wf):
    unpack_cols(w_ref, wf)
    D = x_ref.shape[1]
    R = 256
    for b in range(x_ref.shape[0] // R):
        rows = pl.ds(b * R, R)
        n, _ = ln_stats(x_ref[rows, :].astype(F32))
        h1 = (n * par_ref[0:1, :] + par_ref[1:2, :]).astype(BF16)
        h1_ref[rows, :] = h1
        q = (nn(h1, wf[:, 0:D]) + par_ref[4:5, :]).astype(BF16)
        q_ref[rows, :] = q * jnp.asarray(0.125, BF16)
        k_ref[rows, :] = nn(h1, wf[:, D : 2 * D]).astype(BF16)
        v_ref[rows, :] = (nn(h1, wf[:, 2 * D : 3 * D]) + par_ref[5:6, :]).astype(BF16)


def qkv(x, par, w):
    s = jax.ShapeDtypeStruct(x.shape, BF16)
    return pl.pallas_call(
        qkv_kernel, out_shape=[s] * 4, in_specs=[vm()] * 3, out_specs=[vm()] * 4,
        scratch_shapes=[pltpu.VMEM((w.shape[1], w.shape[0] * w.shape[2]), BF16)],
        compiler_params=pltpu.CompilerParams(vmem_limit_bytes=VLIM),
        name="qkv",
    )(x, par, w)


def unpack_pairs(blk_ref, full_ref):
    n, w = blk_ref.shape[0], blk_ref.shape[3] // 2
    for f in range(n):
        for s in range(2):
            full_ref[:, s, :, f * w : (f + 1) * w] = blk_ref[f, :, :, s * w : (s + 1) * w]


def mlp_kernel(R, len_ref, x_ref, cot_ref, mix_ref, par_ref, upb_ref, wo_ref, wu_ref, wd_ref,
               out_ref, gmid_ref, gmix_ref, small_ref, gub_ref, dwo_ref, dwu_ref, dwd_ref,
               wo, wd, act, gin, h2s, gbs):
    T, D = x_ref.shape
    FF = upb_ref.shape[1]
    nf, wf = wu_ref.shape[0], wu_ref.shape[2]
    unpack_cols(wo_ref, wo)
    unpack_pairs(wd_ref, wd)
    _, ends = ends_of(len_ref)
    small_ref[...] = jnp.zeros_like(small_ref)
    gub_ref[...] = jnp.zeros_like(gub_ref)
    cpf = wd.shape[0] // nf
    C0, C1 = 0.7978845608028654, 0.044715

    def block(b, _):
        rows = pl.ds(pl.multiple_of(b * R, R), R)
        x = x_ref[rows, :].astype(F32)
        middle = x + nn(mix_ref[rows, :], wo[...]) + par_ref[6:7, :]
        n2, r2 = ln_stats(middle)
        h2 = (n2 * par_ref[2:3, :] + par_ref[3:4, :]).astype(BF16)
        h2s[rows, :] = h2
        pos = lax.broadcasted_iota(jnp.int32, (R, 1), 0) + b * R
        live = pos < ends[-1]
        gb = jnp.where(live, cot_ref[rows, :].astype(F32), 0.0)
        gbl = gb.astype(BF16)
        gbs[rows, :] = gbl
        branch = jnp.zeros((R, D), F32)
        g_h2 = jnp.zeros((R, D), F32)
        for f in range(nf):
            cols = pl.ds(f * wf, wf)
            wdf = wd[f * cpf : (f + 1) * cpf].reshape(wf, D)
            u = nn(h2, wu_ref[f]) + upb_ref[0:1, f * wf : (f + 1) * wf]
            g_act = nt(gbl, wdf)
            u2 = u * u
            t = jnp.tanh(u * (C0 + (C0 * C1) * u2))
            hp = 0.5 + 0.5 * t
            a = u * hp
            al = a.astype(BF16)
            act[rows, cols] = al
            branch = branch + nn(al, wdf)
            d = hp + (a - a * hp) * (2.0 * C0 + (6.0 * C0 * C1) * u2)
            gi = (g_act * d).astype(BF16)
            gin[rows, cols] = gi
            gub_ref[0:1, f * wf : (f + 1) * wf] += jnp.sum(gi.astype(F32), axis=0, keepdims=True)
            g_h2 = g_h2 + nt(gi, wu_ref[f])
        out_ref[rows, :] = jnp.where(live, middle + branch + par_ref[7:8, :], 0.0).astype(BF16)
        small_ref[2:3, :] += jnp.sum(g_h2 * n2, axis=0, keepdims=True)
        small_ref[3:4, :] += jnp.sum(g_h2, axis=0, keepdims=True)
        g_mid = gb + ln_back(g_h2, n2, r2, par_ref[2:3, :])
        gmid_ref[rows, :] = g_mid
        gml = g_mid.astype(BF16)
        small_ref[6:7, :] += jnp.sum(gml.astype(F32), axis=0, keepdims=True)
        small_ref[7:8, :] += jnp.sum(gb, axis=0, keepdims=True)
        gmix_ref[rows, :] = nt(gml, wo[...]).astype(BF16)
        return 0

    lax.fori_loop(0, T // R, block, 0)
    w4 = D // nf

    def put(ref, grad, lead):
        r = ref.shape[2]
        c = grad.shape[0] // (2 * r)
        g = grad.astype(BF16).reshape(c, 2, r, D)
        for f in range(nf):
            for s in range(2):
                ref[f, pl.ds(lead, c), :, s * w4 : (s + 1) * w4] = g[:, s, :, f * w4 : (f + 1) * w4]

    def outp(i, _):
        g = tn(mix_ref[:, pl.ds(pl.multiple_of(i * 384, 128), 384)], gmid_ref[...].astype(BF16)).astype(BF16)
        for f in range(nf):
            dwo_ref[f, pl.ds(pl.multiple_of(i * 384, 128), 384), :] = g[:, f * w4 : (f + 1) * w4]
        return 0

    lax.fori_loop(0, D // 384, outp, 0)
    K = 384
    cpk = K // (2 * dwd_ref.shape[2])

    def down(i, _):
        put(dwd_ref, tn(act[:, pl.ds(pl.multiple_of(i * K, 128), K)], gbs[...]), i * cpk)
        return 0

    lax.fori_loop(0, FF // K, down, 0)
    H = 384

    def up(i, _):
        f, s = i // (wf // H), i % (wf // H)
        dwu_ref[f, :, pl.ds(pl.multiple_of(s * H, 128), H)] = tn(h2s[...], gin[:, pl.ds(pl.multiple_of(i * H, 128), H)]).astype(BF16)
        return 0

    lax.fori_loop(0, FF // H, up, 0)


def mlp(lengths, x, cot, mixed, par, upb, wo, wu, wd, R=256):
    T, D = x.shape
    FF = upb.shape[1]
    S = jax.ShapeDtypeStruct
    V = pltpu.VMEM
    return pl.pallas_call(
        functools.partial(mlp_kernel, R),
        out_shape=[S((T, D), BF16), S((T, D), F32), S((T, D), BF16), S((8, D), F32), S((8, FF), F32),
                   S(wo.shape, BF16), S(wu.shape, BF16), S(wd.shape, BF16)],
        in_specs=[sm()] + [vm()] * 8, out_specs=[vm()] * 8,
        scratch_shapes=[V((D, D), BF16), V((wd.shape[1], 2, wd.shape[2], D), BF16),
                        V((T, FF), BF16), V((T, FF), BF16), V((T, D), BF16), V((T, D), BF16)],
        compiler_params=pltpu.CompilerParams(vmem_limit_bytes=VLIM),
        name="mlp",
    )(lengths, x, cot, mixed, par, upb, wo, wu, wd)


def qkv_back_kernel(x_ref, h1_ref, gp_ref, gmid_ref, par_ref, w_ref, ig_ref, small_ref, dw_ref):
    T, D = x_ref.shape
    n, _, w = w_ref.shape
    R = 256
    for f in range(n):
        dw_ref[f] = tn(h1_ref[...], gp_ref[:, f * w : (f + 1) * w]).astype(BF16)
    small_ref[...] = jnp.zeros_like(small_ref)
    for b in range(T // R):
        rows = pl.ds(b * R, R)
        g_h1 = jnp.zeros((R, D), F32)
        for f in range(n):
            g_h1 = g_h1 + nt(gp_ref[rows, f * w : (f + 1) * w], w_ref[f])
        n1, r1 = ln_stats(x_ref[rows, :].astype(F32))
        small_ref[0:1, :] += jnp.sum(g_h1 * n1, axis=0, keepdims=True)
        small_ref[1:2, :] += jnp.sum(g_h1, axis=0, keepdims=True)
        small_ref[4:5, :] += jnp.sum(gp_ref[rows, 0:D].astype(F32), axis=0, keepdims=True)
        small_ref[5:6, :] += jnp.sum(gp_ref[rows, 2 * D : 3 * D].astype(F32), axis=0, keepdims=True)
        ig_ref[rows, :] = (gmid_ref[rows, :] + ln_back(g_h1, n1, r1, par_ref[0:1, :])).astype(BF16)


def qkv_back(x, h1, gp, gmid, par, w):
    S = jax.ShapeDtypeStruct
    return pl.pallas_call(
        qkv_back_kernel, out_shape=[S(x.shape, BF16), S((8, x.shape[1]), F32), S(w.shape, BF16)],
        in_specs=[vm()] * 6, out_specs=[vm()] * 3,
        compiler_params=pltpu.CompilerParams(vmem_limit_bytes=VLIM),
        name="qkv_back",
    )(x, h1, gp, gmid, par, w)


def masks_t(len_ref, r0, R, J):
    starts, ends = ends_of(len_ref)
    key = lax.broadcasted_iota(jnp.int32, (J, 1), 0)
    row = lax.broadcasted_iota(jnp.int32, (1, R), 1) + r0
    same = segment(key, ends) == segment(row, ends)
    return same & (key < row) & (opens(key, starts, ends) == 0)


def carried_scores(len_ref, q_ref, k_ref, cm, cmT_ref, carry):
    T = q_ref.shape[0]
    carry[...] = jnp.zeros_like(carry)
    i = lax.broadcasted_iota(jnp.int32, (B, B), 0)
    j = lax.broadcasted_iota(jnp.int32, (B, B), 1)
    lower = jnp.where(j < i, 1.0, 0.0).astype(BF16)
    for b in range(T // B):
        r0, J = b * B, (b + 1) * B
        rows = pl.ds(r0, B)
        allow, pick = masks(len_ref, r0, B, J)
        s0 = jnp.maximum(nt(only(q_ref[rows, 0:128], 0), k_ref[0:J, 0:128]), 0.0)
        chosen = jnp.where(pick, s0 * s0, 0.0)
        hi = chosen.astype(BF16)
        lo = (chosen - hi.astype(F32)).astype(BF16)
        carried = carry[0:1, 0:J] + (nn(lower, hi) + nn(lower, lo))
        c = jnp.where(allow, carried, BIG)
        cm[rows, 0:J] = c
        cmT_ref[0:J, rows] = jnp.transpose(c)
        carry[0:1, 0:J] = carry[0:1, 0:J] + jnp.sum(chosen, axis=0, keepdims=True)


def fwd_pair(p, q_ref, k_ref, v_ref, o_ref, lse, cm, s_sc, p_sc, C):
    T = q_ref.shape[0]
    lane = lax.broadcasted_iota(jnp.int32, (C, 128), 1)
    cols = pl.ds(pl.multiple_of(p * 128, 128), 128)
    k2, v2 = k_ref[:, cols], v_ref[:, cols]
    for half in range(2):
        q2 = only(q_ref[:, cols], half)
        for kb in range(T // B):
            s_sc[half, kb * B :, kb * B : (kb + 1) * B] = nt(q2[kb * B :], k2[kb * B : (kb + 1) * B])
    for rb in range(T // C):
        J = ((rb * C) // B + 1) * B
        rows = slice(rb * C, (rb + 1) * C)
        inv = []
        for half in range(2):
            l = s_sc[half, rows, :J] - cm[rows, :J]
            m = jnp.max(l, axis=1, keepdims=True)
            e = jnp.exp(l - m)
            t = jnp.sum(e, axis=1, keepdims=True)
            p_sc[half, rows, :J] = (e * (1.0 / t)).astype(BF16)
            lse[rows, :] = jnp.where(lane == 2 * p + half, m + jnp.log(t), lse[rows, :])
        if (rb * C) % B == B - C:
            b0 = (rb * C) // B * B
            o = [nn(p_sc[half, b0 : b0 + B, :J], v2[:J]) for half in range(2)]
            lanes = lax.broadcasted_iota(jnp.int32, (B, 128), 1)
            o_ref[b0 : b0 + B, cols] = jnp.where(lanes < 64, o[0], o[1]).astype(BF16)


def attn_fwd_kernel(C, len_ref, q_ref, k_ref, v_ref, o_ref, lseT_ref, cmT_ref, cm, lse, s_sc, p_sc, carry):
    carried_scores(len_ref, q_ref, k_ref, cm, cmT_ref, carry)

    def pair(p, _):
        fwd_pair(p, q_ref, k_ref, v_ref, o_ref, lse, cm, s_sc, p_sc, C)
        return 0

    lax.fori_loop(0, HEADS // 2, pair, 0)
    lseT_ref[...] = jnp.transpose(lse[...])[0:16]


def attn_fwd(lengths, q, k, v, C=64):
    T = q.shape[0]
    V = pltpu.VMEM
    return pl.pallas_call(
        functools.partial(attn_fwd_kernel, C),
        out_shape=[jax.ShapeDtypeStruct(q.shape, BF16), jax.ShapeDtypeStruct((16, T), F32), jax.ShapeDtypeStruct((T, T), F32)],
        in_specs=[sm()] + [vm()] * 3, out_specs=[vm()] * 3,
        scratch_shapes=[V((T, T), F32), V((T, 128), F32), V((2, T, T), F32), V((2, T, T), BF16), V((8, T), F32)],
        compiler_params=pltpu.CompilerParams(vmem_limit_bytes=VLIM),
        name="attn_fwd",
    )(lengths, q, k, v)


def row_sums(do_ref, o_ref, DT):
    T, D = do_ref.shape
    f = lax.broadcasted_iota(jnp.int32, (D, 128), 0)
    h = lax.broadcasted_iota(jnp.int32, (D, 128), 1)
    E = jnp.where((f >= h * 64) & (f < h * 64 + 64), 1.0, 0.0).astype(BF16)
    for b in range(T // B):
        rows = pl.ds(b * B, B)
        x = do_ref[rows, :].astype(F32) * o_ref[rows, :].astype(F32)
        hi = x.astype(BF16)
        lo = (x - hi.astype(F32)).astype(BF16)
        DT[:, rows] = jnp.transpose(nn(hi, E) + nn(lo, E))[0:16]


def bwd_scores(p, half, q_ref, k_ref, v_ref, do_ref, sT, dpT):
    T = q_ref.shape[0]
    cols = p * 128 if isinstance(p, int) else pl.multiple_of(p * 128, 128)
    c = pl.ds(cols, 128)
    k2, v2 = k_ref[:, c], v_ref[:, c]
    q2, do2 = only(q_ref[:, c], half), only(do_ref[:, c], half)
    for rb in range(T // B):
        J, r = (rb + 1) * B, slice(rb * B, (rb + 1) * B)
        sT[0:J, r] = nt(k2[0:J], q2[r])
        dpT[0:J, r] = nt(v2[0:J], do2[r])


def bwd_softmax(h, sT, dpT, pT, dsT, lseT, DT, cmT, C, add_into=None, keep=None):
    T = sT.shape[0]
    for kc in range(T // C):
        i0 = (kc * C) // B * B
        keys = slice(kc * C, (kc + 1) * C)
        pr = jnp.exp(sT[keys, i0:] - cmT[keys, i0:] - lseT[pl.ds(h, 1), i0:])
        ds = pr * (dpT[keys, i0:] - DT[pl.ds(h, 1), i0:])
        pT[keys, i0:] = pr.astype(BF16)
        if keep is not None:
            keep[keys, i0:] = ds
        else:
            dsT[keys, i0:] = ds.astype(BF16)
        add_into[keys, i0:] += ds


def bwd_products(p, half, q_ref, k_ref, do_ref, pT, dsT, gp_ref, dk, dv, first):
    T, D = q_ref.shape
    cols = p * 128 if isinstance(p, int) else pl.multiple_of(p * 128, 128)
    c = pl.ds(cols, 128)
    k2 = k_ref[:, c]
    q2, do2 = only(q_ref[:, c], half), only(do_ref[:, c], half)
    for kb in range(T // B):
        keys = slice(kb * B, (kb + 1) * B)
        a = nn(pT[keys, kb * B :], do2[kb * B :])
        d = nn(dsT[keys, kb * B :], q2[kb * B :])
        if first:
            dv[keys, :], dk[keys, :] = a, d
        else:
            dv[keys, :] += a
            dk[keys, :] += d
    lanes = lax.broadcasted_iota(jnp.int32, (B, 128), 1)
    for rb in range(T // B):
        J, r = (rb + 1) * B, slice(rb * B, (rb + 1) * B)
        dq = (tn(dsT[0:J, r], k2[0:J]) * 0.125).astype(BF16)
        if first:
            gp_ref[r, c] = dq
        else:
            gp_ref[r, c] = jnp.where((lanes < 64) == (half == 0), dq, gp_ref[r, c])


def first_head(len_ref, sT, ds0, dsT, G):
    T = sT.shape[0]
    i = lax.broadcasted_iota(jnp.int32, (B, B), 0)
    j = lax.broadcasted_iota(jnp.int32, (B, B), 1)
    after = jnp.where(i > j, 1.0, 0.0).astype(BF16)
    later = jnp.zeros((T, 1), F32)
    for rb in reversed(range(T // B)):
        J, r = (rb + 1) * B, slice(rb * B, (rb + 1) * B)
        g = -G[0:J, r]
        hi = g.astype(BF16)
        lo = (g - hi.astype(F32)).astype(BF16)
        g_chosen = later[0:J] + (nn(hi, after) + nn(lo, after))
        later = later[0:J] + jnp.sum(g, axis=1, keepdims=True)
        pick = masks_t(len_ref, rb * B, B, J)
        full = ds0[0:J, r] + jnp.where(pick, 2.0 * jnp.maximum(sT[0:J, r], 0.0) * g_chosen, 0.0)
        dsT[0:J, r] = full.astype(BF16)


def attn_bwd_kernel(C, len_ref, q_ref, k_ref, v_ref, do_ref, o_ref, lseT, cmT, gp_ref, DT, sT, dpT, pT, dsT, G, dk, dv):
    T, D = q_ref.shape
    row_sums(do_ref, o_ref, DT)
    G[...] = jnp.zeros_like(G)

    def put(p):
        ck = D + p * 128 if isinstance(p, int) else pl.multiple_of(D + p * 128, 128)
        cv = 2 * D + p * 128 if isinstance(p, int) else pl.multiple_of(2 * D + p * 128, 128)
        gp_ref[:, pl.ds(ck, 128)] = dk[...].astype(BF16)
        gp_ref[:, pl.ds(cv, 128)] = dv[...].astype(BF16)

    def pair(k, _):
        p = HEADS // 2 - 1 - k
        for half in range(2):
            bwd_scores(p, half, q_ref, k_ref, v_ref, do_ref, sT.at[half], dpT.at[half])
        for half in range(2):
            bwd_softmax(2 * p + half, sT.at[half], dpT.at[half], pT.at[half], dsT.at[half], lseT, DT, cmT, C, G)
        for half in range(2):
            bwd_products(p, half, q_ref, k_ref, do_ref, pT.at[half], dsT.at[half], gp_ref, dk, dv, half == 0)
        put(p)
        return 0

    lax.fori_loop(0, HEADS // 2 - 1, pair, 0)
    bwd_scores(0, 1, q_ref, k_ref, v_ref, do_ref, sT.at[1], dpT.at[1])
    bwd_softmax(1, sT.at[1], dpT.at[1], pT.at[1], dsT.at[1], lseT, DT, cmT, C, G)
    bwd_products(0, 1, q_ref, k_ref, do_ref, pT.at[1], dsT.at[1], gp_ref, dk, dv, True)
    bwd_scores(0, 0, q_ref, k_ref, v_ref, do_ref, sT.at[0], dpT.at[0])
    bwd_softmax(0, sT.at[0], dpT.at[0], pT.at[0], dsT.at[0], lseT, DT, cmT, C, G, keep=dpT.at[0])
    first_head(len_ref, sT.at[0], dpT.at[0], dsT.at[0], G)
    bwd_products(0, 0, q_ref, k_ref, do_ref, pT.at[0], dsT.at[0], gp_ref, dk, dv, False)
    put(0)


def attn_bwd(lengths, q, k, v, do, o, lseT, cmT, C=64):
    T, D = q.shape
    V = pltpu.VMEM
    return pl.pallas_call(
        functools.partial(attn_bwd_kernel, C),
        out_shape=jax.ShapeDtypeStruct((T, 3 * D), BF16),
        in_specs=[sm()] + [vm()] * 7, out_specs=vm(),
        scratch_shapes=[V((16, T), F32), V((2, T, T), F32), V((2, T, T), F32), V((2, T, T), BF16), V((2, T, T), BF16), V((T, T), F32), V((T, 128), F32), V((T, 128), F32)],
        compiler_params=pltpu.CompilerParams(vmem_limit_bytes=VLIM),
        name="attn_bwd",
    )(lengths, q, k, v, do, o, lseT, cmT)


def fold_tiny(tiny, par, per, n_dp, F):
    for f in range(F):
        for d in range(n_dp):
            for s in range(2):
                par[s * F + f : s * F + f + 1, d * per : (d + 1) * per] = tiny[f, d, 0, s : s + 1, 0:per].astype(F32)
            par[2 * F + f : 2 * F + f + 1, d * per : (d + 1) * per] = tiny[f, d, 1, 0:1, 0:per].astype(F32)


def front_kernel(geo, C, *refs):
    len_ref, x_ref = refs[0:2]
    shards, bufs = refs[2:7], refs[7:12]
    h1_o, q_o, k_o, v_o, mix_o, lseT_o, cmT_o, par = refs[12:20]
    tiny_v, wq_v, wf, h1, q, k, v, mix, cmT, cm, lse, s_sc, p_sc, carry, lsem, osem = refs[20:36]
    sems = refs[36:]
    T, D = x_ref.shape
    F, per = geo.n_fs, D // geo.n_dp
    barrier(geo)
    G = Gather(geo, shards, bufs, sems)

    def ev(*items):
        for w, stage in items:
            for h in range(2):
                if stage == 4:
                    G.finish(w, h)
                else:
                    G.start(w, h, stage)

    ev((0, 0), (1, 0), (2, 0))
    for b in range(T // B):
        rows = pl.ds(b * B, B)
        n, _ = ln_stats(x_ref[rows, :].astype(F32))
        s_sc[0, rows, 0:D] = n
    ev((0, 1), (1, 1), (3, 0), (0, 2), (1, 2), (2, 1), (0, 3), (1, 3), (2, 2), (4, 0), (3, 1), (0, 4), (1, 4))
    get_t = pltpu.make_async_copy(bufs[0], tiny_v, lsem.at[0])
    get_q = pltpu.make_async_copy(bufs[1], wq_v, lsem.at[1])
    get_t.start()
    get_q.start()
    get_t.wait()
    par[...] = jnp.zeros_like(par)
    fold_tiny(tiny_v.reshape(F, geo.n_dp, 2, 16, 128), par, per, geo.n_dp, F)
    get_q.wait()
    unpack_cols(wq_v.reshape(F, D, wq_v.shape[-1]), wf)
    outs = [pltpu.make_async_copy(a, b, osem.at[i]) for i, (a, b) in enumerate(((h1, h1_o), (q, q_o), (k, k_o), (v, v_o), (cmT, cmT_o), (mix, mix_o), (lse, lse))[:6])]
    for b in range(T // B):
        rows = pl.ds(b * B, B)
        hb = (s_sc[0, rows, 0:D] * par[0:1, :] + par[1:2, :]).astype(BF16)
        h1[rows, :] = hb
        q[rows, :] = (nn(hb, wf[:, 0:D]) + par[4:5, :]).astype(BF16) * jnp.asarray(0.125, BF16)
        k[rows, :] = nn(hb, wf[:, D : 2 * D]).astype(BF16)
        v[rows, :] = (nn(hb, wf[:, 2 * D : 3 * D]) + par[5:6, :]).astype(BF16)
        if b == 1:
            ev((2, 3), (3, 2))
    for i in range(4):
        outs[i].start()
    ev((4, 1))
    carried_scores(len_ref, q, k, cm, cmT, carry)
    outs[4].start()
    plan = {1: ((3, 3),)}

    def pair(p, _):
        for at, items in plan.items():
            @pl.when(p == at)
            def _():
                ev(*items)
        fwd_pair(p, q, k, v, mix, lse, cm, s_sc, p_sc, C)
        return 0

    lax.fori_loop(0, HEADS // 2, pair, 0)
    outs[5].start()
    lseT_o[...] = jnp.transpose(lse[...])[0:16]
    ev((2, 4), (3, 4))
    for h in range(2):
        G.recv(4, h, 1)
    for w in range(5):
        for h in range(2):
            G.drain(w, h, (0, 1) if w == 4 else (0, 1, 2, 3))
    for i in range(6):
        outs[i].wait()


def front(geo, lengths, x, shards, collective_id=0, C=64):
    T, D = x.shape
    V, S, A = pltpu.VMEM, jax.ShapeDtypeStruct, pl.BlockSpec(memory_space=pl.ANY)
    lead = (geo.nx, geo.nc, geo.nz, geo.ny)
    tok = S((T, D), BF16)
    res = pl.pallas_call(
        functools.partial(front_kernel, geo, C),
        out_shape=[S(lead + s.shape, s.dtype) for s in shards] + [tok] * 5 + [S((16, T), F32), S((T, T), F32), S((16, D), F32)],
        in_specs=[sm(), vm()] + [vm()] * 5,
        out_specs=[A] * 10 + [vm(), A, vm()],
        scratch_shapes=[V(lead + shards[0].shape, BF16), V(lead + shards[1].shape, BF16), V((D, 3 * D), BF16)]
        + [V((T, D), BF16)] * 5 + [V((T, T), F32), V((T, T), F32), V((T, 128), F32), V((2, T, T), F32), V((2, T, T), BF16), V((8, T), F32)]
        + [pltpu.SemaphoreType.DMA((2,)), pltpu.SemaphoreType.DMA((6,))] + gather_sems(geo, 5),
        compiler_params=pltpu.CompilerParams(collective_id=collective_id, has_side_effects=True, vmem_limit_bytes=VLIM),
        name="front",
    )(lengths, x, *shards)
    return res[:5], res[5:]


def repeats(w, n):
    r = lax.broadcasted_iota(jnp.int32, (w, n * w), 0)
    m = lax.broadcasted_iota(jnp.int32, (w, n * w), 1)
    return jnp.where((m >= n * r) & (m < n * r + n), 1.0, 0.0).astype(BF16)


def own_row(n, w):
    row = lax.broadcasted_iota(jnp.int32, (8, n * w), 0)
    m = lax.broadcasted_iota(jnp.int32, (8, n * w), 1)
    return row == lax.rem(m, n)


def weave(rows8, n, out_ref):
    w = rows8.shape[1] // n
    rep, own = repeats(w, n), own_row(n, w)
    for f in range(n):
        wide = nn(rows8[:, f * w : (f + 1) * w].astype(BF16), rep)
        line = jnp.sum(jnp.where(own, wide, 0.0), axis=0, keepdims=True)
        out_ref[:, f * n * w : (f + 1) * n * w] = jnp.broadcast_to(line, (8, n * w))


def unweave(line, n, out_ref):
    w = line.shape[1] // n // n
    rep, own = repeats(w, n), own_row(n, w)
    for f in range(n):
        wide = jnp.where(own, jnp.broadcast_to(line[:, f * n * w : (f + 1) * n * w], (8, n * w)), 0.0)
        hi = wide.astype(BF16)
        lo = (wide - hi.astype(F32)).astype(BF16)
        out_ref[:, f * w : (f + 1) * w] = nt(hi, rep) + nt(lo, rep)


def mid_kernel(geo, R, *refs):
    len_ref, par, x_h, cot_h, mix_h, wo_h, wu_h, half_h = refs[0:8]
    out_o, gmid_o, gmix_o, dwo_o, dwu_o, small, gub, part_o = refs[8:16]
    upb, X, C, M, wo_raw, wo, wu, land, wd, act, gin, h2s, gmid, gmix, dwo, dwu, dwd = refs[16:33]
    isem, osem, wsem = refs[33:36]
    bufs, ssems, gsems = refs[36:40], refs[40:42], refs[42:47]
    T, D = X.shape
    FF = act.shape[1]
    F = geo.n_fs
    wf, w4 = FF // F, D // F
    barrier(geo)
    G = Gather(geo, [None], [land], gsems)
    S = Scatter(geo, [dwd], [None], bufs, ssems)
    z, y, xx, c = geo.place()
    keep = [
        pltpu.make_async_copy(half_h.at[xx, c, :, :, 0], land.at[xx, c, :, :, 0], wsem.at[0]),
        pltpu.make_async_copy(half_h.at[:, c, :, y, 1], land.at[:, c, :, y, 1], wsem.at[1]),
    ]
    for cp in keep:
        cp.start()
    ins = [pltpu.make_async_copy(a, b, isem.at[i]) for i, (a, b) in enumerate(((wo_h, wo_raw), (x_h, X), (mix_h, M), (cot_h, C), (wu_h, wu)))]
    for cp in ins:
        cp.start()
    weave(par[8:16, :], F, upb)
    small[...] = jnp.zeros_like(small)
    gub[...] = jnp.zeros_like(gub)
    for cp in keep:
        cp.wait()
    for h in range(2):
        G.send(0, h, 2)
    _, ends = ends_of(len_ref)
    C0, C1 = 0.7978845608028654, 0.044715
    ins[0].wait()
    unpack_cols(wo_raw, wo)
    for cp in ins[1:]:
        cp.wait()

    def first(b, _):
        rows = pl.ds(pl.multiple_of(b * R, R), R)
        middle = X[rows, :].astype(F32) + nn(M[rows, :], wo[...]) + par[6:7, :]
        gmid[rows, :] = middle
        n2, _ = ln_stats(middle)
        h2 = (n2 * par[2:3, :] + par[3:4, :]).astype(BF16)
        h2s[rows, :] = h2
        pos = lax.broadcasted_iota(jnp.int32, (R, 1), 0) + b * R
        gb = jnp.where(pos < ends[-1], C[rows, :].astype(F32), 0.0)
        C[rows, :] = gb.astype(BF16)
        small[7:8, :] += jnp.sum(gb, axis=0, keepdims=True)
        for f in range(F):
            cols = slice(f * wf, (f + 1) * wf)
            u = nn(h2, wu[f]) + upb[0:1, cols]
            u2 = u * u
            t = jnp.tanh(u * (C0 + (C0 * C1) * u2))
            hp = 0.5 + 0.5 * t
            a = u * hp
            act[rows, cols] = a.astype(BF16)
            gin[rows, cols] = (hp + (a - a * hp) * (2.0 * C0 + (6.0 * C0 * C1) * u2)).astype(BF16)
        return 0

    lax.fori_loop(0, T // R, first, 0)
    for h in range(2):
        G.recv(0, h, 2)
        G.send(0, h, 3)

    r = dwd.shape[5]
    dv = dwd.reshape(F, 2 * geo.n_dp, r, 2 * w4)
    K = 768
    per = K // (2 * r)

    def down(i, _):
        g = tn(act[:, pl.ds(pl.multiple_of(i * K, 128), K)], C[...]).astype(BF16).reshape(per, 2, r, D)
        for f in range(F):
            for s in range(2):
                dv[f, pl.ds(i * per, per), :, s * w4 : (s + 1) * w4] = g[:, s, :, f * w4 : (f + 1) * w4]
        return 0

    lax.fori_loop(0, FF // K, down, 0)
    for h in range(2):
        S.step(0, h, 0)
    for h in range(2):
        G.recv(0, h, 3)
    lv = land.reshape(F, 2 * geo.n_dp, r, 2 * w4)
    for f in range(F):
        for s in range(2):
            wd[:, s, :, f * w4 : (f + 1) * w4] = lv[f, :, :, s * w4 : (s + 1) * w4]
    cpf = wd.shape[0] // F

    def second(b, _):
        rows = pl.ds(pl.multiple_of(b * R, R), R)
        pos = lax.broadcasted_iota(jnp.int32, (R, 1), 0) + b * R
        gbl = C[rows, :]
        branch = jnp.zeros((R, D), F32)
        g_h2 = jnp.zeros((R, D), F32)
        for f in range(F):
            cols = slice(f * wf, (f + 1) * wf)
            wdf = wd[f * cpf : (f + 1) * cpf].reshape(wf, D)
            branch = branch + nn(act[rows, cols], wdf)
            gi = (nt(gbl, wdf) * gin[rows, cols].astype(F32)).astype(BF16)
            gin[rows, cols] = gi
            gub[0:1, cols] += jnp.sum(gi.astype(F32), axis=0, keepdims=True)
            g_h2 = g_h2 + nt(gi, wu[f])
        middle = gmid[rows, :]
        X[rows, :] = jnp.where(pos < ends[-1], middle + branch + par[7:8, :], 0.0).astype(BF16)
        n2, r2 = ln_stats(middle)
        small[2:3, :] += jnp.sum(g_h2 * n2, axis=0, keepdims=True)
        small[3:4, :] += jnp.sum(g_h2, axis=0, keepdims=True)
        g_mid = gbl.astype(F32) + ln_back(g_h2, n2, r2, par[2:3, :])
        gmid[rows, :] = g_mid
        gml = g_mid.astype(BF16)
        small[6:7, :] += jnp.sum(gml.astype(F32), axis=0, keepdims=True)
        gmix[rows, :] = nt(gml, wo[...]).astype(BF16)
        return 0

    half = T // R // 2
    lax.fori_loop(0, half, second, 0)
    for h in range(2):
        S.step(0, h, 1)
    lax.fori_loop(half, T // R, second, 0)
    outs = [pltpu.make_async_copy(a, b, osem.at[i]) for i, (a, b) in enumerate(((X, out_o), (gmid, gmid_o), (gmix, gmix_o)))]
    for cp in outs:
        cp.start()
    o4 = dwo.reshape(F, D, w4)
    for i in range(2):
        g = tn(M[:, i * 384 : (i + 1) * 384], gmid[...].astype(BF16)).astype(BF16)
        for f in range(F):
            o4[f, i * 384 : (i + 1) * 384, :] = g[:, f * w4 : (f + 1) * w4]
    outs.append(pltpu.make_async_copy(dwo, dwo_o, osem.at[3]))
    outs[3].start()
    H = 256
    sent = []
    ov = dwu_o.reshape(F, D, wf)
    for f in range(F):
        if f >= 2:
            sent[f - 2].wait()

        def up(i, _):
            dwu[f % 2, :, pl.ds(pl.multiple_of(i * H, 128), H)] = tn(h2s[...], gin[:, pl.ds(pl.multiple_of(f * wf + i * H, 128), H)]).astype(BF16)
            return 0

        lax.fori_loop(0, wf // H, up, 0)
        sent.append(pltpu.make_async_copy(dwu.at[f % 2], ov.at[f], wsem.at[f % 2]))
        sent[f].start()
    for h in range(2):
        for cp in S.copies(0, h, 1):
            cp.wait_recv()
        S.add(0, h, 1)
    part_o[...] = bufs[1][...]
    for h in range(2):
        for stage in range(2):
            for cp in S.copies(0, h, stage):
                cp.wait_send()
        G.drain(0, h, (2, 3))
    for cp in outs + sent[-2:]:
        cp.wait()


def mid(geo, lengths, par, x, cot, mixed, wo, wu, half, collective_id=2, R=512):
    T, D = x.shape
    FF = wu.shape[0] * wu.shape[2]
    V, S, A, D_ = pltpu.VMEM, jax.ShapeDtypeStruct, pl.BlockSpec(memory_space=pl.ANY), pltpu.SemaphoreType.DMA
    lead = (geo.nx, geo.nc, geo.nz, geo.ny, 2)
    rr = D // geo.n_dp // 2
    tok = lambda: V((T, D), BF16)
    dwo, dwu = S(lead + (rr, wo.shape[2]), BF16), S(lead + (rr, wu.shape[2]), BF16)
    n = half.shape[5]
    return pl.pallas_call(
        functools.partial(mid_kernel, geo, R),
        out_shape=[S((T, D), BF16), S((T, D), F32), S((T, D), BF16), dwo, dwu, S((8, D), F32), S((8, FF), F32), S((2, 2, geo.nz) + half.shape[5:], BF16)],
        in_specs=[sm(), vm()] + [A] * 6,
        out_specs=[A] * 5 + [vm()] * 3,
        scratch_shapes=[V((8, FF), F32), tok(), tok(), tok(), V(wo.shape, BF16), V((D, D), BF16), V(wu.shape, BF16), V(half.shape, BF16),
                        V((2 * geo.n_dp, 2, n, D), BF16), V((T, FF), BF16), V((T, FF), BF16), tok(), V((T, D), F32), tok(), V(dwo.shape, BF16), V((2, D, wu.shape[2]), BF16), V(half.shape, BF16),
                        D_((5,)), D_((4,)), D_((2,))]
        + scatter_bufs(geo, [half]) + scatter_sems(geo, 1) + gather_sems(geo, 1),
        compiler_params=pltpu.CompilerParams(collective_id=collective_id, has_side_effects=True, vmem_limit_bytes=VLIM),
        name="mid",
    )(lengths, par, x, cot, mixed, wo, wu, half)


def spread_tiny(small, ub, tiny, per, n_dp, F):
    for f in range(F):
        for d in range(n_dp):
            for s in range(2):
                tiny[f, d, 0, s : s + 1, 0:per] = small[s * F + f : s * F + f + 1, d * per : (d + 1) * per]
            tiny[f, d, 1, 0:1, 0:per] = ub[f : f + 1, d * per : (d + 1) * per]


def back_kernel(geo, C, *refs):
    len_ref, lseT, part, small_b, gub, par = refs[0:6]
    q_h, k_h, v_h, do_h, o_h, cmT_h, x_h, h1_h, gmid_h, wq_h = refs[6:16]
    parts = refs[16:18]
    ig_o = refs[18]
    outs = refs[19:24]
    gp, DT, small, tiny, isem, osem, own_sem = refs[24:31]
    owns = [None] + list(refs[31:33]) + [None, None]
    bufs, sems = [None, part] + list(refs[33:51]), refs[51:53]
    D, T = gp.shape[1] // 3, gp.shape[0]
    F, n_dp = geo.n_fs, geo.n_dp
    per = D // n_dp
    barrier(geo)
    S = Scatter(geo, [None] + list(parts) + [None, tiny], outs, bufs, sems, owns, own_sem)
    DOWN, UP, OUT, QKV, TINY = range(5)

    def ev(*items):
        for w, stage in items:
            for h in range(2):
                S.step(w, h, stage)

    for h in range(2):
        for cp in S.copies(DOWN, h, 2):
            cp.start()
    ev((UP, 0), (OUT, 0))

    def attention(q, k, v, do, o, cmT, sT, dpT, pT, dsT, G, dk, dv):
        ins = [pltpu.make_async_copy(a, b, isem.at[i]) for i, (a, b) in enumerate(((do_h, do), (o_h, o), (q_h, q), (k_h, k), (v_h, v), (cmT_h, cmT)))]
        for cp in ins:
            cp.start()
        G[...] = jnp.zeros_like(G)
        ins[0].wait()
        ins[1].wait()
        row_sums(do, o, DT)
        for cp in ins[2:]:
            cp.wait()

        def put(p):
            ck = D + p * 128 if isinstance(p, int) else pl.multiple_of(D + p * 128, 128)
            cv = 2 * D + p * 128 if isinstance(p, int) else pl.multiple_of(2 * D + p * 128, 128)
            gp[:, pl.ds(ck, 128)] = dk[...].astype(BF16)
            gp[:, pl.ds(cv, 128)] = dv[...].astype(BF16)

        plan = {(0, 0): ((UP, 1),), (0, 1): ((OUT, 1),), (1, 1): ((DOWN, 3),), (3, 0): ((UP, 2),), (4, 0): ((OUT, 2), (DOWN, 4)), (4, 1): ((UP, 3),)}

        def pair(n, _):
            p = HEADS // 2 - 1 - n
            for half in range(2):
                for (at, hf), items in plan.items():
                    if hf == half:
                        @pl.when(n == at)
                        def _():
                            ev(*items)
                bwd_scores(p, half, q, k, v, do, sT, dpT)
                bwd_softmax(2 * p + half, sT, dpT, pT, dsT, lseT, DT, cmT, C, G)
                bwd_products(p, half, q, k, do, pT, dsT, gp, dk, dv, half == 0)
            put(p)
            return 0

        lax.fori_loop(0, HEADS // 2 - 1, pair, 0)
        bwd_scores(0, 1, q, k, v, do, sT, dpT)
        bwd_softmax(1, sT, dpT, pT, dsT, lseT, DT, cmT, C, G)
        bwd_products(0, 1, q, k, do, pT, dsT, gp, dk, dv, True)
        ev((OUT, 3))
        bwd_scores(0, 0, q, k, v, do, sT, dpT)
        bwd_softmax(0, sT, dpT, pT, dsT, lseT, DT, cmT, C, G, keep=dpT)
        first_head(len_ref, sT, dpT, dsT, G)
        bwd_products(0, 0, q, k, do, pT, dsT, gp, dk, dv, False)
        put(0)

    V = pltpu.VMEM
    pl.run_scoped(
        attention, *[V((T, D), BF16)] * 5, V((T, T), F32), V((T, T), F32), V((T, T), F32), V((T, T), BF16), V((T, T), BF16), V((T, T), F32),
        V((T, 128), F32), V((T, 128), F32),
    )

    def projections(x, h1, gmid, wq, dwq, ig, ub):
        ins = [pltpu.make_async_copy(a, b, isem.at[i]) for i, (a, b) in enumerate(((h1_h, h1), (wq_h, wq), (x_h, x), (gmid_h, gmid)))]
        for cp in ins:
            cp.start()
        n, _, w = wq.shape
        dw = dwq.reshape(n, D, w)
        ins[0].wait()
        for f in range(n):
            dw[f] = tn(h1[...], gp[:, f * w : (f + 1) * w]).astype(BF16)
            if f == 1:
                ev((UP, 4), (OUT, 4))
        S.grads[QKV] = dwq
        ev((QKV, 0))
        small[...] = small_b[...]
        for cp in ins[1:]:
            cp.wait()
        for b in range(T // B):
            rows = pl.ds(b * B, B)
            g_h1 = jnp.zeros((B, D), F32)
            for f in range(n):
                g_h1 = g_h1 + nt(gp[rows, f * w : (f + 1) * w], wq[f])
            n1, r1 = ln_stats(x[rows, :].astype(F32))
            small[0:1, :] += jnp.sum(g_h1 * n1, axis=0, keepdims=True)
            small[1:2, :] += jnp.sum(g_h1, axis=0, keepdims=True)
            small[4:5, :] += jnp.sum(gp[rows, 0:D].astype(F32), axis=0, keepdims=True)
            small[5:6, :] += jnp.sum(gp[rows, 2 * D : 3 * D].astype(F32), axis=0, keepdims=True)
            ig[rows, :] = (gmid[rows, :] + ln_back(g_h1, n1, r1, par[0:1, :])).astype(BF16)
            if b == 1:
                ev((QKV, 1))
        out_cp = pltpu.make_async_copy(ig, ig_o, osem)
        out_cp.start()
        tiny[...] = jnp.zeros_like(tiny)
        unweave(gub[0:1, :], F, ub)
        spread_tiny(small, ub, tiny.reshape(F, n_dp, 2, 8, 128), per, n_dp, F)
        ev((TINY, 0), (TINY, 1), (QKV, 2), (TINY, 2), (TINY, 3), (QKV, 3), (TINY, 4), (QKV, 4))
        for wt in range(5):
            for h in range(2):
                S.drain(wt, h, (2, 3) if wt == DOWN else (0, 1, 2, 3))
        out_cp.wait()

    pl.run_scoped(projections, V((T, D), BF16), V((T, D), BF16), V((T, D), F32), V(wq_h.shape, BF16), V((geo.nx, geo.nc, geo.nz, geo.ny, 2, per // 2, wq_h.shape[-1]), BF16), V((T, D), BF16), V((8, D), F32))


def back(geo, lengths, lseT, part, small_b, gub, par, q, k, v, do, o, cmT, x, h1, gmid, wq, parts, collective_id=1, C=64):
    T, D = x.shape
    V, S, A, D_ = pltpu.VMEM, jax.ShapeDtypeStruct, pl.BlockSpec(memory_space=pl.ANY), pltpu.SemaphoreType.DMA
    per = D // geo.n_dp
    dwq = S((geo.nx, geo.nc, geo.nz, geo.ny, 2, per // 2, wq.shape[-1]), BF16)
    tiny = S((geo.nx, geo.nc, geo.nz, geo.ny, 2, 8, 128), F32)
    down = S((geo.nx, geo.nc, geo.nz, geo.ny, 2) + part.shape[3:], BF16)
    grads = [down] + list(parts) + [dwq, tiny]
    owns = [V((2, geo.nx, geo.nz, geo.ny) + g.shape[5:], BF16) for g in parts]
    return pl.pallas_call(
        functools.partial(back_kernel, geo, C),
        out_shape=[S((T, D), BF16)] + [S(g.shape[4:], F32) for g in grads],
        in_specs=[sm()] + [vm()] * 5 + [A] * 12,
        out_specs=[A] + [vm()] * 5,
        scratch_shapes=[V((T, 3 * D), BF16), V((16, T), F32), V((8, D), F32), V(tiny.shape, F32), D_((6,)), D_, D_((5, 2))]
        + owns + scatter_bufs(geo, grads)[2:] + scatter_sems(geo, 5),
        compiler_params=pltpu.CompilerParams(collective_id=collective_id, has_side_effects=True, vmem_limit_bytes=VLIM),
        name="back",
    )(lengths, lseT, part, small_b, gub, par, q, k, v, do, o, cmT, x, h1, gmid, wq, *parts)


def pair_up(shard):
    w = shard.shape[1]
    return shard.reshape(2, 2, -1, w).transpose(0, 2, 1, 3).reshape(2, -1, 2 * w)


def pair_down(halves):
    w = halves.shape[2] // 2
    return halves.reshape(2, -1, 2, w).transpose(0, 2, 1, 3).reshape(-1, w)


def repair(blocks, r):
    n, c, r0, w2 = blocks.shape
    if r0 == r:
        return blocks
    w = w2 // 2
    flat = blocks.reshape(n, c, r0, 2, w).transpose(0, 1, 3, 2, 4).reshape(n, -1, 2, r, w)
    return flat.transpose(0, 1, 3, 2, 4).reshape(n, -1, r, w2)


def body(geo, tokens, cotangent, lengths, norm_params, bias_params, w_qkv, w_out, w_up, up_bias, w_down):
    T, D = tokens.shape
    F, n_dp, per = geo.n_fs, geo.n_dp, D // geo.n_dp
    FF = D * F * up_bias.shape[1]
    fused = (per // 2) % 16 == 0
    tiny = jnp.stack([jnp.stack([norm_params[:, 0], bias_params[:, 0]]), jnp.stack([up_bias[:, 0]] * 2)])
    tiny = jnp.pad(tiny, ((0, 0), (0, 14), (0, 128 - per)))

    def halves(shard):
        return shard.reshape(2, -1, shard.shape[1])

    shards = [tiny, halves(w_qkv), halves(w_out), halves(w_up), pair_up(w_down)]
    if fused:
        bufs, (h1, q, k, v, mixed, lse, cm, par) = front(geo, lengths, tokens, shards)
        wq, wo, wu = (b.reshape(F, D, b.shape[-1]) for b in bufs[1:4])
        out, gmid, gmix, dwo, dwu, small, gub, part = mid(geo, lengths, par, tokens, cotangent, mixed, wo, wu, bufs[4])
        ig, s_down, s_up, s_out, s_qkv, s_tiny = back(
            geo, lengths, lse, part, small, gub, par, q, k, v, gmix, mixed, cm, tokens, h1, gmid, wq, [dwu, dwo]
        )
    else:
        bufs = gather(geo, shards)
        t = bufs[0].reshape(F, n_dp, 2, 16, 128)[..., :per].astype(F32)
        par = jnp.concatenate([t[:, :, 0, 0].reshape(F, D), t[:, :, 0, 1].reshape(F, D)], axis=0)
        upb = jnp.broadcast_to(t[:, :, 1, 0].reshape(F, D).T.reshape(1, FF), (8, FF))
        wq, wo, wu = (b.reshape(F, D, b.shape[-1]) for b in bufs[1:4])
        wd = repair(bufs[4].reshape((F, n_dp * 2) + bufs[4].shape[-2:]), FF // 32)
        h1, q, k, v = qkv(tokens, par, wq)
        mixed, lse, cm = attn_fwd(lengths, q, k, v)
        out, gmid, gmix, small_b, gub, dwo, dwu, dwd = mlp(lengths, tokens, cotangent, mixed, par, upb, wo, wu, wd)
        gp = attn_bwd(lengths, q, k, v, gmix, mixed, lse, cm)
        ig, small_a, dwq = qkv_back(tokens, h1, gp, gmid, par, wq)
        small = small_a + small_b

        def split(grad, rows):
            return grad.reshape((geo.nx, geo.nc, geo.nz, geo.ny, 2, rows, grad.shape[-1]))

        ub = gub[0].reshape(D, F).T.reshape(F, n_dp, per)
        rows = jnp.stack([small[0:4], small[4:8]]).reshape(2, F, n_dp, per)
        g = jnp.stack([jnp.stack([rows[0], rows[1]], axis=2), jnp.stack([ub, ub], axis=2)], axis=2)
        g = split(jnp.pad(g, ((0, 0), (0, 0), (0, 0), (0, 6), (0, 128 - per))), 8)
        r, rd = per // 2, FF // n_dp // 4
        s_tiny, s_out, s_up, s_down, s_qkv = scatter(geo, [g, split(dwo, r), split(dwu, r), split(repair(dwd, rd), rd), split(dwq, r)], 1)
    return (
        out,
        ig,
        s_tiny[0, 0, :per, None],
        s_tiny[0, 1, :per, None],
        s_qkv.reshape(-1, s_qkv.shape[-1]),
        s_out.reshape(-1, s_out.shape[-1]),
        s_up.reshape(-1, s_up.shape[-1]),
        s_tiny[1, 0, :per, None],
        pair_down(s_down),
    )


def solution(mesh):
    geo = Geo(mesh.shape["dp"], mesh.shape["fsdp"])
    both, split = P(("dp", "fsdp"), None), P("dp", "fsdp")
    return jax.shard_map(
        functools.partial(body, geo), mesh=mesh, in_specs=(both,) * 3 + (split,) * 7, out_specs=(both,) * 2 + (split,) * 7, check_vma=False
    )
```

```python
import functools

import jax
import jax.numpy as jnp
from jax import lax
from jax.experimental import pallas as pl
from jax.experimental.pallas import tpu as pltpu
from jax.sharding import PartitionSpec as P

HEADS = 12
EPS = 1e-05
BIG = 1e30
B = 256
F32, BF16 = jnp.float32, jnp.bfloat16
VLIM = 60 << 20
MESH = pl.DeviceIdType.MESH


class Geo:
    def __init__(self, n_dp, n_fs):
        self.n_dp, self.n_fs = n_dp, n_fs
        self.ny = 2 if n_dp % 2 == 0 else 1
        self.nz = n_dp // self.ny
        self.nc = 2 if n_fs % 2 == 0 else 1
        self.nx = n_fs // self.nc

    def place(self):
        dp, fs = lax.axis_index("dp"), lax.axis_index("fsdp")
        return dp // self.ny, dp % self.ny, fs // self.nc, fs % self.nc

    def dev(self, z, y, x, c):
        return {"dp": z * self.ny + y, "fsdp": x * self.nc + c}


def others(n, me):
    return [lax.rem(me + k, n) for k in range(1, n)]

def barrier(geo):
    z, y, x, c = geo.place()
    sem = pltpu.get_barrier_semaphore()
    count = 0
    for k in range(1, geo.nz):
        pl.semaphore_signal(sem, inc=1, device_id=geo.dev(lax.rem(z + k, geo.nz), y, x, c), device_id_type=MESH); count += 1
    for k in range(1, geo.ny):
        pl.semaphore_signal(sem, inc=1, device_id=geo.dev(z, lax.rem(y + k, geo.ny), x, c), device_id_type=MESH); count += 1
    for k in range(1, geo.nx):
        pl.semaphore_signal(sem, inc=1, device_id=geo.dev(z, y, lax.rem(x + k, geo.nx), c), device_id_type=MESH); count += 1
    for k in range(1, geo.nc):
        pl.semaphore_signal(sem, inc=1, device_id=geo.dev(z, y, x, lax.rem(c + k, geo.nc)), device_id_type=MESH); count += 1
    pl.semaphore_wait(sem, count)

class Gather:
    def __init__(self, geo, shards, outs, sems):
        self.geo, self.shards, self.outs = geo, shards, outs
        self.lsem, self.s0, self.r0, self.s1, self.r1 = sems
        self.z, self.y, self.x, self.c = geo.place()

    def local(self, w, h):
        o = self.outs[w]
        return pltpu.make_async_copy(self.shards[w].at[h], o.at[self.x, self.c, self.z, self.y, h], self.lsem.at[w, h])

    def zcopy(self, w, h, k):
        g = self.geo
        zt = lax.rem(self.z + k, g.nz)
        return pltpu.make_async_remote_copy(
            src_ref=self.shards[w].at[h], dst_ref=self.outs[w].at[self.x, self.c, self.z, self.y, h],
            send_sem=self.s0.at[w, h, k], recv_sem=self.r0.at[w, h, k],
            device_id=g.dev(zt, self.y, self.x, self.c), device_id_type=MESH)

    def zrecv(self, w, h, k):
        g = self.geo
        zf = lax.rem(self.z + g.nz - k, g.nz)
        return pltpu.make_async_remote_copy(
            src_ref=self.shards[w].at[h], dst_ref=self.outs[w].at[self.x, self.c, zf, self.y, h],
            send_sem=self.s0.at[w, h, k], recv_sem=self.r0.at[w, h, k],
            device_id=g.dev(zf, self.y, self.x, self.c), device_id_type=MESH)

    def pair(self, w, h, stage, k, recv, piece=None):
        g, o = self.geo, self.outs[w]
        z, y, x, c = self.z, self.y, self.x, self.c
        sgn = -1 if recv else 1
        kind = "c" if stage == 3 else ("y" if (stage == 1) == (h == 0) else "x")
        py = lax.rem(y + sgn * k + g.ny, g.ny); px = lax.rem(x + sgn * k + g.nx, g.nx); pc = lax.rem(c + sgn * k + g.nc, g.nc)
        zs = slice(None) if piece is None else lax.rem(z + g.nz - piece, g.nz)
        def view(sx, sc, sy):
            if stage == 1: return o.at[sx, sc, zs, sy, h]
            if stage == 2: return o.at[sx, sc, zs, :, h] if kind == "x" else o.at[:, sc, zs, sy, h]
            return o.at[:, sc, zs, :, h]
        if kind == "y": peer = g.dev(z, py, x, c); pv = view(x, c, py)
        elif kind == "x": peer = g.dev(z, y, px, c); pv = view(px, c, y)
        else: peer = g.dev(z, y, x, pc); pv = view(x, pc, y)
        mine = view(x, c, y)
        ref = pv if recv else mine
        i = (w, h, stage - 1, k, 0 if piece is None else piece)
        return pltpu.make_async_remote_copy(src_ref=ref, dst_ref=ref, send_sem=self.s1.at[i], recv_sem=self.r1.at[i], device_id=peer, device_id_type=MESH)

    def npeers(self, h, stage):
        g = self.geo
        if stage == 3: return g.nc - 1
        return g.ny - 1 if (stage == 1) == (h == 0) else g.nx - 1

    def send(self, w, h, stage):
        if stage == 0:
            self.local(w, h).start()
            for k in range(1, self.geo.nz):
                self.zcopy(w, h, k).start()
        else:
            for k in range(1, 1 + self.npeers(h, stage)):
                self.pair(w, h, stage, k, False).start()

    def recv(self, w, h, stage):
        if stage == 0:
            self.local(w, h).wait()
            for k in range(1, self.geo.nz):
                self.zrecv(w, h, k).wait_recv()
        else:
            for k in range(1, 1 + self.npeers(h, stage)):
                self.pair(w, h, stage, k, True).wait_recv()

    def fine(self, w, t):
        g = self.geo
        for k in range(g.nz):
            stage = t - k + 1
            if not 1 <= stage <= 4:
                continue
            for h in range(2):
                if stage == 1:
                    if k == 0:
                        self.local(w, h).wait()
                    else:
                        self.zrecv(w, h, k).wait_recv()
                else:
                    for n in range(1, 1 + self.npeers(h, stage - 1)):
                        self.pair(w, h, stage - 1, n, True, k).wait_recv()
                if stage < 4:
                    for n in range(1, 1 + self.npeers(h, stage)):
                        self.pair(w, h, stage, n, False, k).start()

    def drain_fine(self, w, h):
        for k in range(1, self.geo.nz):
            self.zcopy(w, h, k).wait_send()
        for stage in (1, 2, 3):
            for n in range(1, 1 + self.npeers(h, stage)):
                for k in range(self.geo.nz):
                    self.pair(w, h, stage, n, False, k).wait_send()

    def start(self, w, h, stage):
        if stage > 0:
            self.recv(w, h, stage - 1)
        self.send(w, h, stage)

    def finish(self, w, h):
        self.recv(w, h, 3)

    def drain(self, w, h, stages=(0, 1, 2, 3)):
        for stage in stages:
            if stage == 0:
                for k in range(1, self.geo.nz):
                    self.zcopy(w, h, k).wait_send()
            else:
                for k in range(1, 1 + self.npeers(h, stage)):
                    self.pair(w, h, stage, k, False).wait_send()


def gather_sems(geo, W, pieces=1):
    m = max(geo.nx, geo.ny, geo.nc)
    D = pltpu.SemaphoreType.DMA
    return [D((W, 2)), D((W, 2, geo.nz)), D((W, 2, geo.nz)), D((W, 2, 3, m, pieces)), D((W, 2, 3, m, pieces))]

def gather_kernel(geo, W, *refs):
    shards, outs, sems = refs[:W], refs[W:2 * W], refs[2 * W:]
    barrier(geo)
    G = Gather(geo, shards, outs, sems)
    for t in range(W + 4):
        for stage in range(4):
            w = t - stage
            if 0 <= w < W:
                for h in range(2): G.start(w, h, stage)
        if t >= 4:
            for h in range(2): G.finish(t - 4, h)
    for w in range(W):
        for h in range(2): G.drain(w, h)

def gather(geo, shards, collective_id=0):
    W = len(shards)
    outs = [jax.ShapeDtypeStruct((geo.nx, geo.nc, geo.nz, geo.ny) + s.shape, s.dtype) for s in shards]
    A = pl.BlockSpec(memory_space=pl.ANY)
    return pl.pallas_call(
        functools.partial(gather_kernel, geo, W), out_shape=outs, in_specs=[A] * W, out_specs=[A] * W,
        scratch_shapes=gather_sems(geo, W),
        compiler_params=pltpu.CompilerParams(collective_id=collective_id, has_side_effects=True, vmem_limit_bytes=16 << 20),
    )(*shards)


class Scatter:

    def __init__(self, geo, grads, outs, bufs, sems, owns=None, own_sem=None, forms=None):
        self.geo, self.grads, self.outs, self.bufs = geo, list(grads), outs, bufs
        self.ss, self.rs = sems
        self.owns, self.own_sem = owns or [None] * len(grads), own_sem
        self.forms = forms or [None] * len(grads)
        self.z, self.y, self.x, self.c = geo.place()

    def copies(self, w, h, stage):
        g, q = self.geo, self.grads[w]
        b1, b2, b3, b4 = self.bufs[4 * w : 4 * w + 4]
        z, y, x, c = self.z, self.y, self.x, self.c
        pc, py, px = 1 - c, 1 - y, 1 - x
        if stage == 0:
            moves = [(q.at[:, pc, :, :, h], b1.at[h], g.dev(z, y, x, pc))]
        elif stage == 1 and h == 0:
            moves = [(b1.at[0, px, :, k], b2.at[0, k], g.dev(z, y, px, c)) for k in range(g.ny)]
        elif stage == 1:
            moves = [(b1.at[1, :, :, py], b2.at[1], g.dev(z, py, x, c))]
        elif stage == 2:
            moves = [(b2.at[h, py if h == 0 else px], b3.at[h], g.dev(z, py, x, c) if h == 0 else g.dev(z, y, px, c))]
        else:
            moves = []
            for k in range(1, g.nz):
                zt = lax.rem(z + k, g.nz)
                moves.append((b3.at[h, zt], b4.at[h, k - 1], g.dev(zt, y, x, c)))
        return [
            pltpu.make_async_remote_copy(src_ref=s, dst_ref=d, send_sem=self.ss.at[w, h, stage, i], recv_sem=self.rs.at[w, h, stage, i], device_id=p, device_id_type=MESH)
            for i, (s, d, p) in enumerate(moves)
        ]

    def own_copy(self, w, h):
        return pltpu.make_async_copy(self.grads[w].at[:, self.c, :, :, h], self.owns[w].at[h], self.own_sem.at[w, h])

    def add(self, w, h, stage):
        g, q = self.geo, self.grads[w]
        b1, b2, b3, b4 = self.bufs[4 * w : 4 * w + 4]
        z, y, x, c = self.z, self.y, self.x, self.c

        def into(ref, at, other):
            ref[at] = (ref[at].astype(F32) + other.astype(F32)).astype(ref.dtype)

        if stage == 0:
            def one(i, _):
                xx, zz, yy = i // (g.nz * g.ny), (i // g.ny) % g.nz, i % g.ny
                mine = q[xx, c, zz, yy, h] if self.owns[w] is None else self.owns[w][h, xx, zz, yy]
                into(b1, (h, xx, zz, yy), mine)
                return 0
            lax.fori_loop(0, g.nx * g.nz * g.ny, one, 0)
        elif stage == 1:
            def one(i, _):
                k, zz = i // g.nz, i % g.nz
                into(b2, (h, k, zz), b1[0, x, zz, k] if h == 0 else b1[1, k, zz, y])
                return 0
            lax.fori_loop(0, 2 * g.nz, one, 0)
        elif stage == 2:
            def one(i, _):
                into(b3, (h, i), b2[h, y if h == 0 else x, i])
                return 0
            lax.fori_loop(0, g.nz, one, 0)
        else:
            if g.nz <= 8:
                total = b3[h, z].astype(F32)
                for k in range(g.nz - 1):
                    total = total + b4[h, k].astype(F32)
            else:
                total = lax.fori_loop(0, g.nz - 1, lambda k, t: t + b4[h, k].astype(F32), b3[h, z].astype(F32))
            self.put(w, h, total)

    def put(self, w, h, total):
        o, form = self.outs[w], self.forms[w]
        r, t = total.shape
        if form is None:
            o[h] = total
        elif form == "rows":
            o[h * r : (h + 1) * r, :] = total
        else:
            for s in range(2):
                o[(2 * h + s) * r : (2 * h + s + 1) * r, :] = total[:, s * (t // 2) : (s + 1) * (t // 2)]

    def remote(self, w, h, stage, i, src, dst, peer):
        return pltpu.make_async_remote_copy(src_ref=src, dst_ref=dst, send_sem=self.ss.at[w, h, stage, i], recv_sem=self.rs.at[w, h, stage, i], device_id=peer, device_id_type=MESH)

    def first(self, w, h, xx):
        g = self.geo
        return self.remote(w, h, 0, xx, self.grads[w].at[xx, 1 - self.c, :, :, h], self.bufs[4 * w].at[h, xx], g.dev(self.z, self.y, self.x, 1 - self.c))

    def piece(self, w, h, stage, k):
        g = self.geo
        b1, b2, b3, b4 = self.bufs[4 * w : 4 * w + 4]
        z, y, x, c = self.z, self.y, self.x, self.c
        zt = lax.rem(z + 1 + k, g.nz)
        over_x, over_y = g.dev(z, y, 1 - x, c), g.dev(z, 1 - y, x, c)
        if stage == 1 and h == 0:
            return self.remote(w, h, 1, k, b1.at[0, 1 - x, zt], b2.at[0, :, zt], over_x)
        if stage == 1:
            return self.remote(w, h, 1, k, b1.at[1, :, zt, 1 - y], b2.at[1, :, zt], over_y)
        if stage == 2:
            return self.remote(w, h, 2, k, b2.at[h, 1 - y if h == 0 else 1 - x, zt], b3.at[h, zt], over_y if h == 0 else over_x)
        return self.remote(w, h, 3, k, b3.at[h, zt], b4.at[h, k], g.dev(zt, y, x, c))

    def tick(self, w, k, stage):
        g, q = self.geo, self.grads[w]
        b1, b2, b3, b4 = self.bufs[4 * w : 4 * w + 4]
        z, y, x, c = self.z, self.y, self.x, self.c

        def into(ref, at, other):
            ref[at] = (ref[at].astype(F32) + other.astype(F32)).astype(ref.dtype)

        if True:
            zt = lax.rem(z + 1 + k, g.nz)
            for h in range(2):
                if stage == 0:
                    if k == 0:
                        for xx in range(g.nx):
                            self.first(w, h, xx).wait_recv()
                    for xx in range(g.nx):
                        for yy in range(g.ny):
                            into(b1, (h, xx, zt, yy), q[xx, c, zt, yy, h])
                    self.piece(w, h, 1, k).start()
                elif stage == 1:
                    self.piece(w, h, 1, k).wait_recv()
                    for n in range(2):
                        into(b2, (h, n, zt), b1[0, x, zt, n] if h == 0 else b1[1, n, zt, y])
                    self.piece(w, h, 2, k).start()
                elif stage == 2:
                    self.piece(w, h, 2, k).wait_recv()
                    into(b3, (h, zt), b2[h, y if h == 0 else x, zt])
                    if k < g.nz - 1:
                        self.piece(w, h, 3, k).start()
                elif stage == 3 and k == g.nz - 1:
                    total = b3[h, z].astype(F32)
                    for n in range(g.nz - 1):
                        self.piece(w, h, 3, n).wait_recv()
                        total = total + b4[h, n].astype(F32)
                    self.put(w, h, total)

    def drain_fine(self, w, h):
        g = self.geo
        for xx in range(g.nx):
            self.first(w, h, xx).wait_send()
        for k in range(g.nz):
            for stage in (1, 2) if k == g.nz - 1 else (1, 2, 3):
                self.piece(w, h, stage, k).wait_send()

    def step(self, w, h, stage):
        if self.owns[w] is not None:
            if stage == 0:
                self.own_copy(w, h).start()
            elif stage == 1:
                self.own_copy(w, h).wait()
        if stage > 0:
            for cp in self.copies(w, h, stage - 1):
                cp.wait_recv()
            self.add(w, h, stage - 1)
        if stage < 4:
            for cp in self.copies(w, h, stage):
                cp.start()

    def drain(self, w, h, stages=(0, 1, 2, 3)):
        for stage in stages:
            for cp in self.copies(w, h, stage):
                cp.wait_send()


def scatter_bufs(geo, shapes):
    out = []
    for s in shapes:
        r, t, d = s.shape[-2], s.shape[-1], s.dtype
        out += [
            pltpu.VMEM((2, geo.nx, geo.nz, geo.ny, r, t), d), pltpu.VMEM((2, 2, geo.nz, r, t), d),
            pltpu.VMEM((2, geo.nz, r, t), d), pltpu.VMEM((2, geo.nz - 1, r, t), d),
        ]
    return out


def scatter_sems(geo, W):
    n = max(2, geo.nz)
    return [pltpu.SemaphoreType.DMA((W, 2, 4, n)), pltpu.SemaphoreType.DMA((W, 2, 4, n))]


def scatter_kernel(geo, W, *refs):
    grads, outs, bufs, sems = refs[:W], refs[W : 2 * W], refs[2 * W : 6 * W], refs[6 * W :]
    barrier(geo)
    S = Scatter(geo, grads, outs, bufs, sems)
    for t in range(W + 4):
        for stage in range(5):
            w = t - stage
            if 0 <= w < W:
                for h in range(2):
                    S.step(w, h, stage)
    for w in range(W):
        for h in range(2):
            S.drain(w, h)


def scatter(geo, grads, collective_id):
    W = len(grads)
    V = pl.BlockSpec(memory_space=pltpu.VMEM)
    return pl.pallas_call(
        functools.partial(scatter_kernel, geo, W),
        out_shape=[jax.ShapeDtypeStruct(g.shape[4:], F32) for g in grads],
        in_specs=[V] * W, out_specs=[V] * W,
        scratch_shapes=scatter_bufs(geo, grads) + scatter_sems(geo, W),
        compiler_params=pltpu.CompilerParams(collective_id=collective_id, has_side_effects=True, vmem_limit_bytes=60 << 20),
        name="scatter",
    )(*grads)


def nn(a, b):
    return lax.dot_general(a, b, (((1,), (0,)), ((), ())), preferred_element_type=F32)


def nt(a, b):
    return lax.dot_general(a, b, (((1,), (1,)), ((), ())), preferred_element_type=F32)


def tn(a, b):
    return lax.dot_general(a, b, (((0,), (0,)), ((), ())), preferred_element_type=F32)


def vm():
    return pl.BlockSpec(memory_space=pltpu.VMEM)


def sm():
    return pl.BlockSpec(memory_space=pltpu.SMEM)


def ends_of(len_ref):
    total, starts, ends = jnp.int32(0), [], []
    for t in range(len_ref.shape[1]):
        starts.append(total)
        total = total + len_ref[0, t]
        ends.append(total)
    return starts, ends


def segment(pos, ends):
    seg = jnp.zeros_like(pos)
    for e in ends:
        seg = seg + (pos >= e).astype(jnp.int32)
    return jnp.where(pos < ends[-1], seg, len(ends) + pos)


def opens(pos, starts, ends):
    hit = jnp.zeros_like(pos)
    for s in starts:
        hit = jnp.where(pos == s, 1, hit)
    return jnp.where(pos < ends[-1], hit, 0)


def lane_half(rows, which):
    lane = lax.broadcasted_iota(jnp.int32, (rows, 128), 1)
    return (lane < 64) if which == 0 else (lane >= 64)


def only(x, which):
    return jnp.where(lane_half(x.shape[0], which), x, jnp.zeros_like(x))


def masks(len_ref, r0, R, J):
    starts, ends = ends_of(len_ref)
    row = lax.broadcasted_iota(jnp.int32, (R, 1), 0) + r0
    col = lax.broadcasted_iota(jnp.int32, (1, J), 1)
    same = segment(row, ends) == segment(col, ends)
    allow = same & (col <= row)
    pick = same & (col < row) & (opens(col, starts, ends) == 0)
    return allow, pick


def ln_stats(x):
    center = x - jnp.mean(x, axis=-1, keepdims=True)
    spread = jnp.mean(center * center, axis=-1, keepdims=True)
    r = lax.rsqrt(spread + EPS)
    return center * r, r


def ln_back(g_h, n, r, gain):
    g_n = g_h * gain
    return r * (g_n - jnp.mean(g_n, axis=-1, keepdims=True) - n * jnp.mean(g_n * n, axis=-1, keepdims=True))


def unpack_cols(blk_ref, full_ref):
    n, _, w = blk_ref.shape
    for f in range(n):
        full_ref[:, f * w : (f + 1) * w] = blk_ref[f]


def qkv_kernel(x_ref, par_ref, w_ref, h1_ref, q_ref, k_ref, v_ref, wf):
    unpack_cols(w_ref, wf)
    D = x_ref.shape[1]
    R = 256
    for b in range(x_ref.shape[0] // R):
        rows = pl.ds(b * R, R)
        n, _ = ln_stats(x_ref[rows, :].astype(F32))
        h1 = (n * par_ref[0:1, :] + par_ref[1:2, :]).astype(BF16)
        h1_ref[rows, :] = h1
        q = (nn(h1, wf[:, 0:D]) + par_ref[4:5, :]).astype(BF16)
        q_ref[rows, :] = q * jnp.asarray(0.125, BF16)
        k_ref[rows, :] = nn(h1, wf[:, D : 2 * D]).astype(BF16)
        v_ref[rows, :] = (nn(h1, wf[:, 2 * D : 3 * D]) + par_ref[5:6, :]).astype(BF16)


def qkv(x, par, w):
    s = jax.ShapeDtypeStruct(x.shape, BF16)
    return pl.pallas_call(
        qkv_kernel, out_shape=[s] * 4, in_specs=[vm()] * 3, out_specs=[vm()] * 4,
        scratch_shapes=[pltpu.VMEM((w.shape[1], w.shape[0] * w.shape[2]), BF16)],
        compiler_params=pltpu.CompilerParams(vmem_limit_bytes=VLIM),
        name="qkv",
    )(x, par, w)


def unpack_pairs(blk_ref, full_ref):
    n, w = blk_ref.shape[0], blk_ref.shape[3] // 2
    for f in range(n):
        for s in range(2):
            full_ref[:, s, :, f * w : (f + 1) * w] = blk_ref[f, :, :, s * w : (s + 1) * w]


def mlp_kernel(R, len_ref, x_ref, cot_ref, mix_ref, par_ref, upb_ref, wo_ref, wu_ref, wd_ref,
               out_ref, gmid_ref, gmix_ref, small_ref, gub_ref, dwo_ref, dwu_ref, dwd_ref,
               wo, wd, act, gin, h2s, gbs):
    T, D = x_ref.shape
    FF = upb_ref.shape[1]
    nf, wf = wu_ref.shape[0], wu_ref.shape[2]
    unpack_cols(wo_ref, wo)
    unpack_pairs(wd_ref, wd)
    _, ends = ends_of(len_ref)
    small_ref[...] = jnp.zeros_like(small_ref)
    gub_ref[...] = jnp.zeros_like(gub_ref)
    cpf = wd.shape[0] // nf
    C0, C1 = 0.7978845608028654, 0.044715

    def block(b, _):
        rows = pl.ds(pl.multiple_of(b * R, R), R)
        x = x_ref[rows, :].astype(F32)
        middle = x + nn(mix_ref[rows, :], wo[...]) + par_ref[6:7, :]
        n2, r2 = ln_stats(middle)
        h2 = (n2 * par_ref[2:3, :] + par_ref[3:4, :]).astype(BF16)
        h2s[rows, :] = h2
        pos = lax.broadcasted_iota(jnp.int32, (R, 1), 0) + b * R
        live = pos < ends[-1]
        gb = jnp.where(live, cot_ref[rows, :].astype(F32), 0.0)
        gbl = gb.astype(BF16)
        gbs[rows, :] = gbl
        branch = jnp.zeros((R, D), F32)
        g_h2 = jnp.zeros((R, D), F32)
        for f in range(nf):
            cols = pl.ds(f * wf, wf)
            wdf = wd[f * cpf : (f + 1) * cpf].reshape(wf, D)
            u = nn(h2, wu_ref[f]) + upb_ref[0:1, f * wf : (f + 1) * wf]
            g_act = nt(gbl, wdf)
            u2 = u * u
            t = jnp.tanh(u * (C0 + (C0 * C1) * u2))
            hp = 0.5 + 0.5 * t
            a = u * hp
            al = a.astype(BF16)
            act[rows, cols] = al
            branch = branch + nn(al, wdf)
            d = hp + (a - a * hp) * (2.0 * C0 + (6.0 * C0 * C1) * u2)
            gi = (g_act * d).astype(BF16)
            gin[rows, cols] = gi
            gub_ref[0:1, f * wf : (f + 1) * wf] += jnp.sum(gi.astype(F32), axis=0, keepdims=True)
            g_h2 = g_h2 + nt(gi, wu_ref[f])
        out_ref[rows, :] = jnp.where(live, middle + branch + par_ref[7:8, :], 0.0).astype(BF16)
        small_ref[2:3, :] += jnp.sum(g_h2 * n2, axis=0, keepdims=True)
        small_ref[3:4, :] += jnp.sum(g_h2, axis=0, keepdims=True)
        g_mid = gb + ln_back(g_h2, n2, r2, par_ref[2:3, :])
        gmid_ref[rows, :] = g_mid
        gml = g_mid.astype(BF16)
        small_ref[6:7, :] += jnp.sum(gml.astype(F32), axis=0, keepdims=True)
        small_ref[7:8, :] += jnp.sum(gb, axis=0, keepdims=True)
        gmix_ref[rows, :] = nt(gml, wo[...]).astype(BF16)
        return 0

    lax.fori_loop(0, T // R, block, 0)
    w4 = D // nf

    def put(ref, grad, lead):
        r = ref.shape[2]
        c = grad.shape[0] // (2 * r)
        g = grad.astype(BF16).reshape(c, 2, r, D)
        for f in range(nf):
            for s in range(2):
                ref[f, pl.ds(lead, c), :, s * w4 : (s + 1) * w4] = g[:, s, :, f * w4 : (f + 1) * w4]

    def outp(i, _):
        g = tn(mix_ref[:, pl.ds(pl.multiple_of(i * 384, 128), 384)], gmid_ref[...].astype(BF16)).astype(BF16)
        for f in range(nf):
            dwo_ref[f, pl.ds(pl.multiple_of(i * 384, 128), 384), :] = g[:, f * w4 : (f + 1) * w4]
        return 0

    lax.fori_loop(0, D // 384, outp, 0)
    K = 384
    cpk = K // (2 * dwd_ref.shape[2])

    def down(i, _):
        put(dwd_ref, tn(act[:, pl.ds(pl.multiple_of(i * K, 128), K)], gbs[...]), i * cpk)
        return 0

    lax.fori_loop(0, FF // K, down, 0)
    H = 384

    def up(i, _):
        f, s = i // (wf // H), i % (wf // H)
        dwu_ref[f, :, pl.ds(pl.multiple_of(s * H, 128), H)] = tn(h2s[...], gin[:, pl.ds(pl.multiple_of(i * H, 128), H)]).astype(BF16)
        return 0

    lax.fori_loop(0, FF // H, up, 0)


def mlp(lengths, x, cot, mixed, par, upb, wo, wu, wd, R=256):
    T, D = x.shape
    FF = upb.shape[1]
    S = jax.ShapeDtypeStruct
    V = pltpu.VMEM
    return pl.pallas_call(
        functools.partial(mlp_kernel, R),
        out_shape=[S((T, D), BF16), S((T, D), F32), S((T, D), BF16), S((8, D), F32), S((8, FF), F32),
                   S(wo.shape, BF16), S(wu.shape, BF16), S(wd.shape, BF16)],
        in_specs=[sm()] + [vm()] * 8, out_specs=[vm()] * 8,
        scratch_shapes=[V((D, D), BF16), V((wd.shape[1], 2, wd.shape[2], D), BF16),
                        V((T, FF), BF16), V((T, FF), BF16), V((T, D), BF16), V((T, D), BF16)],
        compiler_params=pltpu.CompilerParams(vmem_limit_bytes=VLIM),
        name="mlp",
    )(lengths, x, cot, mixed, par, upb, wo, wu, wd)


def qkv_back_kernel(x_ref, h1_ref, gp_ref, gmid_ref, par_ref, w_ref, ig_ref, small_ref, dw_ref):
    T, D = x_ref.shape
    n, _, w = w_ref.shape
    R = 256
    for f in range(n):
        dw_ref[f] = tn(h1_ref[...], gp_ref[:, f * w : (f + 1) * w]).astype(BF16)
    small_ref[...] = jnp.zeros_like(small_ref)
    for b in range(T // R):
        rows = pl.ds(b * R, R)
        g_h1 = jnp.zeros((R, D), F32)
        for f in range(n):
            g_h1 = g_h1 + nt(gp_ref[rows, f * w : (f + 1) * w], w_ref[f])
        n1, r1 = ln_stats(x_ref[rows, :].astype(F32))
        small_ref[0:1, :] += jnp.sum(g_h1 * n1, axis=0, keepdims=True)
        small_ref[1:2, :] += jnp.sum(g_h1, axis=0, keepdims=True)
        small_ref[4:5, :] += jnp.sum(gp_ref[rows, 0:D].astype(F32), axis=0, keepdims=True)
        small_ref[5:6, :] += jnp.sum(gp_ref[rows, 2 * D : 3 * D].astype(F32), axis=0, keepdims=True)
        ig_ref[rows, :] = (gmid_ref[rows, :] + ln_back(g_h1, n1, r1, par_ref[0:1, :])).astype(BF16)


def qkv_back(x, h1, gp, gmid, par, w):
    S = jax.ShapeDtypeStruct
    return pl.pallas_call(
        qkv_back_kernel, out_shape=[S(x.shape, BF16), S((8, x.shape[1]), F32), S(w.shape, BF16)],
        in_specs=[vm()] * 6, out_specs=[vm()] * 3,
        compiler_params=pltpu.CompilerParams(vmem_limit_bytes=VLIM),
        name="qkv_back",
    )(x, h1, gp, gmid, par, w)


def masks_t(len_ref, r0, R, J):
    starts, ends = ends_of(len_ref)
    key = lax.broadcasted_iota(jnp.int32, (J, 1), 0)
    row = lax.broadcasted_iota(jnp.int32, (1, R), 1) + r0
    same = segment(key, ends) == segment(row, ends)
    return same & (key < row) & (opens(key, starts, ends) == 0)


def carried_scores(len_ref, q_ref, k_ref, cm, cmT_ref, carry):
    T = q_ref.shape[0]
    carry[...] = jnp.zeros_like(carry)
    i = lax.broadcasted_iota(jnp.int32, (B, B), 0)
    j = lax.broadcasted_iota(jnp.int32, (B, B), 1)
    lower = jnp.where(j < i, 1.0, 0.0).astype(BF16)
    for b in range(T // B):
        r0, J = b * B, (b + 1) * B
        rows = pl.ds(r0, B)
        allow, pick = masks(len_ref, r0, B, J)
        s0 = jnp.maximum(nt(only(q_ref[rows, 0:128], 0), k_ref[0:J, 0:128]), 0.0)
        chosen = jnp.where(pick, s0 * s0, 0.0)
        hi = chosen.astype(BF16)
        lo = (chosen - hi.astype(F32)).astype(BF16)
        carried = carry[0:1, 0:J] + (nn(lower, hi) + nn(lower, lo))
        c = jnp.where(allow, carried, BIG)
        cm[rows, 0:J] = c
        cmT_ref[0:J, rows] = jnp.transpose(c)
        carry[0:1, 0:J] = carry[0:1, 0:J] + jnp.sum(chosen, axis=0, keepdims=True)


def fwd_pair(p, q_ref, k_ref, v_ref, o_ref, lse, cm, s_sc, p_sc, C):
    T = q_ref.shape[0]
    lane = lax.broadcasted_iota(jnp.int32, (C, 128), 1)
    cols = pl.ds(pl.multiple_of(p * 128, 128), 128)
    k2, v2 = k_ref[:, cols], v_ref[:, cols]
    for half in range(2):
        q2 = only(q_ref[:, cols], half)
        for kb in range(T // B):
            s_sc[half, kb * B :, kb * B : (kb + 1) * B] = nt(q2[kb * B :], k2[kb * B : (kb + 1) * B])
    for rb in range(T // C):
        J = ((rb * C) // B + 1) * B
        rows = slice(rb * C, (rb + 1) * C)
        inv = []
        for half in range(2):
            l = s_sc[half, rows, :J] - cm[rows, :J]
            m = jnp.max(l, axis=1, keepdims=True)
            e = jnp.exp(l - m)
            t = jnp.sum(e, axis=1, keepdims=True)
            p_sc[half, rows, :J] = (e * (1.0 / t)).astype(BF16)
            lse[rows, :] = jnp.where(lane == 2 * p + half, m + jnp.log(t), lse[rows, :])
        if (rb * C) % B == B - C:
            b0 = (rb * C) // B * B
            o = [nn(p_sc[half, b0 : b0 + B, :J], v2[:J]) for half in range(2)]
            lanes = lax.broadcasted_iota(jnp.int32, (B, 128), 1)
            o_ref[b0 : b0 + B, cols] = jnp.where(lanes < 64, o[0], o[1]).astype(BF16)


def attn_fwd_kernel(C, len_ref, q_ref, k_ref, v_ref, o_ref, lseT_ref, cmT_ref, cm, lse, s_sc, p_sc, carry):
    carried_scores(len_ref, q_ref, k_ref, cm, cmT_ref, carry)

    def pair(p, _):
        fwd_pair(p, q_ref, k_ref, v_ref, o_ref, lse, cm, s_sc, p_sc, C)
        return 0

    lax.fori_loop(0, HEADS // 2, pair, 0)
    lseT_ref[...] = jnp.transpose(lse[...])[0:16]


def attn_fwd(lengths, q, k, v, C=64):
    T = q.shape[0]
    V = pltpu.VMEM
    return pl.pallas_call(
        functools.partial(attn_fwd_kernel, C),
        out_shape=[jax.ShapeDtypeStruct(q.shape, BF16), jax.ShapeDtypeStruct((16, T), F32), jax.ShapeDtypeStruct((T, T), F32)],
        in_specs=[sm()] + [vm()] * 3, out_specs=[vm()] * 3,
        scratch_shapes=[V((T, T), F32), V((T, 128), F32), V((2, T, T), F32), V((2, T, T), BF16), V((8, T), F32)],
        compiler_params=pltpu.CompilerParams(vmem_limit_bytes=VLIM),
        name="attn_fwd",
    )(lengths, q, k, v)


def row_sums(do_ref, o_ref, DT):
    T, D = do_ref.shape
    f = lax.broadcasted_iota(jnp.int32, (D, 128), 0)
    h = lax.broadcasted_iota(jnp.int32, (D, 128), 1)
    E = jnp.where((f >= h * 64) & (f < h * 64 + 64), 1.0, 0.0).astype(BF16)
    for b in range(T // B):
        rows = pl.ds(b * B, B)
        x = do_ref[rows, :].astype(F32) * o_ref[rows, :].astype(F32)
        hi = x.astype(BF16)
        lo = (x - hi.astype(F32)).astype(BF16)
        DT[:, rows] = jnp.transpose(nn(hi, E) + nn(lo, E))[0:16]


def bwd_scores(p, half, q_ref, k_ref, v_ref, do_ref, sT, dpT):
    T = q_ref.shape[0]
    cols = p * 128 if isinstance(p, int) else pl.multiple_of(p * 128, 128)
    c = pl.ds(cols, 128)
    k2, v2 = k_ref[:, c], v_ref[:, c]
    q2, do2 = only(q_ref[:, c], half), only(do_ref[:, c], half)
    for rb in range(T // B):
        J, r = (rb + 1) * B, slice(rb * B, (rb + 1) * B)
        sT[0:J, r] = nt(k2[0:J], q2[r])
        dpT[0:J, r] = nt(v2[0:J], do2[r])


def bwd_softmax(h, sT, dpT, pT, dsT, lseT, DT, cmT, C, add_into=None, keep=None):
    T = sT.shape[0]
    for kc in range(T // C):
        i0 = (kc * C) // B * B
        keys = slice(kc * C, (kc + 1) * C)
        pr = jnp.exp(sT[keys, i0:] - cmT[keys, i0:] - lseT[pl.ds(h, 1), i0:])
        ds = pr * (dpT[keys, i0:] - DT[pl.ds(h, 1), i0:])
        pT[keys, i0:] = pr.astype(BF16)
        if keep is not None:
            keep[keys, i0:] = ds
        else:
            dsT[keys, i0:] = ds.astype(BF16)
        add_into[keys, i0:] += ds


def bwd_products(p, half, q_ref, k_ref, do_ref, pT, dsT, gp_ref, dk, dv, first):
    T, D = q_ref.shape
    cols = p * 128 if isinstance(p, int) else pl.multiple_of(p * 128, 128)
    c = pl.ds(cols, 128)
    k2 = k_ref[:, c]
    q2, do2 = only(q_ref[:, c], half), only(do_ref[:, c], half)
    for kb in range(T // B):
        keys = slice(kb * B, (kb + 1) * B)
        a = nn(pT[keys, kb * B :], do2[kb * B :])
        d = nn(dsT[keys, kb * B :], q2[kb * B :])
        if first:
            dv[keys, :], dk[keys, :] = a, d
        else:
            dv[keys, :] += a
            dk[keys, :] += d
    lanes = lax.broadcasted_iota(jnp.int32, (B, 128), 1)
    for rb in range(T // B):
        J, r = (rb + 1) * B, slice(rb * B, (rb + 1) * B)
        dq = (tn(dsT[0:J, r], k2[0:J]) * 0.125).astype(BF16)
        if first:
            gp_ref[r, c] = dq
        else:
            gp_ref[r, c] = jnp.where((lanes < 64) == (half == 0), dq, gp_ref[r, c])


def first_head(len_ref, sT, ds0, dsT, G):
    T = sT.shape[0]
    i = lax.broadcasted_iota(jnp.int32, (B, B), 0)
    j = lax.broadcasted_iota(jnp.int32, (B, B), 1)
    after = jnp.where(i > j, 1.0, 0.0).astype(BF16)
    later = jnp.zeros((T, 1), F32)
    for rb in reversed(range(T // B)):
        J, r = (rb + 1) * B, slice(rb * B, (rb + 1) * B)
        g = -G[0:J, r]
        hi = g.astype(BF16)
        lo = (g - hi.astype(F32)).astype(BF16)
        g_chosen = later[0:J] + (nn(hi, after) + nn(lo, after))
        later = later[0:J] + jnp.sum(g, axis=1, keepdims=True)
        pick = masks_t(len_ref, rb * B, B, J)
        full = ds0[0:J, r] + jnp.where(pick, 2.0 * jnp.maximum(sT[0:J, r], 0.0) * g_chosen, 0.0)
        dsT[0:J, r] = full.astype(BF16)


def attn_bwd_kernel(C, len_ref, q_ref, k_ref, v_ref, do_ref, o_ref, lseT, cmT, gp_ref, DT, sT, dpT, pT, dsT, G, dk, dv):
    T, D = q_ref.shape
    row_sums(do_ref, o_ref, DT)
    G[...] = jnp.zeros_like(G)

    def put(p):
        ck = D + p * 128 if isinstance(p, int) else pl.multiple_of(D + p * 128, 128)
        cv = 2 * D + p * 128 if isinstance(p, int) else pl.multiple_of(2 * D + p * 128, 128)
        gp_ref[:, pl.ds(ck, 128)] = dk[...].astype(BF16)
        gp_ref[:, pl.ds(cv, 128)] = dv[...].astype(BF16)

    def pair(k, _):
        p = HEADS // 2 - 1 - k
        for half in range(2):
            bwd_scores(p, half, q_ref, k_ref, v_ref, do_ref, sT.at[half], dpT.at[half])
        for half in range(2):
            bwd_softmax(2 * p + half, sT.at[half], dpT.at[half], pT.at[half], dsT.at[half], lseT, DT, cmT, C, G)
        for half in range(2):
            bwd_products(p, half, q_ref, k_ref, do_ref, pT.at[half], dsT.at[half], gp_ref, dk, dv, half == 0)
        put(p)
        return 0

    lax.fori_loop(0, HEADS // 2 - 1, pair, 0)
    bwd_scores(0, 1, q_ref, k_ref, v_ref, do_ref, sT.at[1], dpT.at[1])
    bwd_softmax(1, sT.at[1], dpT.at[1], pT.at[1], dsT.at[1], lseT, DT, cmT, C, G)
    bwd_products(0, 1, q_ref, k_ref, do_ref, pT.at[1], dsT.at[1], gp_ref, dk, dv, True)
    bwd_scores(0, 0, q_ref, k_ref, v_ref, do_ref, sT.at[0], dpT.at[0])
    bwd_softmax(0, sT.at[0], dpT.at[0], pT.at[0], dsT.at[0], lseT, DT, cmT, C, G, keep=dpT.at[0])
    first_head(len_ref, sT.at[0], dpT.at[0], dsT.at[0], G)
    bwd_products(0, 0, q_ref, k_ref, do_ref, pT.at[0], dsT.at[0], gp_ref, dk, dv, False)
    put(0)


def attn_bwd(lengths, q, k, v, do, o, lseT, cmT, C=64):
    T, D = q.shape
    V = pltpu.VMEM
    return pl.pallas_call(
        functools.partial(attn_bwd_kernel, C),
        out_shape=jax.ShapeDtypeStruct((T, 3 * D), BF16),
        in_specs=[sm()] + [vm()] * 7, out_specs=vm(),
        scratch_shapes=[V((16, T), F32), V((2, T, T), F32), V((2, T, T), F32), V((2, T, T), BF16), V((2, T, T), BF16), V((T, T), F32), V((T, 128), F32), V((T, 128), F32)],
        compiler_params=pltpu.CompilerParams(vmem_limit_bytes=VLIM),
        name="attn_bwd",
    )(lengths, q, k, v, do, o, lseT, cmT)


def fold_tiny(tiny, par, per, n_dp, F):
    for f in range(F):
        for d in range(n_dp):
            for s in range(2):
                par[s * F + f : s * F + f + 1, d * per : (d + 1) * per] = tiny[f, d, 0, s : s + 1, 0:per].astype(F32)
            par[2 * F + f : 2 * F + f + 1, d * per : (d + 1) * per] = tiny[f, d, 1, 0:1, 0:per].astype(F32)


def front_kernel(geo, C, *refs):
    len_ref, x_ref = refs[0:2]
    raw, bufs = refs[2:7], refs[7:12]
    h1_o, q_o, k_o, v_o, mix_o, lseT_o, cmT_o, par = refs[12:20]
    tiny_v, wq_v, wf, h1, q, k, v, mix, cmT, cm, lse, s_sc, p_sc, carry, lsem, osem, down = refs[20:37]
    sems = refs[37:]
    T, D = x_ref.shape
    F, per = geo.n_fs, D // geo.n_dp
    shards = [raw[0]] + [s.reshape(2, s.shape[0] // 2, s.shape[1]) for s in raw[1:4]] + [down]
    r, w = down.shape[1], raw[4].shape[1]
    for i in range(4):
        down[i // 2, :, (i % 2) * w : (i % 2 + 1) * w] = raw[4][i * r : (i + 1) * r, :]
    barrier(geo)
    G = Gather(geo, shards, bufs, sems)
    at_block = {1: ((3, 1),), 3: ((2, 2),)}
    at_middle = ()
    plan = {0: ((3, 2),), 1: ((4, 1), (2, 3)), 4: ((3, 3),)}

    def ev(*items):
        for w, stage in items:
            for h in range(2):
                if stage == 4:
                    G.finish(w, h)
                else:
                    G.start(w, h, stage)

    ev((0, 0), (1, 0))
    G.fine(1, 0)
    ev((2, 0))
    for b in range(T // B):
        rows = pl.ds(b * B, B)
        n, _ = ln_stats(x_ref[rows, :].astype(F32))
        s_sc[0, rows, 0:D] = n
    ev((0, 1))
    G.fine(1, 1)
    ev((3, 0), (0, 2))
    G.fine(1, 2)
    ev((0, 3))
    G.fine(1, 3)
    ev((4, 0))
    for t in range(4, geo.nz + 3):
        G.fine(1, t)
        if t == geo.nz + 1:
            ev((2, 1))
    ev((0, 4))
    get_t = pltpu.make_async_copy(bufs[0], tiny_v, lsem.at[0])
    get_q = pltpu.make_async_copy(bufs[1], wq_v, lsem.at[1])
    get_t.start()
    get_q.start()
    get_t.wait()
    par[...] = jnp.zeros_like(par)
    fold_tiny(tiny_v.reshape(F, geo.n_dp, 2, 16, 128), par, per, geo.n_dp, F)
    get_q.wait()
    unpack_cols(wq_v.reshape(F, D, wq_v.shape[-1]), wf)
    outs = [pltpu.make_async_copy(a, b, osem.at[i]) for i, (a, b) in enumerate(((h1, h1_o), (q, q_o), (k, k_o), (v, v_o), (cmT, cmT_o), (mix, mix_o), (lse, lse))[:6])]
    for b in range(T // B):
        rows = pl.ds(b * B, B)
        hb = (s_sc[0, rows, 0:D] * par[0:1, :] + par[1:2, :]).astype(BF16)
        h1[rows, :] = hb
        q[rows, :] = (nn(hb, wf[:, 0:D]) + par[4:5, :]).astype(BF16) * jnp.asarray(0.125, BF16)
        k[rows, :] = nn(hb, wf[:, D : 2 * D]).astype(BF16)
        v[rows, :] = (nn(hb, wf[:, 2 * D : 3 * D]) + par[5:6, :]).astype(BF16)
        if b in at_block:
            ev(*at_block[b])
    for i in range(4):
        outs[i].start()
    ev(*at_middle)
    carried_scores(len_ref, q, k, cm, cmT, carry)
    outs[4].start()

    def pair(p, _):
        for at, items in plan.items():
            @pl.when(p == at)
            def _():
                ev(*items)
        fwd_pair(p, q, k, v, mix, lse, cm, s_sc, p_sc, C)
        return 0

    lax.fori_loop(0, HEADS // 2, pair, 0)
    outs[5].start()
    lseT_o[...] = jnp.transpose(lse[...])[0:16]
    ev((2, 4), (3, 4))
    for h in range(2):
        G.recv(4, h, 1)
    for w in range(5):
        for h in range(2):
            if w == 1:
                G.drain_fine(w, h)
            else:
                G.drain(w, h, (0, 1) if w == 4 else (0, 1, 2, 3))
    for i in range(6):
        outs[i].wait()


def front(geo, lengths, x, raw, collective_id=0, C=64):
    shards = [raw[0]] + [jax.ShapeDtypeStruct((2, s.shape[0] // 2, s.shape[1]), s.dtype) for s in raw[1:4]]
    shards.append(jax.ShapeDtypeStruct((2, raw[4].shape[0] // 4, 2 * raw[4].shape[1]), BF16))
    T, D = x.shape
    V, S, A = pltpu.VMEM, jax.ShapeDtypeStruct, pl.BlockSpec(memory_space=pl.ANY)
    lead = (geo.nx, geo.nc, geo.nz, geo.ny)
    tok = S((T, D), BF16)
    res = pl.pallas_call(
        functools.partial(front_kernel, geo, C),
        out_shape=[S(lead + s.shape, s.dtype) for s in shards] + [tok] * 5 + [S((16, T), F32), S((T, T), F32), S((16, D), F32)],
        in_specs=[sm(), vm()] + [vm()] * 5,
        out_specs=[A] * 10 + [vm(), A, vm()],
        scratch_shapes=[V(lead + shards[0].shape, BF16), V(lead + shards[1].shape, BF16), V((D, 3 * D), BF16)]
        + [V((T, D), BF16)] * 5 + [V((T, T), F32), V((T, T), F32), V((T, 128), F32), V((2, T, T), F32), V((2, T, T), BF16), V((8, T), F32)]
        + [pltpu.SemaphoreType.DMA((2,)), pltpu.SemaphoreType.DMA((6,)), V(shards[4].shape, BF16)] + gather_sems(geo, 5, geo.nz),
        compiler_params=pltpu.CompilerParams(collective_id=collective_id, has_side_effects=True, vmem_limit_bytes=VLIM),
        name="front",
    )(lengths, x, *raw)
    return res[:5], res[5:]


def repeats(w, n):
    r = lax.broadcasted_iota(jnp.int32, (w, n * w), 0)
    m = lax.broadcasted_iota(jnp.int32, (w, n * w), 1)
    return jnp.where((m >= n * r) & (m < n * r + n), 1.0, 0.0).astype(BF16)


def own_row(n, w):
    row = lax.broadcasted_iota(jnp.int32, (8, n * w), 0)
    m = lax.broadcasted_iota(jnp.int32, (8, n * w), 1)
    return row == lax.rem(m, n)


def weave(rows8, n, out_ref):
    w = rows8.shape[1] // n
    rep, own = repeats(w, n), own_row(n, w)
    for f in range(n):
        wide = nn(rows8[:, f * w : (f + 1) * w].astype(BF16), rep)
        line = jnp.sum(jnp.where(own, wide, 0.0), axis=0, keepdims=True)
        out_ref[:, f * n * w : (f + 1) * n * w] = jnp.broadcast_to(line, (8, n * w))


def unweave(line, n, out_ref):
    w = line.shape[1] // n // n
    rep, own = repeats(w, n), own_row(n, w)
    for f in range(n):
        wide = jnp.where(own, jnp.broadcast_to(line[:, f * n * w : (f + 1) * n * w], (8, n * w)), 0.0)
        hi = wide.astype(BF16)
        lo = (wide - hi.astype(F32)).astype(BF16)
        out_ref[:, f * w : (f + 1) * w] = nt(hi, rep) + nt(lo, rep)


def mid_kernel(geo, R, *refs):
    len_ref, par, x_h, cot_h, mix_h, wo_h, wu_h, half_h = refs[0:8]
    out_o, gmid_o, gmix_o, dwo_o, dwu_o, small, gub, part_o = refs[8:16]
    upb, X, C, M, wo_raw, wo, wu, land, wd, act, gin, h2s, gmid, gmix, dwo, dwu, dwd = refs[16:33]
    isem, osem, wsem = refs[33:36]
    bufs, ssems, gsems = refs[36:40], refs[40:42], refs[42:47]
    T, D = X.shape
    FF = act.shape[1]
    F = geo.n_fs
    wf, w4 = FF // F, D // F
    barrier(geo)
    G = Gather(geo, [None], [land], gsems)
    S = Scatter(geo, [dwd], [None], bufs, ssems)
    z, y, xx, c = geo.place()
    keep = [
        pltpu.make_async_copy(half_h.at[xx, c, :, :, 0], land.at[xx, c, :, :, 0], wsem.at[0]),
        pltpu.make_async_copy(half_h.at[:, c, :, y, 1], land.at[:, c, :, y, 1], wsem.at[1]),
    ]
    for cp in keep:
        cp.start()
    ins = [pltpu.make_async_copy(a, b, isem.at[i]) for i, (a, b) in enumerate(((wo_h, wo_raw), (x_h, X), (mix_h, M), (cot_h, C), (wu_h, wu)))]
    for cp in ins:
        cp.start()
    weave(par[8:16, :], F, upb)
    small[...] = jnp.zeros_like(small)
    gub[...] = jnp.zeros_like(gub)
    for cp in keep:
        cp.wait()
    for h in range(2):
        G.send(0, h, 2)
    _, ends = ends_of(len_ref)
    C0, C1 = 0.7978845608028654, 0.044715
    ins[0].wait()
    unpack_cols(wo_raw, wo)
    for cp in ins[1:]:
        cp.wait()

    def first(b, _):
        rows = pl.ds(pl.multiple_of(b * R, R), R)
        middle = X[rows, :].astype(F32) + nn(M[rows, :], wo[...]) + par[6:7, :]
        gmid[rows, :] = middle
        n2, _ = ln_stats(middle)
        h2 = (n2 * par[2:3, :] + par[3:4, :]).astype(BF16)
        h2s[rows, :] = h2
        pos = lax.broadcasted_iota(jnp.int32, (R, 1), 0) + b * R
        gb = jnp.where(pos < ends[-1], C[rows, :].astype(F32), 0.0)
        C[rows, :] = gb.astype(BF16)
        small[7:8, :] += jnp.sum(gb, axis=0, keepdims=True)
        for f in range(F):
            cols = slice(f * wf, (f + 1) * wf)
            u = nn(h2, wu[f]) + upb[0:1, cols]
            u2 = u * u
            t = jnp.tanh(u * (C0 + (C0 * C1) * u2))
            hp = 0.5 + 0.5 * t
            a = u * hp
            act[rows, cols] = a.astype(BF16)
            gin[rows, cols] = (hp + (a - a * hp) * (2.0 * C0 + (6.0 * C0 * C1) * u2)).astype(BF16)
        return 0

    lax.fori_loop(0, T // R, first, 0)
    for h in range(2):
        G.recv(0, h, 2)
        G.send(0, h, 3)

    r = dwd.shape[5]
    dv = dwd.reshape(F, 2 * geo.n_dp, r, 2 * w4)
    K = 768
    per = K // (2 * r)

    def down(i, _):
        g = tn(act[:, pl.ds(pl.multiple_of(i * K, 128), K)], C[...]).astype(BF16).reshape(per, 2, r, D)
        for f in range(F):
            for s in range(2):
                dv[f, pl.ds(i * per, per), :, s * w4 : (s + 1) * w4] = g[:, s, :, f * w4 : (f + 1) * w4]
        return 0

    lax.fori_loop(0, FF // K, down, 0)
    for h in range(2):
        S.step(0, h, 0)
    for h in range(2):
        G.recv(0, h, 3)
    lv = land.reshape(F, 2 * geo.n_dp, r, 2 * w4)
    for f in range(F):
        for s in range(2):
            wd[:, s, :, f * w4 : (f + 1) * w4] = lv[f, :, :, s * w4 : (s + 1) * w4]
    cpf = wd.shape[0] // F

    def second(b, _):
        rows = pl.ds(pl.multiple_of(b * R, R), R)
        pos = lax.broadcasted_iota(jnp.int32, (R, 1), 0) + b * R
        gbl = C[rows, :]
        branch = jnp.zeros((R, D), F32)
        g_h2 = jnp.zeros((R, D), F32)
        for f in range(F):
            cols = slice(f * wf, (f + 1) * wf)
            wdf = wd[f * cpf : (f + 1) * cpf].reshape(wf, D)
            branch = branch + nn(act[rows, cols], wdf)
            gi = (nt(gbl, wdf) * gin[rows, cols].astype(F32)).astype(BF16)
            gin[rows, cols] = gi
            gub[0:1, cols] += jnp.sum(gi.astype(F32), axis=0, keepdims=True)
            g_h2 = g_h2 + nt(gi, wu[f])
        middle = gmid[rows, :]
        X[rows, :] = jnp.where(pos < ends[-1], middle + branch + par[7:8, :], 0.0).astype(BF16)
        n2, r2 = ln_stats(middle)
        small[2:3, :] += jnp.sum(g_h2 * n2, axis=0, keepdims=True)
        small[3:4, :] += jnp.sum(g_h2, axis=0, keepdims=True)
        g_mid = gbl.astype(F32) + ln_back(g_h2, n2, r2, par[2:3, :])
        gmid[rows, :] = g_mid
        gml = g_mid.astype(BF16)
        small[6:7, :] += jnp.sum(gml.astype(F32), axis=0, keepdims=True)
        gmix[rows, :] = nt(gml, wo[...]).astype(BF16)
        return 0

    half = T // R // 2
    lax.fori_loop(0, half, second, 0)
    for h in range(2):
        S.step(0, h, 1)
    lax.fori_loop(half, T // R, second, 0)
    outs = [pltpu.make_async_copy(a, b, osem.at[i]) for i, (a, b) in enumerate(((X, out_o), (gmid, gmid_o), (gmix, gmix_o)))]
    for cp in outs:
        cp.start()
    o4 = dwo.reshape(F, D, w4)
    for i in range(2):
        g = tn(M[:, i * 384 : (i + 1) * 384], gmid[...].astype(BF16)).astype(BF16)
        for f in range(F):
            o4[f, i * 384 : (i + 1) * 384, :] = g[:, f * w4 : (f + 1) * w4]
    outs.append(pltpu.make_async_copy(dwo, dwo_o, osem.at[3]))
    outs[3].start()
    H = 256
    sent = []
    ov = dwu_o.reshape(F, D, wf)
    for f in range(F):
        if f >= 2:
            sent[f - 2].wait()

        def up(i, _):
            dwu[f % 2, :, pl.ds(pl.multiple_of(i * H, 128), H)] = tn(h2s[...], gin[:, pl.ds(pl.multiple_of(f * wf + i * H, 128), H)]).astype(BF16)
            return 0

        lax.fori_loop(0, wf // H, up, 0)
        sent.append(pltpu.make_async_copy(dwu.at[f % 2], ov.at[f], wsem.at[f % 2]))
        sent[f].start()
    for h in range(2):
        for cp in S.copies(0, h, 1):
            cp.wait_recv()
        S.add(0, h, 1)
    part_o[...] = bufs[1][...]
    for h in range(2):
        for stage in range(2):
            for cp in S.copies(0, h, stage):
                cp.wait_send()
        G.drain(0, h, (2, 3))
    for cp in outs + sent[-2:]:
        cp.wait()


def mid(geo, lengths, par, x, cot, mixed, wo, wu, half, collective_id=2, R=512):
    T, D = x.shape
    FF = wu.shape[0] * wu.shape[2]
    V, S, A, D_ = pltpu.VMEM, jax.ShapeDtypeStruct, pl.BlockSpec(memory_space=pl.ANY), pltpu.SemaphoreType.DMA
    lead = (geo.nx, geo.nc, geo.nz, geo.ny, 2)
    rr = D // geo.n_dp // 2
    tok = lambda: V((T, D), BF16)
    dwo, dwu = S(lead + (rr, wo.shape[2]), BF16), S(lead + (rr, wu.shape[2]), BF16)
    n = half.shape[5]
    return pl.pallas_call(
        functools.partial(mid_kernel, geo, R),
        out_shape=[S((T, D), BF16), S((T, D), F32), S((T, D), BF16), dwo, dwu, S((8, D), F32), S((8, FF), F32), S((2, 2, geo.nz) + half.shape[5:], BF16)],
        in_specs=[sm(), vm()] + [A] * 6,
        out_specs=[A] * 5 + [vm()] * 3,
        scratch_shapes=[V((8, FF), F32), tok(), tok(), tok(), V(wo.shape, BF16), V((D, D), BF16), V(wu.shape, BF16), V(half.shape, BF16),
                        V((2 * geo.n_dp, 2, n, D), BF16), V((T, FF), BF16), V((T, FF), BF16), tok(), V((T, D), F32), tok(), V(dwo.shape, BF16), V((2, D, wu.shape[2]), BF16), V(half.shape, BF16),
                        D_((5,)), D_((4,)), D_((2,))]
        + scatter_bufs(geo, [half]) + scatter_sems(geo, 1) + gather_sems(geo, 1),
        compiler_params=pltpu.CompilerParams(collective_id=collective_id, has_side_effects=True, vmem_limit_bytes=VLIM),
        name="mid",
    )(lengths, par, x, cot, mixed, wo, wu, half)


def spread_tiny(small, ub, tiny, per, n_dp, F):
    for f in range(F):
        for d in range(n_dp):
            for s in range(2):
                tiny[f, d, 0, s : s + 1, 0:per] = small[s * F + f : s * F + f + 1, d * per : (d + 1) * per]
            tiny[f, d, 1, 0:1, 0:per] = ub[f : f + 1, d * per : (d + 1) * per]


def back_kernel(geo, C, *refs):
    len_ref, lseT, part, small_b, gub, par = refs[0:6]
    q_h, k_h, v_h, do_h, o_h, cmT_h, x_h, h1_h, gmid_h, wq_h = refs[6:16]
    parts = refs[16:18]
    ig_o = refs[18]
    outs = refs[19:24]
    gp, DT, small, tiny, isem, osem, own_sem = refs[24:31]
    owns = [None] + list(refs[31:33]) + [None, None]
    bufs, sems = [None, part] + list(refs[33:51]), refs[51:53]
    D, T = gp.shape[1] // 3, gp.shape[0]
    F, n_dp = geo.n_fs, geo.n_dp
    per = D // n_dp
    barrier(geo)
    S = Scatter(geo, [None] + list(parts) + [None, tiny], outs, bufs, sems, owns, own_sem, ["pairs", "rows", "rows", "rows", None])
    DOWN, UP, OUT, QKV, TINY = range(5)

    def ev(*items):
        for w, stage in items:
            for h in range(2):
                S.step(w, h, stage)

    for h in range(2):
        for cp in S.copies(DOWN, h, 2):
            cp.start()
    ev((UP, 0), (OUT, 0))

    def attention(q, k, v, do, o, cmT, sT, dpT, pT, dsT, G, dk, dv):
        ins = [pltpu.make_async_copy(a, b, isem.at[i]) for i, (a, b) in enumerate(((do_h, do), (o_h, o), (q_h, q), (k_h, k), (v_h, v), (cmT_h, cmT)))]
        for cp in ins:
            cp.start()
        G[...] = jnp.zeros_like(G)
        ins[0].wait()
        ins[1].wait()
        row_sums(do, o, DT)
        for cp in ins[2:]:
            cp.wait()

        def put(p):
            ck = D + p * 128 if isinstance(p, int) else pl.multiple_of(D + p * 128, 128)
            cv = 2 * D + p * 128 if isinstance(p, int) else pl.multiple_of(2 * D + p * 128, 128)
            gp[:, pl.ds(ck, 128)] = dk[...].astype(BF16)
            gp[:, pl.ds(cv, 128)] = dv[...].astype(BF16)

        plan = {(0, 0): ((UP, 1),), (0, 1): ((OUT, 1),), (1, 1): ((DOWN, 3),), (3, 0): ((UP, 2),), (4, 0): ((OUT, 2),), (4, 1): ((UP, 3),)}

        def pair(n, _):
            p = HEADS // 2 - 1 - n
            for half in range(2):
                for (at, hf), items in plan.items():
                    if hf == half:
                        @pl.when(n == at)
                        def _():
                            ev(*items)
                bwd_scores(p, half, q, k, v, do, sT, dpT)
                bwd_softmax(2 * p + half, sT, dpT, pT, dsT, lseT, DT, cmT, C, G)
                bwd_products(p, half, q, k, do, pT, dsT, gp, dk, dv, half == 0)
            put(p)
            return 0

        lax.fori_loop(0, HEADS // 2 - 1, pair, 0)
        bwd_scores(0, 1, q, k, v, do, sT, dpT)
        bwd_softmax(1, sT, dpT, pT, dsT, lseT, DT, cmT, C, G)
        bwd_products(0, 1, q, k, do, pT, dsT, gp, dk, dv, True)
        ev((OUT, 3))
        bwd_scores(0, 0, q, k, v, do, sT, dpT)
        bwd_softmax(0, sT, dpT, pT, dsT, lseT, DT, cmT, C, G, keep=dpT)
        first_head(len_ref, sT, dpT, dsT, G)
        bwd_products(0, 0, q, k, do, pT, dsT, gp, dk, dv, False)
        put(0)

    V = pltpu.VMEM
    pl.run_scoped(
        attention, *[V((T, D), BF16)] * 5, V((T, T), F32), V((T, T), F32), V((T, T), F32), V((T, T), BF16), V((T, T), BF16), V((T, T), F32),
        V((T, 128), F32), V((T, 128), F32),
    )

    def projections(x, h1, gmid, wq, dwq, ig, ub):
        ins = [pltpu.make_async_copy(a, b, isem.at[i]) for i, (a, b) in enumerate(((h1_h, h1), (wq_h, wq), (x_h, x), (gmid_h, gmid)))]
        for cp in ins:
            cp.start()
        n, _, w = wq.shape
        dw = dwq.reshape(n, D, w)
        ins[0].wait()
        S.grads[QKV] = dwq
        for f in range(n):
            dw[f] = tn(h1[...], gp[:, f * w : (f + 1) * w]).astype(BF16)

            @pl.when(S.c != f % geo.nc)
            def _():
                for h in range(2):
                    S.first(QKV, h, f // geo.nc).start()

        for k in range(geo.nz):
            S.tick(QKV, k, 0)
        small[...] = small_b[...]
        order = {0: (), 1: (), 2: ((0, 1), (1, 1)), 3: ((2, 1), (0, 2), (3, 1), (1, 2), (2, 2))}
        for cp in ins[1:]:
            cp.wait()
        for b in range(T // B):
            rows = pl.ds(b * B, B)
            g_h1 = jnp.zeros((B, D), F32)
            for f in range(n):
                g_h1 = g_h1 + nt(gp[rows, f * w : (f + 1) * w], wq[f])
            n1, r1 = ln_stats(x[rows, :].astype(F32))
            small[0:1, :] += jnp.sum(g_h1 * n1, axis=0, keepdims=True)
            small[1:2, :] += jnp.sum(g_h1, axis=0, keepdims=True)
            small[4:5, :] += jnp.sum(gp[rows, 0:D].astype(F32), axis=0, keepdims=True)
            small[5:6, :] += jnp.sum(gp[rows, 2 * D : 3 * D].astype(F32), axis=0, keepdims=True)
            ig[rows, :] = (gmid[rows, :] + ln_back(g_h1, n1, r1, par[0:1, :])).astype(BF16)
            for k, stage in order[b]:
                S.tick(QKV, k, stage)
        out_cp = pltpu.make_async_copy(ig, ig_o, osem)
        out_cp.start()
        tiny[...] = jnp.zeros_like(tiny)
        unweave(gub[0:1, :], F, ub)
        spread_tiny(small, ub, tiny.reshape(F, n_dp, 2, 8, 128), per, n_dp, F)
        ev((TINY, 0))
        S.tick(QKV, 3, 2)
        ev((DOWN, 4), (UP, 4), (OUT, 4))
        ev((TINY, 1), (TINY, 2), (TINY, 3))
        S.tick(QKV, 3, 3)
        ev((TINY, 4))
        for h in range(2):
            S.drain_fine(QKV, h)
            for wt in (DOWN, UP, OUT, TINY):
                S.drain(wt, h, (2, 3) if wt == DOWN else (0, 1, 2, 3))
        out_cp.wait()

    pl.run_scoped(projections, V((T, D), BF16), V((T, D), BF16), V((T, D), F32), V(wq_h.shape, BF16), V((geo.nx, geo.nc, geo.nz, geo.ny, 2, per // 2, wq_h.shape[-1]), BF16), V((T, D), BF16), V((8, D), F32))


def back(geo, lengths, lseT, part, small_b, gub, par, q, k, v, do, o, cmT, x, h1, gmid, wq, parts, collective_id=1, C=64):
    T, D = x.shape
    V, S, A, D_ = pltpu.VMEM, jax.ShapeDtypeStruct, pl.BlockSpec(memory_space=pl.ANY), pltpu.SemaphoreType.DMA
    per = D // geo.n_dp
    dwq = S((geo.nx, geo.nc, geo.nz, geo.ny, 2, per // 2, wq.shape[-1]), BF16)
    tiny = S((geo.nx, geo.nc, geo.nz, geo.ny, 2, 8, 128), F32)
    down = S((geo.nx, geo.nc, geo.nz, geo.ny, 2) + part.shape[3:], BF16)
    grads = [down] + list(parts) + [dwq, tiny]
    finals = [S((4 * part.shape[3], part.shape[4] // 2), F32)] + [S((2 * g.shape[5], g.shape[6]), F32) for g in grads[1:4]] + [S(tiny.shape[4:], F32)]
    owns = [V((2, geo.nx, geo.nz, geo.ny) + g.shape[5:], BF16) for g in parts]
    return pl.pallas_call(
        functools.partial(back_kernel, geo, C),
        out_shape=[S((T, D), BF16)] + finals,
        in_specs=[sm()] + [vm()] * 5 + [A] * 12,
        out_specs=[A] + [vm()] * 5,
        scratch_shapes=[V((T, 3 * D), BF16), V((16, T), F32), V((8, D), F32), V(tiny.shape, F32), D_((6,)), D_, D_((5, 2))]
        + owns + scatter_bufs(geo, grads)[2:] + scatter_sems(geo, 5),
        compiler_params=pltpu.CompilerParams(collective_id=collective_id, has_side_effects=True, vmem_limit_bytes=VLIM),
        name="back",
    )(lengths, lseT, part, small_b, gub, par, q, k, v, do, o, cmT, x, h1, gmid, wq, *parts)


def pair_up(shard):
    w = shard.shape[1]
    return shard.reshape(2, 2, -1, w).transpose(0, 2, 1, 3).reshape(2, -1, 2 * w)


def pair_down(halves):
    w = halves.shape[2] // 2
    return halves.reshape(2, -1, 2, w).transpose(0, 2, 1, 3).reshape(-1, w)


def repair(blocks, r):
    n, c, r0, w2 = blocks.shape
    if r0 == r:
        return blocks
    w = w2 // 2
    flat = blocks.reshape(n, c, r0, 2, w).transpose(0, 1, 3, 2, 4).reshape(n, -1, 2, r, w)
    return flat.transpose(0, 1, 3, 2, 4).reshape(n, -1, r, w2)


def body(geo, tokens, cotangent, lengths, norm_params, bias_params, w_qkv, w_out, w_up, up_bias, w_down):
    T, D = tokens.shape
    F, n_dp, per = geo.n_fs, geo.n_dp, D // geo.n_dp
    FF = D * F * up_bias.shape[1]
    fused = (per // 2) % 16 == 0
    tiny = jnp.stack([jnp.stack([norm_params[:, 0], bias_params[:, 0]]), jnp.stack([up_bias[:, 0]] * 2)])
    tiny = jnp.pad(tiny, ((0, 0), (0, 14), (0, 128 - per)))

    def halves(shard):
        return shard.reshape(2, -1, shard.shape[1])

    if fused:
        bufs, (h1, q, k, v, mixed, lse, cm, par) = front(geo, lengths, tokens, [tiny, w_qkv, w_out, w_up, w_down])
        wq, wo, wu = (b.reshape(F, D, b.shape[-1]) for b in bufs[1:4])
        out, gmid, gmix, dwo, dwu, small, gub, part = mid(geo, lengths, par, tokens, cotangent, mixed, wo, wu, bufs[4])
        ig, s_down, s_up, s_out, s_qkv, s_tiny = back(
            geo, lengths, lse, part, small, gub, par, q, k, v, gmix, mixed, cm, tokens, h1, gmid, wq, [dwu, dwo]
        )
    else:
        bufs = gather(geo, [tiny, halves(w_qkv), halves(w_out), halves(w_up), pair_up(w_down)])
        t = bufs[0].reshape(F, n_dp, 2, 16, 128)[..., :per].astype(F32)
        par = jnp.concatenate([t[:, :, 0, 0].reshape(F, D), t[:, :, 0, 1].reshape(F, D)], axis=0)
        upb = jnp.broadcast_to(t[:, :, 1, 0].reshape(F, D).T.reshape(1, FF), (8, FF))
        wq, wo, wu = (b.reshape(F, D, b.shape[-1]) for b in bufs[1:4])
        wd = repair(bufs[4].reshape((F, n_dp * 2) + bufs[4].shape[-2:]), FF // 32)
        h1, q, k, v = qkv(tokens, par, wq)
        mixed, lse, cm = attn_fwd(lengths, q, k, v)
        out, gmid, gmix, small_b, gub, dwo, dwu, dwd = mlp(lengths, tokens, cotangent, mixed, par, upb, wo, wu, wd)
        gp = attn_bwd(lengths, q, k, v, gmix, mixed, lse, cm)
        ig, small_a, dwq = qkv_back(tokens, h1, gp, gmid, par, wq)
        small = small_a + small_b

        def split(grad, rows):
            return grad.reshape((geo.nx, geo.nc, geo.nz, geo.ny, 2, rows, grad.shape[-1]))

        ub = gub[0].reshape(D, F).T.reshape(F, n_dp, per)
        rows = jnp.stack([small[0:4], small[4:8]]).reshape(2, F, n_dp, per)
        g = jnp.stack([jnp.stack([rows[0], rows[1]], axis=2), jnp.stack([ub, ub], axis=2)], axis=2)
        g = split(jnp.pad(g, ((0, 0), (0, 0), (0, 0), (0, 6), (0, 128 - per))), 8)
        r, rd = per // 2, FF // n_dp // 4
        s_tiny, s_out, s_up, s_down, s_qkv = scatter(geo, [g, split(dwo, r), split(dwu, r), split(repair(dwd, rd), rd), split(dwq, r)], 1)
        s_qkv, s_out, s_up = (s.reshape(-1, s.shape[-1]) for s in (s_qkv, s_out, s_up))
        s_down = pair_down(s_down)
    return (
        out,
        ig,
        s_tiny[0, 0, :per, None],
        s_tiny[0, 1, :per, None],
        s_qkv,
        s_out,
        s_up,
        s_tiny[1, 0, :per, None],
        s_down,
    )


def solution(mesh):
    geo = Geo(mesh.shape["dp"], mesh.shape["fsdp"])
    both, split = P(("dp", "fsdp"), None), P("dp", "fsdp")
    return jax.shard_map(
        functools.partial(body, geo), mesh=mesh, in_specs=(both,) * 3 + (split,) * 7, out_specs=(both,) * 2 + (split,) * 7, check_vma=False
    )
```

```python
import functools

import jax
import jax.numpy as jnp
from jax import lax
from jax.experimental import pallas as pl
from jax.experimental.pallas import tpu as pltpu
from jax.sharding import PartitionSpec as P

HEADS = 12
EPS = 1e-05
BIG = 1e30
B = 256
F32, BF16 = jnp.float32, jnp.bfloat16
VLIM = 60 << 20
MESH = pl.DeviceIdType.MESH


class Geo:
    def __init__(self, n_dp, n_fs):
        self.n_dp, self.n_fs = n_dp, n_fs
        self.ny = 2 if n_dp % 2 == 0 else 1
        self.nz = n_dp // self.ny
        self.nc = 2 if n_fs % 2 == 0 else 1
        self.nx = n_fs // self.nc

    def place(self):
        dp, fs = lax.axis_index("dp"), lax.axis_index("fsdp")
        return dp // self.ny, dp % self.ny, fs // self.nc, fs % self.nc

    def dev(self, z, y, x, c):
        return {"dp": z * self.ny + y, "fsdp": x * self.nc + c}


def others(n, me):
    return [lax.rem(me + k, n) for k in range(1, n)]

def barrier(geo):
    z, y, x, c = geo.place()
    sem = pltpu.get_barrier_semaphore()
    count = 0
    for k in range(1, geo.nz):
        pl.semaphore_signal(sem, inc=1, device_id=geo.dev(lax.rem(z + k, geo.nz), y, x, c), device_id_type=MESH); count += 1
    for k in range(1, geo.ny):
        pl.semaphore_signal(sem, inc=1, device_id=geo.dev(z, lax.rem(y + k, geo.ny), x, c), device_id_type=MESH); count += 1
    for k in range(1, geo.nx):
        pl.semaphore_signal(sem, inc=1, device_id=geo.dev(z, y, lax.rem(x + k, geo.nx), c), device_id_type=MESH); count += 1
    for k in range(1, geo.nc):
        pl.semaphore_signal(sem, inc=1, device_id=geo.dev(z, y, x, lax.rem(c + k, geo.nc)), device_id_type=MESH); count += 1
    pl.semaphore_wait(sem, count)

class Gather:
    def __init__(self, geo, shards, outs, sems):
        self.geo, self.shards, self.outs = geo, shards, outs
        self.lsem, self.s0, self.r0, self.s1, self.r1 = sems
        self.z, self.y, self.x, self.c = geo.place()

    def local(self, w, h):
        o = self.outs[w]
        return pltpu.make_async_copy(self.shards[w].at[h], o.at[self.x, self.c, self.z, self.y, h], self.lsem.at[w, h])

    def zcopy(self, w, h, k):
        g = self.geo
        zt = lax.rem(self.z + k, g.nz)
        return pltpu.make_async_remote_copy(
            src_ref=self.shards[w].at[h], dst_ref=self.outs[w].at[self.x, self.c, self.z, self.y, h],
            send_sem=self.s0.at[w, h, k], recv_sem=self.r0.at[w, h, k],
            device_id=g.dev(zt, self.y, self.x, self.c), device_id_type=MESH)

    def zrecv(self, w, h, k):
        g = self.geo
        zf = lax.rem(self.z + g.nz - k, g.nz)
        return pltpu.make_async_remote_copy(
            src_ref=self.shards[w].at[h], dst_ref=self.outs[w].at[self.x, self.c, zf, self.y, h],
            send_sem=self.s0.at[w, h, k], recv_sem=self.r0.at[w, h, k],
            device_id=g.dev(zf, self.y, self.x, self.c), device_id_type=MESH)

    def pair(self, w, h, stage, k, recv, piece=None):
        g, o = self.geo, self.outs[w]
        z, y, x, c = self.z, self.y, self.x, self.c
        sgn = -1 if recv else 1
        kind = "c" if stage == 3 else ("y" if (stage == 1) == (h == 0) else "x")
        py = lax.rem(y + sgn * k + g.ny, g.ny); px = lax.rem(x + sgn * k + g.nx, g.nx); pc = lax.rem(c + sgn * k + g.nc, g.nc)
        zs = slice(None) if piece is None else lax.rem(z + g.nz - piece, g.nz)
        def view(sx, sc, sy):
            if stage == 1: return o.at[sx, sc, zs, sy, h]
            if stage == 2: return o.at[sx, sc, zs, :, h] if kind == "x" else o.at[:, sc, zs, sy, h]
            return o.at[:, sc, zs, :, h]
        if kind == "y": peer = g.dev(z, py, x, c); pv = view(x, c, py)
        elif kind == "x": peer = g.dev(z, y, px, c); pv = view(px, c, y)
        else: peer = g.dev(z, y, x, pc); pv = view(x, pc, y)
        mine = view(x, c, y)
        ref = pv if recv else mine
        i = (w, h, stage - 1, k, 0 if piece is None else piece)
        return pltpu.make_async_remote_copy(src_ref=ref, dst_ref=ref, send_sem=self.s1.at[i], recv_sem=self.r1.at[i], device_id=peer, device_id_type=MESH)

    def npeers(self, h, stage):
        g = self.geo
        if stage == 3: return g.nc - 1
        return g.ny - 1 if (stage == 1) == (h == 0) else g.nx - 1

    def send(self, w, h, stage):
        if stage == 0:
            self.local(w, h).start()
            for k in range(1, self.geo.nz):
                self.zcopy(w, h, k).start()
        else:
            for k in range(1, 1 + self.npeers(h, stage)):
                self.pair(w, h, stage, k, False).start()

    def recv(self, w, h, stage):
        if stage == 0:
            self.local(w, h).wait()
            for k in range(1, self.geo.nz):
                self.zrecv(w, h, k).wait_recv()
        else:
            for k in range(1, 1 + self.npeers(h, stage)):
                self.pair(w, h, stage, k, True).wait_recv()

    def fine(self, w, t):
        g = self.geo
        for k in range(g.nz):
            stage = t - k + 1
            if not 1 <= stage <= 4:
                continue
            for h in range(2):
                if stage == 1:
                    if k == 0:
                        self.local(w, h).wait()
                    else:
                        self.zrecv(w, h, k).wait_recv()
                else:
                    for n in range(1, 1 + self.npeers(h, stage - 1)):
                        self.pair(w, h, stage - 1, n, True, k).wait_recv()
                if stage < 4:
                    for n in range(1, 1 + self.npeers(h, stage)):
                        self.pair(w, h, stage, n, False, k).start()

    def drain_fine(self, w, h):
        for k in range(1, self.geo.nz):
            self.zcopy(w, h, k).wait_send()
        for stage in (1, 2, 3):
            for n in range(1, 1 + self.npeers(h, stage)):
                for k in range(self.geo.nz):
                    self.pair(w, h, stage, n, False, k).wait_send()

    def start(self, w, h, stage):
        if stage > 0:
            self.recv(w, h, stage - 1)
        self.send(w, h, stage)

    def finish(self, w, h):
        self.recv(w, h, 3)

    def drain(self, w, h, stages=(0, 1, 2, 3)):
        for stage in stages:
            if stage == 0:
                for k in range(1, self.geo.nz):
                    self.zcopy(w, h, k).wait_send()
            else:
                for k in range(1, 1 + self.npeers(h, stage)):
                    self.pair(w, h, stage, k, False).wait_send()


def gather_sems(geo, W, pieces=1):
    m = max(geo.nx, geo.ny, geo.nc)
    D = pltpu.SemaphoreType.DMA
    return [D((W, 2)), D((W, 2, geo.nz)), D((W, 2, geo.nz)), D((W, 2, 3, m, pieces)), D((W, 2, 3, m, pieces))]

def gather_kernel(geo, W, *refs):
    shards, outs, sems = refs[:W], refs[W:2 * W], refs[2 * W:]
    barrier(geo)
    G = Gather(geo, shards, outs, sems)
    for t in range(W + 4):
        for stage in range(4):
            w = t - stage
            if 0 <= w < W:
                for h in range(2): G.start(w, h, stage)
        if t >= 4:
            for h in range(2): G.finish(t - 4, h)
    for w in range(W):
        for h in range(2): G.drain(w, h)

def gather(geo, shards, collective_id=0):
    W = len(shards)
    outs = [jax.ShapeDtypeStruct((geo.nx, geo.nc, geo.nz, geo.ny) + s.shape, s.dtype) for s in shards]
    A = pl.BlockSpec(memory_space=pl.ANY)
    return pl.pallas_call(
        functools.partial(gather_kernel, geo, W), out_shape=outs, in_specs=[A] * W, out_specs=[A] * W,
        scratch_shapes=gather_sems(geo, W),
        compiler_params=pltpu.CompilerParams(collective_id=collective_id, has_side_effects=True, vmem_limit_bytes=16 << 20),
    )(*shards)


class Scatter:

    def __init__(self, geo, grads, outs, bufs, sems, owns=None, own_sem=None, forms=None):
        self.geo, self.grads, self.outs, self.bufs = geo, list(grads), outs, bufs
        self.ss, self.rs = sems
        self.owns, self.own_sem = owns or [None] * len(grads), own_sem
        self.forms = forms or [None] * len(grads)
        self.z, self.y, self.x, self.c = geo.place()

    def copies(self, w, h, stage):
        g, q = self.geo, self.grads[w]
        b1, b2, b3, b4 = self.bufs[4 * w : 4 * w + 4]
        z, y, x, c = self.z, self.y, self.x, self.c
        pc, py, px = 1 - c, 1 - y, 1 - x
        if stage == 0:
            moves = [(q.at[:, pc, :, :, h], b1.at[h], g.dev(z, y, x, pc))]
        elif stage == 1 and h == 0:
            moves = [(b1.at[0, px, :, k], b2.at[0, k], g.dev(z, y, px, c)) for k in range(g.ny)]
        elif stage == 1:
            moves = [(b1.at[1, :, :, py], b2.at[1], g.dev(z, py, x, c))]
        elif stage == 2:
            moves = [(b2.at[h, py if h == 0 else px], b3.at[h], g.dev(z, py, x, c) if h == 0 else g.dev(z, y, px, c))]
        else:
            moves = []
            for k in range(1, g.nz):
                zt = lax.rem(z + k, g.nz)
                moves.append((b3.at[h, zt], b4.at[h, k - 1], g.dev(zt, y, x, c)))
        return [
            pltpu.make_async_remote_copy(src_ref=s, dst_ref=d, send_sem=self.ss.at[w, h, stage, i], recv_sem=self.rs.at[w, h, stage, i], device_id=p, device_id_type=MESH)
            for i, (s, d, p) in enumerate(moves)
        ]

    def own_copy(self, w, h):
        return pltpu.make_async_copy(self.grads[w].at[:, self.c, :, :, h], self.owns[w].at[h], self.own_sem.at[w, h])

    def add(self, w, h, stage):
        g, q = self.geo, self.grads[w]
        b1, b2, b3, b4 = self.bufs[4 * w : 4 * w + 4]
        z, y, x, c = self.z, self.y, self.x, self.c

        def into(ref, at, other):
            ref[at] = (ref[at].astype(F32) + other.astype(F32)).astype(ref.dtype)

        if stage == 0:
            def one(i, _):
                xx, zz, yy = i // (g.nz * g.ny), (i // g.ny) % g.nz, i % g.ny
                mine = q[xx, c, zz, yy, h] if self.owns[w] is None else self.owns[w][h, xx, zz, yy]
                into(b1, (h, xx, zz, yy), mine)
                return 0
            lax.fori_loop(0, g.nx * g.nz * g.ny, one, 0)
        elif stage == 1:
            def one(i, _):
                k, zz = i // g.nz, i % g.nz
                into(b2, (h, k, zz), b1[0, x, zz, k] if h == 0 else b1[1, k, zz, y])
                return 0
            lax.fori_loop(0, 2 * g.nz, one, 0)
        elif stage == 2:
            def one(i, _):
                into(b3, (h, i), b2[h, y if h == 0 else x, i])
                return 0
            lax.fori_loop(0, g.nz, one, 0)
        else:
            if g.nz <= 8:
                total = b3[h, z].astype(F32)
                for k in range(g.nz - 1):
                    total = total + b4[h, k].astype(F32)
            else:
                total = lax.fori_loop(0, g.nz - 1, lambda k, t: t + b4[h, k].astype(F32), b3[h, z].astype(F32))
            self.put(w, h, total)

    def put(self, w, h, total):
        o, form = self.outs[w], self.forms[w]
        r, t = total.shape
        if form is None:
            o[h] = total
        elif form == "rows":
            o[h * r : (h + 1) * r, :] = total
        else:
            for s in range(2):
                o[:, (2 * h + s) * r : (2 * h + s + 1) * r] = jnp.transpose(total[:, s * (t // 2) : (s + 1) * (t // 2)])

    def remote(self, w, h, stage, i, src, dst, peer):
        return pltpu.make_async_remote_copy(src_ref=src, dst_ref=dst, send_sem=self.ss.at[w, h, stage, i], recv_sem=self.rs.at[w, h, stage, i], device_id=peer, device_id_type=MESH)

    def first(self, w, h, xx):
        g = self.geo
        return self.remote(w, h, 0, xx, self.grads[w].at[xx, 1 - self.c, :, :, h], self.bufs[4 * w].at[h, xx], g.dev(self.z, self.y, self.x, 1 - self.c))

    def piece(self, w, h, stage, k):
        g = self.geo
        b1, b2, b3, b4 = self.bufs[4 * w : 4 * w + 4]
        z, y, x, c = self.z, self.y, self.x, self.c
        zt = lax.rem(z + 1 + k, g.nz)
        over_x, over_y = g.dev(z, y, 1 - x, c), g.dev(z, 1 - y, x, c)
        if stage == 1 and h == 0:
            return self.remote(w, h, 1, k, b1.at[0, 1 - x, zt], b2.at[0, :, zt], over_x)
        if stage == 1:
            return self.remote(w, h, 1, k, b1.at[1, :, zt, 1 - y], b2.at[1, :, zt], over_y)
        if stage == 2:
            return self.remote(w, h, 2, k, b2.at[h, 1 - y if h == 0 else 1 - x, zt], b3.at[h, zt], over_y if h == 0 else over_x)
        return self.remote(w, h, 3, k, b3.at[h, zt], b4.at[h, k], g.dev(zt, y, x, c))

    def tick(self, w, k, stage):
        g, q = self.geo, self.grads[w]
        b1, b2, b3, b4 = self.bufs[4 * w : 4 * w + 4]
        z, y, x, c = self.z, self.y, self.x, self.c

        def into(ref, at, other):
            ref[at] = (ref[at].astype(F32) + other.astype(F32)).astype(ref.dtype)

        if True:
            zt = lax.rem(z + 1 + k, g.nz)
            for h in range(2):
                if stage == 0:
                    if k == 0:
                        for xx in range(g.nx):
                            self.first(w, h, xx).wait_recv()
                    for xx in range(g.nx):
                        for yy in range(g.ny):
                            into(b1, (h, xx, zt, yy), q[xx, c, zt, yy, h])
                    self.piece(w, h, 1, k).start()
                elif stage == 1:
                    self.piece(w, h, 1, k).wait_recv()
                    for n in range(2):
                        into(b2, (h, n, zt), b1[0, x, zt, n] if h == 0 else b1[1, n, zt, y])
                    self.piece(w, h, 2, k).start()
                elif stage == 2:
                    self.piece(w, h, 2, k).wait_recv()
                    into(b3, (h, zt), b2[h, y if h == 0 else x, zt])
                    if k < g.nz - 1:
                        self.piece(w, h, 3, k).start()
                elif stage == 3 and k == g.nz - 1:
                    total = b3[h, z].astype(F32)
                    for n in range(g.nz - 1):
                        self.piece(w, h, 3, n).wait_recv()
                        total = total + b4[h, n].astype(F32)
                    self.put(w, h, total)

    def drain_fine(self, w, h):
        g = self.geo
        for xx in range(g.nx):
            self.first(w, h, xx).wait_send()
        for k in range(g.nz):
            for stage in (1, 2) if k == g.nz - 1 else (1, 2, 3):
                self.piece(w, h, stage, k).wait_send()

    def step(self, w, h, stage):
        if self.owns[w] is not None:
            if stage == 0:
                self.own_copy(w, h).start()
            elif stage == 1:
                self.own_copy(w, h).wait()
        if stage > 0:
            for cp in self.copies(w, h, stage - 1):
                cp.wait_recv()
            self.add(w, h, stage - 1)
        if stage < 4:
            for cp in self.copies(w, h, stage):
                cp.start()

    def drain(self, w, h, stages=(0, 1, 2, 3)):
        for stage in stages:
            for cp in self.copies(w, h, stage):
                cp.wait_send()


def scatter_bufs(geo, shapes):
    out = []
    for s in shapes:
        r, t, d = s.shape[-2], s.shape[-1], s.dtype
        out += [
            pltpu.VMEM((2, geo.nx, geo.nz, geo.ny, r, t), d), pltpu.VMEM((2, 2, geo.nz, r, t), d),
            pltpu.VMEM((2, geo.nz, r, t), d), pltpu.VMEM((2, geo.nz - 1, r, t), d),
        ]
    return out


def scatter_sems(geo, W):
    n = max(2, geo.nz)
    return [pltpu.SemaphoreType.DMA((W, 2, 4, n)), pltpu.SemaphoreType.DMA((W, 2, 4, n))]


def scatter_kernel(geo, W, *refs):
    grads, outs, bufs, sems = refs[:W], refs[W : 2 * W], refs[2 * W : 6 * W], refs[6 * W :]
    barrier(geo)
    S = Scatter(geo, grads, outs, bufs, sems)
    for t in range(W + 4):
        for stage in range(5):
            w = t - stage
            if 0 <= w < W:
                for h in range(2):
                    S.step(w, h, stage)
    for w in range(W):
        for h in range(2):
            S.drain(w, h)


def scatter(geo, grads, collective_id):
    W = len(grads)
    V = pl.BlockSpec(memory_space=pltpu.VMEM)
    return pl.pallas_call(
        functools.partial(scatter_kernel, geo, W),
        out_shape=[jax.ShapeDtypeStruct(g.shape[4:], F32) for g in grads],
        in_specs=[V] * W, out_specs=[V] * W,
        scratch_shapes=scatter_bufs(geo, grads) + scatter_sems(geo, W),
        compiler_params=pltpu.CompilerParams(collective_id=collective_id, has_side_effects=True, vmem_limit_bytes=60 << 20),
        name="scatter",
    )(*grads)


def nn(a, b):
    return lax.dot_general(a, b, (((1,), (0,)), ((), ())), preferred_element_type=F32)


def nt(a, b):
    return lax.dot_general(a, b, (((1,), (1,)), ((), ())), preferred_element_type=F32)


def tn(a, b):
    return lax.dot_general(a, b, (((0,), (0,)), ((), ())), preferred_element_type=F32)


def vm():
    return pl.BlockSpec(memory_space=pltpu.VMEM)


def sm():
    return pl.BlockSpec(memory_space=pltpu.SMEM)


def ends_of(len_ref):
    total, starts, ends = jnp.int32(0), [], []
    for t in range(len_ref.shape[1]):
        starts.append(total)
        total = total + len_ref[0, t]
        ends.append(total)
    return starts, ends


def segment(pos, ends):
    seg = jnp.zeros_like(pos)
    for e in ends:
        seg = seg + (pos >= e).astype(jnp.int32)
    return jnp.where(pos < ends[-1], seg, len(ends) + pos)


def opens(pos, starts, ends):
    hit = jnp.zeros_like(pos)
    for s in starts:
        hit = jnp.where(pos == s, 1, hit)
    return jnp.where(pos < ends[-1], hit, 0)


def lane_half(rows, which):
    lane = lax.broadcasted_iota(jnp.int32, (rows, 128), 1)
    return (lane < 64) if which == 0 else (lane >= 64)


def only(x, which):
    return jnp.where(lane_half(x.shape[0], which), x, jnp.zeros_like(x))


def masks(len_ref, r0, R, J):
    starts, ends = ends_of(len_ref)
    row = lax.broadcasted_iota(jnp.int32, (R, 1), 0) + r0
    col = lax.broadcasted_iota(jnp.int32, (1, J), 1)
    same = segment(row, ends) == segment(col, ends)
    allow = same & (col <= row)
    pick = same & (col < row) & (opens(col, starts, ends) == 0)
    return allow, pick


def ln_stats(x):
    center = x - jnp.mean(x, axis=-1, keepdims=True)
    spread = jnp.mean(center * center, axis=-1, keepdims=True)
    r = lax.rsqrt(spread + EPS)
    return center * r, r


def ln_back(g_h, n, r, gain):
    g_n = g_h * gain
    return r * (g_n - jnp.mean(g_n, axis=-1, keepdims=True) - n * jnp.mean(g_n * n, axis=-1, keepdims=True))


def unpack_cols(blk_ref, full_ref):
    n, _, w = blk_ref.shape
    for f in range(n):
        full_ref[:, f * w : (f + 1) * w] = blk_ref[f]


def qkv_kernel(x_ref, par_ref, w_ref, h1_ref, q_ref, k_ref, v_ref, wf):
    unpack_cols(w_ref, wf)
    D = x_ref.shape[1]
    R = 256
    for b in range(x_ref.shape[0] // R):
        rows = pl.ds(b * R, R)
        n, _ = ln_stats(x_ref[rows, :].astype(F32))
        h1 = (n * par_ref[0:1, :] + par_ref[1:2, :]).astype(BF16)
        h1_ref[rows, :] = h1
        q = (nn(h1, wf[:, 0:D]) + par_ref[4:5, :]).astype(BF16)
        q_ref[rows, :] = q * jnp.asarray(0.125, BF16)
        k_ref[rows, :] = nn(h1, wf[:, D : 2 * D]).astype(BF16)
        v_ref[rows, :] = (nn(h1, wf[:, 2 * D : 3 * D]) + par_ref[5:6, :]).astype(BF16)


def qkv(x, par, w):
    s = jax.ShapeDtypeStruct(x.shape, BF16)
    return pl.pallas_call(
        qkv_kernel, out_shape=[s] * 4, in_specs=[vm()] * 3, out_specs=[vm()] * 4,
        scratch_shapes=[pltpu.VMEM((w.shape[1], w.shape[0] * w.shape[2]), BF16)],
        compiler_params=pltpu.CompilerParams(vmem_limit_bytes=VLIM),
        name="qkv",
    )(x, par, w)


def unpack_pairs(blk_ref, full_ref):
    n, w = blk_ref.shape[0], blk_ref.shape[3] // 2
    for f in range(n):
        for s in range(2):
            full_ref[:, s, :, f * w : (f + 1) * w] = blk_ref[f, :, :, s * w : (s + 1) * w]


def mlp_kernel(R, len_ref, x_ref, cot_ref, mix_ref, par_ref, upb_ref, wo_ref, wu_ref, wd_ref,
               out_ref, gmid_ref, gmix_ref, small_ref, gub_ref, dwo_ref, dwu_ref, dwd_ref,
               wo, wd, act, gin, h2s, gbs):
    T, D = x_ref.shape
    FF = upb_ref.shape[1]
    nf, wf = wu_ref.shape[0], wu_ref.shape[2]
    unpack_cols(wo_ref, wo)
    unpack_pairs(wd_ref, wd)
    _, ends = ends_of(len_ref)
    small_ref[...] = jnp.zeros_like(small_ref)
    gub_ref[...] = jnp.zeros_like(gub_ref)
    cpf = wd.shape[0] // nf
    C0, C1 = 0.7978845608028654, 0.044715

    def block(b, _):
        rows = pl.ds(pl.multiple_of(b * R, R), R)
        x = x_ref[rows, :].astype(F32)
        middle = x + nn(mix_ref[rows, :], wo[...]) + par_ref[6:7, :]
        n2, r2 = ln_stats(middle)
        h2 = (n2 * par_ref[2:3, :] + par_ref[3:4, :]).astype(BF16)
        h2s[rows, :] = h2
        pos = lax.broadcasted_iota(jnp.int32, (R, 1), 0) + b * R
        live = pos < ends[-1]
        gb = jnp.where(live, cot_ref[rows, :].astype(F32), 0.0)
        gbl = gb.astype(BF16)
        gbs[rows, :] = gbl
        branch = jnp.zeros((R, D), F32)
        g_h2 = jnp.zeros((R, D), F32)
        for f in range(nf):
            cols = pl.ds(f * wf, wf)
            wdf = wd[f * cpf : (f + 1) * cpf].reshape(wf, D)
            u = nn(h2, wu_ref[f]) + upb_ref[0:1, f * wf : (f + 1) * wf]
            g_act = nt(gbl, wdf)
            u2 = u * u
            t = jnp.tanh(u * (C0 + (C0 * C1) * u2))
            hp = 0.5 + 0.5 * t
            a = u * hp
            al = a.astype(BF16)
            act[rows, cols] = al
            branch = branch + nn(al, wdf)
            d = hp + (a - a * hp) * (2.0 * C0 + (6.0 * C0 * C1) * u2)
            gi = (g_act * d).astype(BF16)
            gin[rows, cols] = gi
            gub_ref[0:1, f * wf : (f + 1) * wf] += jnp.sum(gi.astype(F32), axis=0, keepdims=True)
            g_h2 = g_h2 + nt(gi, wu_ref[f])
        out_ref[rows, :] = jnp.where(live, middle + branch + par_ref[7:8, :], 0.0).astype(BF16)
        small_ref[2:3, :] += jnp.sum(g_h2 * n2, axis=0, keepdims=True)
        small_ref[3:4, :] += jnp.sum(g_h2, axis=0, keepdims=True)
        g_mid = gb + ln_back(g_h2, n2, r2, par_ref[2:3, :])
        gmid_ref[rows, :] = g_mid
        gml = g_mid.astype(BF16)
        small_ref[6:7, :] += jnp.sum(gml.astype(F32), axis=0, keepdims=True)
        small_ref[7:8, :] += jnp.sum(gb, axis=0, keepdims=True)
        gmix_ref[rows, :] = nt(gml, wo[...]).astype(BF16)
        return 0

    lax.fori_loop(0, T // R, block, 0)
    w4 = D // nf

    def put(ref, grad, lead):
        r = ref.shape[2]
        c = grad.shape[0] // (2 * r)
        g = grad.astype(BF16).reshape(c, 2, r, D)
        for f in range(nf):
            for s in range(2):
                ref[f, pl.ds(lead, c), :, s * w4 : (s + 1) * w4] = g[:, s, :, f * w4 : (f + 1) * w4]

    def outp(i, _):
        g = tn(mix_ref[:, pl.ds(pl.multiple_of(i * 384, 128), 384)], gmid_ref[...].astype(BF16)).astype(BF16)
        for f in range(nf):
            dwo_ref[f, pl.ds(pl.multiple_of(i * 384, 128), 384), :] = g[:, f * w4 : (f + 1) * w4]
        return 0

    lax.fori_loop(0, D // 384, outp, 0)
    K = 384
    cpk = K // (2 * dwd_ref.shape[2])

    def down(i, _):
        put(dwd_ref, tn(act[:, pl.ds(pl.multiple_of(i * K, 128), K)], gbs[...]), i * cpk)
        return 0

    lax.fori_loop(0, FF // K, down, 0)
    H = 384

    def up(i, _):
        f, s = i // (wf // H), i % (wf // H)
        dwu_ref[f, :, pl.ds(pl.multiple_of(s * H, 128), H)] = tn(h2s[...], gin[:, pl.ds(pl.multiple_of(i * H, 128), H)]).astype(BF16)
        return 0

    lax.fori_loop(0, FF // H, up, 0)


def mlp(lengths, x, cot, mixed, par, upb, wo, wu, wd, R=256):
    T, D = x.shape
    FF = upb.shape[1]
    S = jax.ShapeDtypeStruct
    V = pltpu.VMEM
    return pl.pallas_call(
        functools.partial(mlp_kernel, R),
        out_shape=[S((T, D), BF16), S((T, D), F32), S((T, D), BF16), S((8, D), F32), S((8, FF), F32),
                   S(wo.shape, BF16), S(wu.shape, BF16), S(wd.shape, BF16)],
        in_specs=[sm()] + [vm()] * 8, out_specs=[vm()] * 8,
        scratch_shapes=[V((D, D), BF16), V((wd.shape[1], 2, wd.shape[2], D), BF16),
                        V((T, FF), BF16), V((T, FF), BF16), V((T, D), BF16), V((T, D), BF16)],
        compiler_params=pltpu.CompilerParams(vmem_limit_bytes=VLIM),
        name="mlp",
    )(lengths, x, cot, mixed, par, upb, wo, wu, wd)


def qkv_back_kernel(x_ref, h1_ref, gp_ref, gmid_ref, par_ref, w_ref, ig_ref, small_ref, dw_ref):
    T, D = x_ref.shape
    n, _, w = w_ref.shape
    R = 256
    for f in range(n):
        dw_ref[f] = tn(h1_ref[...], gp_ref[:, f * w : (f + 1) * w]).astype(BF16)
    small_ref[...] = jnp.zeros_like(small_ref)
    for b in range(T // R):
        rows = pl.ds(b * R, R)
        g_h1 = jnp.zeros((R, D), F32)
        for f in range(n):
            g_h1 = g_h1 + nt(gp_ref[rows, f * w : (f + 1) * w], w_ref[f])
        n1, r1 = ln_stats(x_ref[rows, :].astype(F32))
        small_ref[0:1, :] += jnp.sum(g_h1 * n1, axis=0, keepdims=True)
        small_ref[1:2, :] += jnp.sum(g_h1, axis=0, keepdims=True)
        small_ref[4:5, :] += jnp.sum(gp_ref[rows, 0:D].astype(F32), axis=0, keepdims=True)
        small_ref[5:6, :] += jnp.sum(gp_ref[rows, 2 * D : 3 * D].astype(F32), axis=0, keepdims=True)
        ig_ref[rows, :] = (gmid_ref[rows, :] + ln_back(g_h1, n1, r1, par_ref[0:1, :])).astype(BF16)


def qkv_back(x, h1, gp, gmid, par, w):
    S = jax.ShapeDtypeStruct
    return pl.pallas_call(
        qkv_back_kernel, out_shape=[S(x.shape, BF16), S((8, x.shape[1]), F32), S(w.shape, BF16)],
        in_specs=[vm()] * 6, out_specs=[vm()] * 3,
        compiler_params=pltpu.CompilerParams(vmem_limit_bytes=VLIM),
        name="qkv_back",
    )(x, h1, gp, gmid, par, w)


def masks_t(len_ref, r0, R, J):
    starts, ends = ends_of(len_ref)
    key = lax.broadcasted_iota(jnp.int32, (J, 1), 0)
    row = lax.broadcasted_iota(jnp.int32, (1, R), 1) + r0
    same = segment(key, ends) == segment(row, ends)
    return same & (key < row) & (opens(key, starts, ends) == 0)


def carried_scores(len_ref, q_ref, k_ref, cm, cmT_ref, carry):
    T = q_ref.shape[0]
    carry[...] = jnp.zeros_like(carry)
    i = lax.broadcasted_iota(jnp.int32, (B, B), 0)
    j = lax.broadcasted_iota(jnp.int32, (B, B), 1)
    lower = jnp.where(j < i, 1.0, 0.0).astype(BF16)
    for b in range(T // B):
        r0, J = b * B, (b + 1) * B
        rows = pl.ds(r0, B)
        allow, pick = masks(len_ref, r0, B, J)
        s0 = jnp.maximum(nt(only(q_ref[rows, 0:128], 0), k_ref[0:J, 0:128]), 0.0)
        chosen = jnp.where(pick, s0 * s0, 0.0)
        hi = chosen.astype(BF16)
        lo = (chosen - hi.astype(F32)).astype(BF16)
        carried = carry[0:1, 0:J] + (nn(lower, hi) + nn(lower, lo))
        c = jnp.where(allow, carried, BIG)
        cm[rows, 0:J] = c
        cmT_ref[0:J, rows] = jnp.transpose(c)
        carry[0:1, 0:J] = carry[0:1, 0:J] + jnp.sum(chosen, axis=0, keepdims=True)


def fwd_pair(p, q_ref, k_ref, v_ref, o_ref, lse, cm, s_sc, p_sc, C):
    T = q_ref.shape[0]
    lane = lax.broadcasted_iota(jnp.int32, (C, 128), 1)
    cols = pl.ds(pl.multiple_of(p * 128, 128), 128)
    k2, v2 = k_ref[:, cols], v_ref[:, cols]
    for half in range(2):
        q2 = only(q_ref[:, cols], half)
        for kb in range(T // B):
            s_sc[half, kb * B :, kb * B : (kb + 1) * B] = nt(q2[kb * B :], k2[kb * B : (kb + 1) * B])
    for rb in range(T // C):
        J = ((rb * C) // B + 1) * B
        rows = slice(rb * C, (rb + 1) * C)
        inv = []
        for half in range(2):
            l = s_sc[half, rows, :J] - cm[rows, :J]
            m = jnp.max(l, axis=1, keepdims=True)
            e = jnp.exp(l - m)
            t = jnp.sum(e, axis=1, keepdims=True)
            p_sc[half, rows, :J] = (e * (1.0 / t)).astype(BF16)
            lse[rows, :] = jnp.where(lane == 2 * p + half, m + jnp.log(t), lse[rows, :])
        if (rb * C) % B == B - C:
            b0 = (rb * C) // B * B
            o = [nn(p_sc[half, b0 : b0 + B, :J], v2[:J]) for half in range(2)]
            lanes = lax.broadcasted_iota(jnp.int32, (B, 128), 1)
            o_ref[b0 : b0 + B, cols] = jnp.where(lanes < 64, o[0], o[1]).astype(BF16)


def attn_fwd_kernel(C, len_ref, q_ref, k_ref, v_ref, o_ref, lseT_ref, cmT_ref, cm, lse, s_sc, p_sc, carry):
    carried_scores(len_ref, q_ref, k_ref, cm, cmT_ref, carry)

    def pair(p, _):
        fwd_pair(p, q_ref, k_ref, v_ref, o_ref, lse, cm, s_sc, p_sc, C)
        return 0

    lax.fori_loop(0, HEADS // 2, pair, 0)
    lseT_ref[...] = jnp.transpose(lse[...])[0:16]


def attn_fwd(lengths, q, k, v, C=64):
    T = q.shape[0]
    V = pltpu.VMEM
    return pl.pallas_call(
        functools.partial(attn_fwd_kernel, C),
        out_shape=[jax.ShapeDtypeStruct(q.shape, BF16), jax.ShapeDtypeStruct((16, T), F32), jax.ShapeDtypeStruct((T, T), F32)],
        in_specs=[sm()] + [vm()] * 3, out_specs=[vm()] * 3,
        scratch_shapes=[V((T, T), F32), V((T, 128), F32), V((2, T, T), F32), V((2, T, T), BF16), V((8, T), F32)],
        compiler_params=pltpu.CompilerParams(vmem_limit_bytes=VLIM),
        name="attn_fwd",
    )(lengths, q, k, v)


def row_sums(do_ref, o_ref, DT):
    T, D = do_ref.shape
    f = lax.broadcasted_iota(jnp.int32, (D, 128), 0)
    h = lax.broadcasted_iota(jnp.int32, (D, 128), 1)
    E = jnp.where((f >= h * 64) & (f < h * 64 + 64), 1.0, 0.0).astype(BF16)
    for b in range(T // B):
        rows = pl.ds(b * B, B)
        x = do_ref[rows, :].astype(F32) * o_ref[rows, :].astype(F32)
        hi = x.astype(BF16)
        lo = (x - hi.astype(F32)).astype(BF16)
        DT[:, rows] = jnp.transpose(nn(hi, E) + nn(lo, E))[0:16]


def bwd_scores(p, half, q_ref, k_ref, v_ref, do_ref, sT, dpT):
    T = q_ref.shape[0]
    cols = p * 128 if isinstance(p, int) else pl.multiple_of(p * 128, 128)
    c = pl.ds(cols, 128)
    k2, v2 = k_ref[:, c], v_ref[:, c]
    q2, do2 = only(q_ref[:, c], half), only(do_ref[:, c], half)
    for rb in range(T // B):
        J, r = (rb + 1) * B, slice(rb * B, (rb + 1) * B)
        sT[0:J, r] = nt(k2[0:J], q2[r])
        dpT[0:J, r] = nt(v2[0:J], do2[r])


def bwd_softmax(h, sT, dpT, pT, dsT, lseT, DT, cmT, C, add_into=None, keep=None):
    T = sT.shape[0]
    for kc in range(T // C):
        i0 = (kc * C) // B * B
        keys = slice(kc * C, (kc + 1) * C)
        pr = jnp.exp(sT[keys, i0:] - cmT[keys, i0:] - lseT[pl.ds(h, 1), i0:])
        ds = pr * (dpT[keys, i0:] - DT[pl.ds(h, 1), i0:])
        pT[keys, i0:] = pr.astype(BF16)
        if keep is not None:
            keep[keys, i0:] = ds
        else:
            dsT[keys, i0:] = ds.astype(BF16)
        add_into[keys, i0:] += ds


def bwd_products(p, half, q_ref, k_ref, do_ref, pT, dsT, gp_ref, dk, dv, first):
    T, D = q_ref.shape
    cols = p * 128 if isinstance(p, int) else pl.multiple_of(p * 128, 128)
    c = pl.ds(cols, 128)
    k2 = k_ref[:, c]
    q2, do2 = only(q_ref[:, c], half), only(do_ref[:, c], half)
    for kb in range(T // B):
        keys = slice(kb * B, (kb + 1) * B)
        a = nn(pT[keys, kb * B :], do2[kb * B :])
        d = nn(dsT[keys, kb * B :], q2[kb * B :])
        if first:
            dv[keys, :], dk[keys, :] = a, d
        else:
            dv[keys, :] += a
            dk[keys, :] += d
    lanes = lax.broadcasted_iota(jnp.int32, (B, 128), 1)
    for rb in range(T // B):
        J, r = (rb + 1) * B, slice(rb * B, (rb + 1) * B)
        dq = (tn(dsT[0:J, r], k2[0:J]) * 0.125).astype(BF16)
        if first:
            gp_ref[r, c] = dq
        else:
            gp_ref[r, c] = jnp.where((lanes < 64) == (half == 0), dq, gp_ref[r, c])


def first_head(len_ref, sT, ds0, dsT, G):
    T = sT.shape[0]
    i = lax.broadcasted_iota(jnp.int32, (B, B), 0)
    j = lax.broadcasted_iota(jnp.int32, (B, B), 1)
    after = jnp.where(i > j, 1.0, 0.0).astype(BF16)
    later = jnp.zeros((T, 1), F32)
    for rb in reversed(range(T // B)):
        J, r = (rb + 1) * B, slice(rb * B, (rb + 1) * B)
        g = -G[0:J, r]
        hi = g.astype(BF16)
        lo = (g - hi.astype(F32)).astype(BF16)
        g_chosen = later[0:J] + (nn(hi, after) + nn(lo, after))
        later = later[0:J] + jnp.sum(g, axis=1, keepdims=True)
        pick = masks_t(len_ref, rb * B, B, J)
        full = ds0[0:J, r] + jnp.where(pick, 2.0 * jnp.maximum(sT[0:J, r], 0.0) * g_chosen, 0.0)
        dsT[0:J, r] = full.astype(BF16)


def attn_bwd_kernel(C, len_ref, q_ref, k_ref, v_ref, do_ref, o_ref, lseT, cmT, gp_ref, DT, sT, dpT, pT, dsT, G, dk, dv):
    T, D = q_ref.shape
    row_sums(do_ref, o_ref, DT)
    G[...] = jnp.zeros_like(G)

    def put(p):
        ck = D + p * 128 if isinstance(p, int) else pl.multiple_of(D + p * 128, 128)
        cv = 2 * D + p * 128 if isinstance(p, int) else pl.multiple_of(2 * D + p * 128, 128)
        gp_ref[:, pl.ds(ck, 128)] = dk[...].astype(BF16)
        gp_ref[:, pl.ds(cv, 128)] = dv[...].astype(BF16)

    def pair(k, _):
        p = HEADS // 2 - 1 - k
        for half in range(2):
            bwd_scores(p, half, q_ref, k_ref, v_ref, do_ref, sT.at[half], dpT.at[half])
        for half in range(2):
            bwd_softmax(2 * p + half, sT.at[half], dpT.at[half], pT.at[half], dsT.at[half], lseT, DT, cmT, C, G)
        for half in range(2):
            bwd_products(p, half, q_ref, k_ref, do_ref, pT.at[half], dsT.at[half], gp_ref, dk, dv, half == 0)
        put(p)
        return 0

    lax.fori_loop(0, HEADS // 2 - 1, pair, 0)
    bwd_scores(0, 1, q_ref, k_ref, v_ref, do_ref, sT.at[1], dpT.at[1])
    bwd_softmax(1, sT.at[1], dpT.at[1], pT.at[1], dsT.at[1], lseT, DT, cmT, C, G)
    bwd_products(0, 1, q_ref, k_ref, do_ref, pT.at[1], dsT.at[1], gp_ref, dk, dv, True)
    bwd_scores(0, 0, q_ref, k_ref, v_ref, do_ref, sT.at[0], dpT.at[0])
    bwd_softmax(0, sT.at[0], dpT.at[0], pT.at[0], dsT.at[0], lseT, DT, cmT, C, G, keep=dpT.at[0])
    first_head(len_ref, sT.at[0], dpT.at[0], dsT.at[0], G)
    bwd_products(0, 0, q_ref, k_ref, do_ref, pT.at[0], dsT.at[0], gp_ref, dk, dv, False)
    put(0)


def attn_bwd(lengths, q, k, v, do, o, lseT, cmT, C=64):
    T, D = q.shape
    V = pltpu.VMEM
    return pl.pallas_call(
        functools.partial(attn_bwd_kernel, C),
        out_shape=jax.ShapeDtypeStruct((T, 3 * D), BF16),
        in_specs=[sm()] + [vm()] * 7, out_specs=vm(),
        scratch_shapes=[V((16, T), F32), V((2, T, T), F32), V((2, T, T), F32), V((2, T, T), BF16), V((2, T, T), BF16), V((T, T), F32), V((T, 128), F32), V((T, 128), F32)],
        compiler_params=pltpu.CompilerParams(vmem_limit_bytes=VLIM),
        name="attn_bwd",
    )(lengths, q, k, v, do, o, lseT, cmT)


def fold_tiny(tiny, par, per, n_dp, F):
    for f in range(F):
        for d in range(n_dp):
            for s in range(2):
                par[s * F + f : s * F + f + 1, d * per : (d + 1) * per] = tiny[f, d, 0, s : s + 1, 0:per].astype(F32)
            par[2 * F + f : 2 * F + f + 1, d * per : (d + 1) * per] = tiny[f, d, 1, 0:1, 0:per].astype(F32)


def front_kernel(geo, C, *refs):
    len_ref, x_ref = refs[0:2]
    raw, bufs = refs[2:7], refs[7:12]
    h1_o, q_o, k_o, v_o, mix_o, lseT_o, cmT_o, par = refs[12:20]
    tiny_v, wq_v, wf, h1, q, k, v, mix, cmT, cm, lse, s_sc, p_sc, carry, lsem, osem, down = refs[20:37]
    sems = refs[37:]
    T, D = x_ref.shape
    F, per = geo.n_fs, D // geo.n_dp
    shards = [raw[0]] + [s.reshape(2, s.shape[0] // 2, s.shape[1]) for s in raw[1:4]] + [down]
    r, w = down.shape[1], raw[4].shape[0]
    turned = jnp.transpose(raw[4][...].astype(F32)).astype(BF16)
    for i in range(4):
        down[i // 2, :, (i % 2) * w : (i % 2 + 1) * w] = turned[i * r : (i + 1) * r, :]
    barrier(geo)
    G = Gather(geo, shards, bufs, sems)
    at_block = {1: ((3, 1),), 3: ((2, 2),)}
    at_middle = ()
    plan = {0: ((3, 2),), 1: ((4, 1), (2, 3)), 4: ((3, 3),)}

    def ev(*items):
        for w, stage in items:
            for h in range(2):
                if stage == 4:
                    G.finish(w, h)
                else:
                    G.start(w, h, stage)

    ev((0, 0), (1, 0))
    G.fine(1, 0)
    ev((2, 0))
    for b in range(T // B):
        rows = pl.ds(b * B, B)
        n, _ = ln_stats(x_ref[rows, :].astype(F32))
        s_sc[0, rows, 0:D] = n
    ev((0, 1))
    G.fine(1, 1)
    ev((3, 0), (0, 2))
    G.fine(1, 2)
    ev((0, 3))
    G.fine(1, 3)
    ev((4, 0))
    for t in range(4, geo.nz + 3):
        G.fine(1, t)
        if t == geo.nz + 1:
            ev((2, 1))
    ev((0, 4))
    get_t = pltpu.make_async_copy(bufs[0], tiny_v, lsem.at[0])
    get_q = pltpu.make_async_copy(bufs[1], wq_v, lsem.at[1])
    get_t.start()
    get_q.start()
    get_t.wait()
    par[...] = jnp.zeros_like(par)
    fold_tiny(tiny_v.reshape(F, geo.n_dp, 2, 16, 128), par, per, geo.n_dp, F)
    get_q.wait()
    unpack_cols(wq_v.reshape(F, D, wq_v.shape[-1]), wf)
    outs = [pltpu.make_async_copy(a, b, osem.at[i]) for i, (a, b) in enumerate(((h1, h1_o), (q, q_o), (k, k_o), (v, v_o), (cmT, cmT_o), (mix, mix_o), (lse, lse))[:6])]
    for b in range(T // B):
        rows = pl.ds(b * B, B)
        hb = (s_sc[0, rows, 0:D] * par[0:1, :] + par[1:2, :]).astype(BF16)
        h1[rows, :] = hb
        q[rows, :] = (nn(hb, wf[:, 0:D]) + par[4:5, :]).astype(BF16) * jnp.asarray(0.125, BF16)
        k[rows, :] = nn(hb, wf[:, D : 2 * D]).astype(BF16)
        v[rows, :] = (nn(hb, wf[:, 2 * D : 3 * D]) + par[5:6, :]).astype(BF16)
        if b in at_block:
            ev(*at_block[b])
    for i in range(4):
        outs[i].start()
    ev(*at_middle)
    carried_scores(len_ref, q, k, cm, cmT, carry)
    outs[4].start()

    def pair(p, _):
        for at, items in plan.items():
            @pl.when(p == at)
            def _():
                ev(*items)
        fwd_pair(p, q, k, v, mix, lse, cm, s_sc, p_sc, C)
        return 0

    lax.fori_loop(0, HEADS // 2, pair, 0)
    outs[5].start()
    lseT_o[...] = jnp.transpose(lse[...])[0:16]
    ev((2, 4), (3, 4))
    for h in range(2):
        G.recv(4, h, 1)
    for w in range(5):
        for h in range(2):
            if w == 1:
                G.drain_fine(w, h)
            else:
                G.drain(w, h, (0, 1) if w == 4 else (0, 1, 2, 3))
    for i in range(6):
        outs[i].wait()


def front(geo, lengths, x, raw, collective_id=0, C=64):
    shards = [raw[0]] + [jax.ShapeDtypeStruct((2, s.shape[0] // 2, s.shape[1]), s.dtype) for s in raw[1:4]]
    shards.append(jax.ShapeDtypeStruct((2, raw[4].shape[1] // 4, 2 * raw[4].shape[0]), BF16))
    T, D = x.shape
    V, S, A = pltpu.VMEM, jax.ShapeDtypeStruct, pl.BlockSpec(memory_space=pl.ANY)
    lead = (geo.nx, geo.nc, geo.nz, geo.ny)
    tok = S((T, D), BF16)
    res = pl.pallas_call(
        functools.partial(front_kernel, geo, C),
        out_shape=[S(lead + s.shape, s.dtype) for s in shards] + [tok] * 5 + [S((16, T), F32), S((T, T), F32), S((16, D), F32)],
        in_specs=[sm(), vm()] + [vm()] * 5,
        out_specs=[A] * 10 + [vm(), A, vm()],
        scratch_shapes=[V(lead + shards[0].shape, BF16), V(lead + shards[1].shape, BF16), V((D, 3 * D), BF16)]
        + [V((T, D), BF16)] * 5 + [V((T, T), F32), V((T, T), F32), V((T, 128), F32), V((2, T, T), F32), V((2, T, T), BF16), V((8, T), F32)]
        + [pltpu.SemaphoreType.DMA((2,)), pltpu.SemaphoreType.DMA((6,)), V(shards[4].shape, BF16)] + gather_sems(geo, 5, geo.nz),
        compiler_params=pltpu.CompilerParams(collective_id=collective_id, has_side_effects=True, vmem_limit_bytes=VLIM),
        name="front",
    )(lengths, x, *raw)
    return res[:5], res[5:]


def repeats(w, n):
    r = lax.broadcasted_iota(jnp.int32, (w, n * w), 0)
    m = lax.broadcasted_iota(jnp.int32, (w, n * w), 1)
    return jnp.where((m >= n * r) & (m < n * r + n), 1.0, 0.0).astype(BF16)


def own_row(n, w):
    row = lax.broadcasted_iota(jnp.int32, (8, n * w), 0)
    m = lax.broadcasted_iota(jnp.int32, (8, n * w), 1)
    return row == lax.rem(m, n)


def weave(rows8, n, out_ref):
    w = rows8.shape[1] // n
    rep, own = repeats(w, n), own_row(n, w)
    for f in range(n):
        wide = nn(rows8[:, f * w : (f + 1) * w].astype(BF16), rep)
        line = jnp.sum(jnp.where(own, wide, 0.0), axis=0, keepdims=True)
        out_ref[:, f * n * w : (f + 1) * n * w] = jnp.broadcast_to(line, (8, n * w))


def unweave(line, n, out_ref):
    w = line.shape[1] // n // n
    rep, own = repeats(w, n), own_row(n, w)
    for f in range(n):
        wide = jnp.where(own, jnp.broadcast_to(line[:, f * n * w : (f + 1) * n * w], (8, n * w)), 0.0)
        hi = wide.astype(BF16)
        lo = (wide - hi.astype(F32)).astype(BF16)
        out_ref[:, f * w : (f + 1) * w] = nt(hi, rep) + nt(lo, rep)


def mid_kernel(geo, R, *refs):
    len_ref, par, x_h, cot_h, mix_h, wo_h, wu_h, half_h = refs[0:8]
    out_o, gmid_o, gmix_o, dwo_o, dwu_o, small, gub, part_o = refs[8:16]
    upb, X, C, M, wo_raw, wo, wu, land, wd, act, gin, h2s, gmid, gmix, dwo, dwu, dwd = refs[16:33]
    isem, osem, wsem = refs[33:36]
    bufs, ssems, gsems = refs[36:40], refs[40:42], refs[42:47]
    T, D = X.shape
    FF = act.shape[1]
    F = geo.n_fs
    wf, w4 = FF // F, D // F
    barrier(geo)
    G = Gather(geo, [None], [land], gsems)
    S = Scatter(geo, [dwd], [None], bufs, ssems)
    z, y, xx, c = geo.place()
    keep = [
        pltpu.make_async_copy(half_h.at[xx, c, :, :, 0], land.at[xx, c, :, :, 0], wsem.at[0]),
        pltpu.make_async_copy(half_h.at[:, c, :, y, 1], land.at[:, c, :, y, 1], wsem.at[1]),
    ]
    for cp in keep:
        cp.start()
    ins = [pltpu.make_async_copy(a, b, isem.at[i]) for i, (a, b) in enumerate(((wo_h, wo_raw), (x_h, X), (mix_h, M), (cot_h, C), (wu_h, wu)))]
    for cp in ins:
        cp.start()
    weave(par[8:16, :], F, upb)
    small[...] = jnp.zeros_like(small)
    gub[...] = jnp.zeros_like(gub)
    for cp in keep:
        cp.wait()
    for h in range(2):
        G.send(0, h, 2)
    _, ends = ends_of(len_ref)
    C0, C1 = 0.7978845608028654, 0.044715
    ins[0].wait()
    unpack_cols(wo_raw, wo)
    for cp in ins[1:]:
        cp.wait()

    def first(b, _):
        rows = pl.ds(pl.multiple_of(b * R, R), R)
        middle = X[rows, :].astype(F32) + nn(M[rows, :], wo[...]) + par[6:7, :]
        gmid[rows, :] = middle
        n2, _ = ln_stats(middle)
        h2 = (n2 * par[2:3, :] + par[3:4, :]).astype(BF16)
        h2s[rows, :] = h2
        pos = lax.broadcasted_iota(jnp.int32, (R, 1), 0) + b * R
        gb = jnp.where(pos < ends[-1], C[rows, :].astype(F32), 0.0)
        C[rows, :] = gb.astype(BF16)
        small[7:8, :] += jnp.sum(gb, axis=0, keepdims=True)
        for f in range(F):
            cols = slice(f * wf, (f + 1) * wf)
            u = nn(h2, wu[f]) + upb[0:1, cols]
            u2 = u * u
            t = jnp.tanh(u * (C0 + (C0 * C1) * u2))
            hp = 0.5 + 0.5 * t
            a = u * hp
            act[rows, cols] = a.astype(BF16)
            gin[rows, cols] = (hp + (a - a * hp) * (2.0 * C0 + (6.0 * C0 * C1) * u2)).astype(BF16)
        return 0

    lax.fori_loop(0, T // R, first, 0)
    for h in range(2):
        G.recv(0, h, 2)
        G.send(0, h, 3)

    r = dwd.shape[5]
    dv = dwd.reshape(F, 2 * geo.n_dp, r, 2 * w4)
    K = 768
    per = K // (2 * r)

    def down(i, _):
        g = tn(act[:, pl.ds(pl.multiple_of(i * K, 128), K)], C[...]).astype(BF16).reshape(per, 2, r, D)
        for f in range(F):
            for s in range(2):
                dv[f, pl.ds(i * per, per), :, s * w4 : (s + 1) * w4] = g[:, s, :, f * w4 : (f + 1) * w4]
        return 0

    lax.fori_loop(0, FF // K, down, 0)
    for h in range(2):
        S.step(0, h, 0)
    for h in range(2):
        G.recv(0, h, 3)
    lv = land.reshape(F, 2 * geo.n_dp, r, 2 * w4)
    for f in range(F):
        for s in range(2):
            wd[:, s, :, f * w4 : (f + 1) * w4] = lv[f, :, :, s * w4 : (s + 1) * w4]
    cpf = wd.shape[0] // F

    def second(b, _):
        rows = pl.ds(pl.multiple_of(b * R, R), R)
        pos = lax.broadcasted_iota(jnp.int32, (R, 1), 0) + b * R
        gbl = C[rows, :]
        branch = jnp.zeros((R, D), F32)
        g_h2 = jnp.zeros((R, D), F32)
        for f in range(F):
            cols = slice(f * wf, (f + 1) * wf)
            wdf = wd[f * cpf : (f + 1) * cpf].reshape(wf, D)
            branch = branch + nn(act[rows, cols], wdf)
            gi = (nt(gbl, wdf) * gin[rows, cols].astype(F32)).astype(BF16)
            gin[rows, cols] = gi
            gub[0:1, cols] += jnp.sum(gi.astype(F32), axis=0, keepdims=True)
            g_h2 = g_h2 + nt(gi, wu[f])
        middle = gmid[rows, :]
        X[rows, :] = jnp.where(pos < ends[-1], middle + branch + par[7:8, :], 0.0).astype(BF16)
        n2, r2 = ln_stats(middle)
        small[2:3, :] += jnp.sum(g_h2 * n2, axis=0, keepdims=True)
        small[3:4, :] += jnp.sum(g_h2, axis=0, keepdims=True)
        g_mid = gbl.astype(F32) + ln_back(g_h2, n2, r2, par[2:3, :])
        gmid[rows, :] = g_mid
        gml = g_mid.astype(BF16)
        small[6:7, :] += jnp.sum(gml.astype(F32), axis=0, keepdims=True)
        gmix[rows, :] = nt(gml, wo[...]).astype(BF16)
        return 0

    half = T // R // 2
    lax.fori_loop(0, half, second, 0)
    for h in range(2):
        S.step(0, h, 1)
    lax.fori_loop(half, T // R, second, 0)
    outs = [pltpu.make_async_copy(a, b, osem.at[i]) for i, (a, b) in enumerate(((X, out_o), (gmid, gmid_o), (gmix, gmix_o)))]
    for cp in outs:
        cp.start()
    o4 = dwo.reshape(F, D, w4)
    for i in range(2):
        g = tn(M[:, i * 384 : (i + 1) * 384], gmid[...].astype(BF16)).astype(BF16)
        for f in range(F):
            o4[f, i * 384 : (i + 1) * 384, :] = g[:, f * w4 : (f + 1) * w4]
    outs.append(pltpu.make_async_copy(dwo, dwo_o, osem.at[3]))
    outs[3].start()
    H = 768
    sent = []
    ov = dwu_o.reshape(F, D, wf)
    for f in range(F):
        if f >= 2:
            sent[f - 2].wait()

        def up(i, _):
            dwu[f % 2, :, pl.ds(pl.multiple_of(i * H, 128), H)] = tn(h2s[...], gin[:, pl.ds(pl.multiple_of(f * wf + i * H, 128), H)]).astype(BF16)
            return 0

        lax.fori_loop(0, wf // H, up, 0)
        sent.append(pltpu.make_async_copy(dwu.at[f % 2], ov.at[f], wsem.at[f % 2]))
        sent[f].start()
    for h in range(2):
        for cp in S.copies(0, h, 1):
            cp.wait_recv()
        S.add(0, h, 1)
    part_o[...] = bufs[1][...]
    for h in range(2):
        for stage in range(2):
            for cp in S.copies(0, h, stage):
                cp.wait_send()
        G.drain(0, h, (2, 3))
    for cp in outs + sent[-2:]:
        cp.wait()


def mid(geo, lengths, par, x, cot, mixed, wo, wu, half, collective_id=2, R=512):
    T, D = x.shape
    FF = wu.shape[0] * wu.shape[2]
    V, S, A, D_ = pltpu.VMEM, jax.ShapeDtypeStruct, pl.BlockSpec(memory_space=pl.ANY), pltpu.SemaphoreType.DMA
    lead = (geo.nx, geo.nc, geo.nz, geo.ny, 2)
    rr = D // geo.n_dp // 2
    tok = lambda: V((T, D), BF16)
    dwo, dwu = S(lead + (rr, wo.shape[2]), BF16), S(lead + (rr, wu.shape[2]), BF16)
    n = half.shape[5]
    return pl.pallas_call(
        functools.partial(mid_kernel, geo, R),
        out_shape=[S((T, D), BF16), S((T, D), F32), S((T, D), BF16), dwo, dwu, S((8, D), F32), S((8, FF), F32), S((2, 2, geo.nz) + half.shape[5:], BF16)],
        in_specs=[sm(), vm()] + [A] * 6,
        out_specs=[A] * 5 + [vm()] * 3,
        scratch_shapes=[V((8, FF), F32), tok(), tok(), tok(), V(wo.shape, BF16), V((D, D), BF16), V(wu.shape, BF16), V(half.shape, BF16),
                        V((2 * geo.n_dp, 2, n, D), BF16), V((T, FF), BF16), V((T, FF), BF16), tok(), V((T, D), F32), tok(), V(dwo.shape, BF16), V((2, D, wu.shape[2]), BF16), V(half.shape, BF16),
                        D_((5,)), D_((4,)), D_((2,))]
        + scatter_bufs(geo, [half]) + scatter_sems(geo, 1) + gather_sems(geo, 1),
        compiler_params=pltpu.CompilerParams(collective_id=collective_id, has_side_effects=True, vmem_limit_bytes=VLIM),
        name="mid",
    )(lengths, par, x, cot, mixed, wo, wu, half)


def spread_tiny(small, ub, tiny, per, n_dp, F):
    for f in range(F):
        for d in range(n_dp):
            for s in range(2):
                tiny[f, d, 0, s : s + 1, 0:per] = small[s * F + f : s * F + f + 1, d * per : (d + 1) * per]
            tiny[f, d, 1, 0:1, 0:per] = ub[f : f + 1, d * per : (d + 1) * per]


def back_kernel(geo, C, *refs):
    len_ref, lseT, part, small_b, gub, par = refs[0:6]
    q_h, k_h, v_h, do_h, o_h, cmT_h, x_h, h1_h, gmid_h, wq_h = refs[6:16]
    parts = refs[16:18]
    ig_o = refs[18]
    outs = refs[19:24]
    gp, DT, small, tiny, isem, osem, own_sem = refs[24:31]
    owns = [None] + list(refs[31:33]) + [None, None]
    bufs, sems = [None, part] + list(refs[33:51]), refs[51:53]
    D, T = gp.shape[1] // 3, gp.shape[0]
    F, n_dp = geo.n_fs, geo.n_dp
    per = D // n_dp
    barrier(geo)
    S = Scatter(geo, [None] + list(parts) + [None, tiny], outs, bufs, sems, owns, own_sem, ["pairs", "rows", "rows", "rows", None])
    DOWN, UP, OUT, QKV, TINY = range(5)

    def ev(*items):
        for w, stage in items:
            for h in range(2):
                S.step(w, h, stage)

    for h in range(2):
        for cp in S.copies(DOWN, h, 2):
            cp.start()
    ev((UP, 0), (OUT, 0))

    def attention(q, k, v, do, o, cmT, sT, dpT, pT, dsT, G, dk, dv):
        ins = [pltpu.make_async_copy(a, b, isem.at[i]) for i, (a, b) in enumerate(((do_h, do), (o_h, o), (q_h, q), (k_h, k), (v_h, v), (cmT_h, cmT)))]
        for cp in ins:
            cp.start()
        G[...] = jnp.zeros_like(G)
        ins[0].wait()
        ins[1].wait()
        row_sums(do, o, DT)
        for cp in ins[2:]:
            cp.wait()

        def put(p):
            ck = D + p * 128 if isinstance(p, int) else pl.multiple_of(D + p * 128, 128)
            cv = 2 * D + p * 128 if isinstance(p, int) else pl.multiple_of(2 * D + p * 128, 128)
            gp[:, pl.ds(ck, 128)] = dk[...].astype(BF16)
            gp[:, pl.ds(cv, 128)] = dv[...].astype(BF16)

        plan = {(0, 0): ((UP, 1),), (0, 1): ((OUT, 1),), (1, 1): ((DOWN, 3),), (3, 0): ((UP, 2),), (4, 0): ((OUT, 2),), (4, 1): ((UP, 3),)}

        def pair(n, _):
            p = HEADS // 2 - 1 - n
            for half in range(2):
                for (at, hf), items in plan.items():
                    if hf == half:
                        @pl.when(n == at)
                        def _():
                            ev(*items)
                bwd_scores(p, half, q, k, v, do, sT, dpT)
                bwd_softmax(2 * p + half, sT, dpT, pT, dsT, lseT, DT, cmT, C, G)
                bwd_products(p, half, q, k, do, pT, dsT, gp, dk, dv, half == 0)
            put(p)
            return 0

        lax.fori_loop(0, HEADS // 2 - 1, pair, 0)
        bwd_scores(0, 1, q, k, v, do, sT, dpT)
        bwd_softmax(1, sT, dpT, pT, dsT, lseT, DT, cmT, C, G)
        bwd_products(0, 1, q, k, do, pT, dsT, gp, dk, dv, True)
        ev((OUT, 3))
        bwd_scores(0, 0, q, k, v, do, sT, dpT)
        bwd_softmax(0, sT, dpT, pT, dsT, lseT, DT, cmT, C, G, keep=dpT)
        first_head(len_ref, sT, dpT, dsT, G)
        bwd_products(0, 0, q, k, do, pT, dsT, gp, dk, dv, False)
        put(0)

    V = pltpu.VMEM
    pl.run_scoped(
        attention, *[V((T, D), BF16)] * 5, V((T, T), F32), V((T, T), F32), V((T, T), F32), V((T, T), BF16), V((T, T), BF16), V((T, T), F32),
        V((T, 128), F32), V((T, 128), F32),
    )

    def projections(x, h1, gmid, wq, dwq, ig, ub):
        ins = [pltpu.make_async_copy(a, b, isem.at[i]) for i, (a, b) in enumerate(((h1_h, h1), (wq_h, wq), (x_h, x), (gmid_h, gmid)))]
        for cp in ins:
            cp.start()
        n, _, w = wq.shape
        dw = dwq.reshape(n, D, w)
        ins[0].wait()
        S.grads[QKV] = dwq
        for f in range(n):
            dw[f] = tn(h1[...], gp[:, f * w : (f + 1) * w]).astype(BF16)

            @pl.when(S.c != f % geo.nc)
            def _():
                for h in range(2):
                    S.first(QKV, h, f // geo.nc).start()

        for k in range(geo.nz):
            S.tick(QKV, k, 0)
        small[...] = small_b[...]
        order = {0: (), 1: (), 2: ((0, 1), (1, 1)), 3: ((2, 1), (0, 2), (3, 1), (1, 2), (2, 2))}
        for cp in ins[1:]:
            cp.wait()
        for b in range(T // B):
            rows = pl.ds(b * B, B)
            g_h1 = jnp.zeros((B, D), F32)
            for f in range(n):
                g_h1 = g_h1 + nt(gp[rows, f * w : (f + 1) * w], wq[f])
            n1, r1 = ln_stats(x[rows, :].astype(F32))
            small[0:1, :] += jnp.sum(g_h1 * n1, axis=0, keepdims=True)
            small[1:2, :] += jnp.sum(g_h1, axis=0, keepdims=True)
            small[4:5, :] += jnp.sum(gp[rows, 0:D].astype(F32), axis=0, keepdims=True)
            small[5:6, :] += jnp.sum(gp[rows, 2 * D : 3 * D].astype(F32), axis=0, keepdims=True)
            ig[rows, :] = (gmid[rows, :] + ln_back(g_h1, n1, r1, par[0:1, :])).astype(BF16)
            for k, stage in order[b]:
                S.tick(QKV, k, stage)
        out_cp = pltpu.make_async_copy(ig, ig_o, osem)
        out_cp.start()
        tiny[...] = jnp.zeros_like(tiny)
        unweave(gub[0:1, :], F, ub)
        spread_tiny(small, ub, tiny.reshape(F, n_dp, 2, 8, 128), per, n_dp, F)
        ev((TINY, 0))
        S.tick(QKV, 3, 2)
        ev((DOWN, 4), (UP, 4), (OUT, 4))
        ev((TINY, 1), (TINY, 2), (TINY, 3))
        S.tick(QKV, 3, 3)
        ev((TINY, 4))
        for h in range(2):
            S.drain_fine(QKV, h)
            for wt in (DOWN, UP, OUT, TINY):
                S.drain(wt, h, (2, 3) if wt == DOWN else (0, 1, 2, 3))
        out_cp.wait()

    pl.run_scoped(projections, V((T, D), BF16), V((T, D), BF16), V((T, D), F32), V(wq_h.shape, BF16), V((geo.nx, geo.nc, geo.nz, geo.ny, 2, per // 2, wq_h.shape[-1]), BF16), V((T, D), BF16), V((8, D), F32))


def back(geo, lengths, lseT, part, small_b, gub, par, q, k, v, do, o, cmT, x, h1, gmid, wq, parts, collective_id=1, C=64):
    T, D = x.shape
    V, S, A, D_ = pltpu.VMEM, jax.ShapeDtypeStruct, pl.BlockSpec(memory_space=pl.ANY), pltpu.SemaphoreType.DMA
    per = D // geo.n_dp
    dwq = S((geo.nx, geo.nc, geo.nz, geo.ny, 2, per // 2, wq.shape[-1]), BF16)
    tiny = S((geo.nx, geo.nc, geo.nz, geo.ny, 2, 8, 128), F32)
    down = S((geo.nx, geo.nc, geo.nz, geo.ny, 2) + part.shape[3:], BF16)
    grads = [down] + list(parts) + [dwq, tiny]
    finals = [S((part.shape[4] // 2, 4 * part.shape[3]), F32)] + [S((2 * g.shape[5], g.shape[6]), F32) for g in grads[1:4]] + [S(tiny.shape[4:], F32)]
    owns = [V((2, geo.nx, geo.nz, geo.ny) + g.shape[5:], BF16) for g in parts]
    return pl.pallas_call(
        functools.partial(back_kernel, geo, C),
        out_shape=[S((T, D), BF16)] + finals,
        in_specs=[sm()] + [vm()] * 5 + [A] * 12,
        out_specs=[A] + [vm()] * 5,
        scratch_shapes=[V((T, 3 * D), BF16), V((16, T), F32), V((8, D), F32), V(tiny.shape, F32), D_((6,)), D_, D_((5, 2))]
        + owns + scatter_bufs(geo, grads)[2:] + scatter_sems(geo, 5),
        compiler_params=pltpu.CompilerParams(collective_id=collective_id, has_side_effects=True, vmem_limit_bytes=VLIM),
        name="back",
    )(lengths, lseT, part, small_b, gub, par, q, k, v, do, o, cmT, x, h1, gmid, wq, *parts)


def pair_up(shard):
    w = shard.shape[1]
    return shard.reshape(2, 2, -1, w).transpose(0, 2, 1, 3).reshape(2, -1, 2 * w)


def pair_down(halves):
    w = halves.shape[2] // 2
    return halves.reshape(2, -1, 2, w).transpose(0, 2, 1, 3).reshape(-1, w)


def repair(blocks, r):
    n, c, r0, w2 = blocks.shape
    if r0 == r:
        return blocks
    w = w2 // 2
    flat = blocks.reshape(n, c, r0, 2, w).transpose(0, 1, 3, 2, 4).reshape(n, -1, 2, r, w)
    return flat.transpose(0, 1, 3, 2, 4).reshape(n, -1, r, w2)


def body(geo, tokens, cotangent, lengths, norm_params, bias_params, w_qkv, w_out, w_up, up_bias, w_down):
    T, D = tokens.shape
    F, n_dp, per = geo.n_fs, geo.n_dp, D // geo.n_dp
    FF = D * F * up_bias.shape[1]
    fused = (per // 2) % 16 == 0
    tiny = jnp.stack([jnp.stack([norm_params[:, 0], bias_params[:, 0]]), jnp.stack([up_bias[:, 0]] * 2)])
    tiny = jnp.pad(tiny, ((0, 0), (0, 14), (0, 128 - per)))

    def halves(shard):
        return shard.reshape(2, -1, shard.shape[1])

    if fused:
        bufs, (h1, q, k, v, mixed, lse, cm, par) = front(geo, lengths, tokens, [tiny, w_qkv, w_out, w_up, w_down.T])
        wq, wo, wu = (b.reshape(F, D, b.shape[-1]) for b in bufs[1:4])
        out, gmid, gmix, dwo, dwu, small, gub, part = mid(geo, lengths, par, tokens, cotangent, mixed, wo, wu, bufs[4])
        ig, s_down, s_up, s_out, s_qkv, s_tiny = back(
            geo, lengths, lse, part, small, gub, par, q, k, v, gmix, mixed, cm, tokens, h1, gmid, wq, [dwu, dwo]
        )
        s_down = s_down.T
    else:
        bufs = gather(geo, [tiny, halves(w_qkv), halves(w_out), halves(w_up), pair_up(w_down)])
        t = bufs[0].reshape(F, n_dp, 2, 16, 128)[..., :per].astype(F32)
        par = jnp.concatenate([t[:, :, 0, 0].reshape(F, D), t[:, :, 0, 1].reshape(F, D)], axis=0)
        upb = jnp.broadcast_to(t[:, :, 1, 0].reshape(F, D).T.reshape(1, FF), (8, FF))
        wq, wo, wu = (b.reshape(F, D, b.shape[-1]) for b in bufs[1:4])
        wd = repair(bufs[4].reshape((F, n_dp * 2) + bufs[4].shape[-2:]), FF // 32)
        h1, q, k, v = qkv(tokens, par, wq)
        mixed, lse, cm = attn_fwd(lengths, q, k, v)
        out, gmid, gmix, small_b, gub, dwo, dwu, dwd = mlp(lengths, tokens, cotangent, mixed, par, upb, wo, wu, wd)
        gp = attn_bwd(lengths, q, k, v, gmix, mixed, lse, cm)
        ig, small_a, dwq = qkv_back(tokens, h1, gp, gmid, par, wq)
        small = small_a + small_b

        def split(grad, rows):
            return grad.reshape((geo.nx, geo.nc, geo.nz, geo.ny, 2, rows, grad.shape[-1]))

        ub = gub[0].reshape(D, F).T.reshape(F, n_dp, per)
        rows = jnp.stack([small[0:4], small[4:8]]).reshape(2, F, n_dp, per)
        g = jnp.stack([jnp.stack([rows[0], rows[1]], axis=2), jnp.stack([ub, ub], axis=2)], axis=2)
        g = split(jnp.pad(g, ((0, 0), (0, 0), (0, 0), (0, 6), (0, 128 - per))), 8)
        r, rd = per // 2, FF // n_dp // 4
        s_tiny, s_out, s_up, s_down, s_qkv = scatter(geo, [g, split(dwo, r), split(dwu, r), split(repair(dwd, rd), rd), split(dwq, r)], 1)
        s_qkv, s_out, s_up = (s.reshape(-1, s.shape[-1]) for s in (s_qkv, s_out, s_up))
        s_down = pair_down(s_down)
    return (
        out,
        ig,
        s_tiny[0, 0, :per, None],
        s_tiny[0, 1, :per, None],
        s_qkv,
        s_out,
        s_up,
        s_tiny[1, 0, :per, None],
        s_down,
    )


def solution(mesh):
    geo = Geo(mesh.shape["dp"], mesh.shape["fsdp"])
    both, split = P(("dp", "fsdp"), None), P("dp", "fsdp")
    return jax.shard_map(
        functools.partial(body, geo), mesh=mesh, in_specs=(both,) * 3 + (split,) * 7, out_specs=(both,) * 2 + (split,) * 7, check_vma=False
    )
```
